32 devices in a mesh: seq: 8 (over z, x), tp: 4 (over y, core).
Axes of the slice: x: 2, y: 2, z: 4, core: 2. Of those that a mesh axis runs over, the one named last changes fastest.
Arguments:
- inputs: bfloat16 [12288, 768], P(('seq', 'tp')), may hold values from -6 to 6
- lengths: int32 [169], replicated, may hold values from 20 to 128, as said below
- w_qkv: bfloat16 [3, 768, 768], P(None, None, 'tp'), may hold values from -0.21875 to 0.21875
- w_out: bfloat16 [768, 768], P('tp'), may hold values from -0.625 to 0.625
- w_in: bfloat16 [768, 2, 3072], P(None, None, 'tp'), may hold values from -0.21875 to 0.21875
- w_down: bfloat16 [3072, 768], P('tp'), may hold values from -0.109375 to 0.109375
- ln1_gain: float32 [768], replicated, may hold values from 0.5 to 1.5
- ln1_bias: float32 [768], replicated, may hold values from -1.2 to 1.2
- ln2_gain: float32 [768], replicated, may hold values from 0.5 to 1.5
- ln2_bias: float32 [768], replicated, may hold values from -1.2 to 1.2
- cotangent: bfloat16 [12288, 768], P(('seq', 'tp')), may hold values from -6 to 6
Outputs:
- layer_out: bfloat16 [12288, 768], P(('seq', 'tp'))
- grad_input: float32 [12288, 768], P(('seq', 'tp'))
- grad_w_qkv: float32 [3, 768, 768], P(None, None, 'tp')
- grad_w_out: float32 [768, 768], P('tp')
- grad_w_in: float32 [768, 2, 3072], P(None, None, 'tp')
- grad_w_down: float32 [3072, 768], P('tp')
- grad_ln1_gain: float32 [768], replicated
- grad_ln1_bias: float32 [768], replicated
- grad_ln2_gain: float32 [768], replicated
- grad_ln2_bias: float32 [768], replicated
The draws below stay inside these ranges and needn't reach their ends.
Inputs may be any that keep to these rules, and one draw needn't show every extreme that they name: The 169 lengths add up to 12288. Every multiple of 1536 strictly between 0 and 12288 falls strictly inside a sequence, which has at most 127 tokens on either side of it.
All inputs are finite; a program needn't handle non-finite values.
Results may differ from the reference program's by a relative error of at most 0.02.
Values may be sent and summed in bfloat16 or wider, within the bound.
No kernel may reach another device: no remote copies, remote signals or barrier semaphores. Data moves between devices by JAX's collectives and lax.ppermute only.
A program may use at most 192 MiB of HBM per device.

```python
import math
import jax
import jax.numpy as jnp
import numpy as np
from jax import lax

D = 768
HEADS = 12
HD = 64
FF = 3072
TOK_DEV = 1536
LMAX = 128
LMIN = 20
REACH = 127
QBLOCK = 512
PAIRS = 8
TOKENS = 12288


def draw_lengths(key, part):
    key = jax.random.fold_in(key, 7)
    blocks = TOKENS // TOK_DEV
    split_keys = jax.random.split(key, 4)
    edge_lengths = jax.random.randint(split_keys[0], (blocks - 1,), LMIN, LMAX + 1, dtype=jnp.int32)
    edge_lengths = edge_lengths.at[blocks - 2].set(LMAX).at[0].set(LMAX)
    before_edge = jax.random.randint(split_keys[1], (blocks - 1,), 1, edge_lengths, dtype=jnp.int32)
    before_edge = before_edge.at[blocks - 2].set(1).at[0].set(REACH)
    after_edge = edge_lengths - before_edge
    closing = jax.random.randint(split_keys[2], (), LMIN, REACH + 1, dtype=jnp.int32)
    heads_in = jnp.concatenate([before_edge, closing[None]])
    tails_in = jnp.concatenate([jnp.full((1,), LMIN, jnp.int32), after_edge])
    paired = jax.random.randint(split_keys[3], (blocks, PAIRS), LMIN, LMAX + 1, dtype=jnp.int32)
    partner = LMIN + LMAX - paired
    remain = TOK_DEV - (LMIN + LMAX) * PAIRS - tails_in - heads_in
    filler_one = remain // 4
    filler_two = (remain - filler_one) // 3
    filler_three = (remain - filler_one - filler_two) // 2
    filler_four = remain - filler_one - filler_two - filler_three
    leading = jnp.concatenate([jnp.full((1,), LMIN, jnp.int32), edge_lengths])
    middle = jnp.stack([paired, partner], axis=2).reshape(blocks, 2 * PAIRS)
    stacked = jnp.concatenate([leading[:, None], middle, filler_one[:, None], filler_two[:, None], filler_three[:, None], filler_four[:, None]], axis=1)
    return jnp.concatenate([stacked.reshape(-1), closing[None]]).astype(jnp.int32)


def steps_of(own_key, extent, cuts, low, largest):
    level = 1.0
    for axis_at, blocks in cuts:
        draws = jax.random.uniform(jax.random.fold_in(jax.random.fold_in(own_key, 6), axis_at), (blocks,), jnp.float32, low / len(cuts), largest / len(cuts))
        level = level * jnp.repeat(jnp.exp(draws), extent[axis_at] // blocks).reshape((-1,) + (1,) * (len(extent) - 1 - axis_at))
    return level


def gaussian(rng, shape, deviation, bound, shards=(), kind=jnp.bfloat16):
    factor_of = steps_of(rng, shape, shards, -0.22, 0.18) if shards else 1.0
    values = jax.random.normal(rng, shape, jnp.float32) * deviation * factor_of
    return jnp.minimum(jnp.maximum(values, -bound), bound).astype(kind)


def setup_inputs(seed: int = 0) -> dict:
    seeds = jax.random.split(jax.random.key(seed), 12)
    return {
        "inputs": gaussian(seeds[0], (TOKENS, D), 1.0, 6.0, ((0, 32),)),
        "lengths": draw_lengths(jax.random.fold_in(seeds[11], 71), 0),
        "w_qkv": gaussian(seeds[2], (3, D, D), D ** -0.5, 0.21875, ((2, 4),)),
        "w_out": gaussian(seeds[3], (D, D), (D // 8) ** -0.5, 0.625, ((0, 4),)),
        "w_in": gaussian(seeds[4], (D, 2, FF), D ** -0.5, 0.21875, ((2, 4),)),
        "w_down": gaussian(seeds[5], (FF, D), FF ** -0.5, 0.109375, ((0, 4),)),
        "ln1_gain": jnp.clip(1.0 + 0.1 * jax.random.normal(seeds[6], (D,), jnp.float32), 0.5, 1.5),
        "ln1_bias": gaussian(seeds[7], (D,), 0.3, 1.2, (), jnp.float32),
        "ln2_gain": jnp.clip(1.0 + 0.1 * jax.random.normal(seeds[8], (D,), jnp.float32), 0.5, 1.5),
        "ln2_bias": gaussian(seeds[9], (D,), 0.3, 1.2, (), jnp.float32),
        "cotangent": gaussian(seeds[10], (TOKENS, D), 1.0, 6.0, ((0, 32),)),
    }


EPSILON = 1e-12
MASKED = -1e+30
FULL_PRECISION = lax.Precision.HIGHEST

@jax.custom_vjp
def low(v):
    return lax.optimization_barrier(v.astype(jnp.bfloat16)).astype(jnp.float32)

@jax.custom_vjp
def low_back(v):
    return v

def low_keep(v):
    return (low(v), None)

def low_pass(kept, grad):
    return (grad,)

def back_keep(v):
    return (v, None)

def back_low(kept, grad):
    return (low(grad),)
low.defvjp(low_keep, low_pass)
low_back.defvjp(back_keep, back_low)

def slope_table(count):
    power_two = 2 ** int(math.floor(math.log2(count)))
    leading = [2.0 ** (-8.0 * (head + 1) / power_two) for head in range(power_two)]
    trailing = [2.0 ** (-4.0 * (2 * other + 1) / power_two) for other in range(count - power_two)]
    return np.array(leading + trailing, np.float32)

def layer_norm(values, norm_gain, norm_bias):
    centred = values - lax.optimization_barrier(jnp.mean(values, axis=-1, keepdims=True))
    spread = lax.optimization_barrier(jnp.mean(centred * centred, axis=-1, keepdims=True))
    return centred * lax.rsqrt(spread + EPSILON) * norm_gain + norm_bias

def sequence_ids(lengths, first_token, count):
    places = first_token + jnp.arange(count, dtype=jnp.int32)
    bounds = jnp.cumsum(lengths).astype(jnp.int32)
    located = jnp.searchsorted(bounds, places, side='right').astype(jnp.int32)
    inside = (places >= 0) & (places < bounds[-1])
    return jnp.where(inside, located, -1)

def neighbours(blocked, fill):
    edge = jnp.full((1, LMAX) + blocked.shape[2:], fill, blocked.dtype)
    before = jnp.concatenate([edge, blocked[:-1, QBLOCK - LMAX:]], axis=0)
    after = jnp.concatenate([blocked[1:, :LMAX], edge], axis=0)
    return (before, after)

def attend(pieces):
    block_number, query_block, key_mid, key_before, key_after, value_mid, value_before, value_after, ids_mid, ids_before, ids_after = pieces
    slopes = jnp.asarray(slope_table(HEADS), dtype=jnp.float32)
    key_block = jnp.concatenate([key_before, key_mid, key_after], axis=0)
    value_block = jnp.concatenate([value_before, value_mid, value_after], axis=0)
    ids_key = jnp.concatenate([ids_before, ids_mid, ids_after], axis=0)
    places_query = block_number * QBLOCK + jnp.arange(QBLOCK, dtype=jnp.int32)
    places_key = block_number * QBLOCK - LMAX + jnp.arange(QBLOCK + 2 * LMAX, dtype=jnp.int32)
    products = jnp.einsum('qhd,khd->hqk', query_block, key_block, precision=FULL_PRECISION) * HD ** (-0.5)
    distance = jnp.abs(places_query[:, None] - places_key[None, :]).astype(jnp.float32)
    scores = products - slopes[:, None, None] * distance[None]
    scores = jnp.where((ids_mid[:, None] == ids_key[None, :])[None], scores, MASKED)
    scores = low_back(scores)
    probs = jax.nn.softmax(scores, axis=-1)
    return jnp.einsum('hqk,khd->qhd', low(probs), value_block, precision=FULL_PRECISION)

def forward_pass(inputs, w_qkv, w_out, w_in, w_down, ln1_gain, ln1_bias, ln2_gain, ln2_bias, ids_all):
    projected = low_back(low(jnp.einsum('nd,cde->nce', inputs, w_qkv, precision=FULL_PRECISION)))
    blocks = TOKENS // QBLOCK
    queries = projected[:, 0].reshape(blocks, QBLOCK, HEADS, HD)
    key_rows = projected[:, 1].reshape(blocks, QBLOCK, HEADS, HD)
    value_rows = projected[:, 2].reshape(blocks, QBLOCK, HEADS, HD)
    ids_rows = ids_all.reshape(blocks, QBLOCK)
    key_before, key_after = neighbours(key_rows, 0.0)
    value_before, value_after = neighbours(value_rows, 0.0)
    ids_before, ids_after = neighbours(ids_rows, -1)
    numbers = jnp.arange(blocks, dtype=jnp.int32)
    context = lax.map(jax.checkpoint(attend), (numbers, queries, key_rows, key_before, key_after, value_rows, value_before, value_after, ids_rows, ids_before, ids_after))
    context = low_back(low(context.reshape(TOKENS, D)))

    def tail_block(pieces):
        row_inputs, row_context = pieces
        attended = low_back(jnp.dot(row_context, w_out, precision=FULL_PRECISION))
        normed = layer_norm(row_inputs + attended, ln1_gain, ln1_bias)
        normed_low = low(normed)
        gate = low_back(jnp.dot(normed_low, w_in[:, 0], precision=FULL_PRECISION))
        upward = low_back(jnp.dot(normed_low, w_in[:, 1], precision=FULL_PRECISION))
        activated = low(jax.nn.gelu(gate, approximate=False) * upward)
        branch = low_back(jnp.dot(activated, w_down, precision=FULL_PRECISION))
        return layer_norm(normed + branch, ln2_gain, ln2_bias)
    stacked = (inputs.reshape(-1, TOK_DEV, D), context.reshape(-1, TOK_DEV, D))
    return lax.map(jax.checkpoint(tail_block), stacked).reshape(TOKENS, D)

def reference(inputs, lengths, w_qkv, w_out, w_in, w_down, ln1_gain, ln1_bias, ln2_gain, ln2_bias, cotangent):
    ids_all = sequence_ids(lengths, 0, TOKENS)
    primals = tuple((array.astype(jnp.float32) for array in (inputs, w_qkv, w_out, w_in, w_down, ln1_gain, ln1_bias, ln2_gain, ln2_bias)))

    def closed(*arrays):
        return forward_pass(*arrays, ids_all)
    result, pullback = jax.vjp(closed, *primals)
    grads = pullback(cotangent.astype(jnp.float32))
    return (result.astype(jnp.bfloat16), grads[0], grads[1], grads[2], grads[3], grads[4], grads[5], grads[6], grads[7], grads[8])
```

```python
import functools
import math

import jax
import jax.numpy as jnp
import numpy as np
from jax import lax
from jax.experimental import pallas as pl
from jax.experimental.pallas import tpu as pltpu
from jax.sharding import PartitionSpec as P

HEADS = 12
HD = 64
QB = 128
WINDOW = 3 * QB
EPSILON = 1e-12
FAR = 1e30

BF = jnp.bfloat16
F32 = jnp.float32
VMEM_LIMIT = 40 * 1024 * 1024


def dot(a, b, ca, cb):
    return lax.dot_general(a, b, (((ca,), (cb,)), ((), ())), preferred_element_type=F32)


def slope_table(count):
    power_two = 2 ** int(math.floor(math.log2(count)))
    leading = [2.0 ** (-8.0 * (head + 1) / power_two) for head in range(power_two)]
    trailing = [2.0 ** (-4.0 * (2 * other + 1) / power_two) for other in range(count - power_two)]
    return np.array(leading + trailing, np.float32)


def smem():
    return pl.BlockSpec(memory_space=pltpu.SMEM)


def full(shape):
    return pl.BlockSpec(shape, lambda *_: (0,) * len(shape))


def cost(flops, moved, transcendentals=0):
    return pl.CostEstimate(flops=flops, bytes_accessed=moved, transcendentals=transcendentals)


def params():
    return pltpu.CompilerParams(vmem_limit_bytes=VMEM_LIMIT)


def block_distance(se_ref, off):
    start = se_ref[0:1, pl.ds(off, QB)] - off
    end = se_ref[1:2, pl.ds(off, QB)] - off
    key = lax.broadcasted_iota(jnp.int32, (WINDOW, QB), 0)
    query = lax.broadcasted_iota(jnp.int32, (WINDOW, QB), 1) + QB
    valid = (key >= start) & (key < end)
    return jnp.where(valid, jnp.abs(key - query).astype(F32), FAR)


def block_probs(key, query, slope, distance):
    scores = dot(key, query, 1, 0) - slope * distance
    shifted = jnp.exp(scores - jnp.max(scores, axis=0, keepdims=True))
    return shifted * (1.0 / jnp.sum(shifted, axis=0, keepdims=True))


def attn_fwd_kernel(heads, slopes_ref, se_ref, qkv_ref, kv_ref, ctx_ref):
    width = heads * HD

    def block(b, carry):
        off = pl.multiple_of(b * QB, QB)
        distance = block_distance(se_ref, off)
        for h in range(heads):
            rows = slice(h * HD, (h + 1) * HD)
            query = qkv_ref[rows, pl.ds(off + QB, QB)] * BF(0.125)
            key = kv_ref[pl.ds(off, WINDOW), h * 128 : h * 128 + HD]
            probs = block_probs(key, query, slopes_ref[h], distance).astype(BF)
            value = qkv_ref[2 * width + h * HD : 2 * width + (h + 1) * HD, pl.ds(off, WINDOW)]
            ctx_ref[rows, pl.ds(off, QB)] = dot(value, probs, 1, 0).astype(BF)
        return carry

    lax.fori_loop(0, ctx_ref.shape[1] // QB, block, 0)


def attn_fwd(heads, slopes, se, qkv, kv):
    rows = se.shape[1]
    elements = heads * rows * WINDOW
    return pl.pallas_call(
        functools.partial(attn_fwd_kernel, heads),
        out_shape=jax.ShapeDtypeStruct((heads * HD, rows), BF),
        in_specs=[smem()] + [pl.BlockSpec(memory_space=pltpu.VMEM)] * 3,
        out_specs=pl.BlockSpec(memory_space=pltpu.VMEM),
        compiler_params=params(),
        cost_estimate=cost(elements * HD * 16, qkv.size * 2 + kv.size * 2, elements),
        name="attention_forward",
    )(slopes, se, qkv, kv)


def attn_bwd_kernel(heads, slopes_ref, se_ref, qkv_ref, kv_ref, dctx_ref, out_ref, acc_ref):
    width = heads * HD
    rows = dctx_ref.shape[1]
    acc_ref[...] = jnp.zeros_like(acc_ref)
    out_ref[0:width, 0:QB] = jnp.zeros((width, QB), BF)
    out_ref[0:width, QB + rows :] = jnp.zeros((width, QB), BF)

    def block(b, carry):
        off = pl.multiple_of(b * QB, QB)
        distance = block_distance(se_ref, off)
        for h in range(heads):
            mine = slice(h * HD, (h + 1) * HD)
            query = qkv_ref[mine, pl.ds(off + QB, QB)] * BF(0.125)
            key = kv_ref[pl.ds(off, WINDOW), h * 128 : h * 128 + HD]
            value = kv_ref[pl.ds(off, WINDOW), (heads + h) * 128 : (heads + h) * 128 + HD]
            probs = block_probs(key, query, slopes_ref[h], distance)
            d_rows = dctx_ref[mine, pl.ds(off, QB)]
            d_probs = dot(value, d_rows, 1, 0)
            row_dot = jnp.sum(d_probs * probs, axis=0, keepdims=True)
            d_scores = (probs * (d_probs - row_dot)).astype(BF)
            key_t = qkv_ref[width + h * HD : width + (h + 1) * HD, pl.ds(off, WINDOW)]
            d_query = dot(key_t, d_scores, 1, 0) * 0.125
            out_ref[mine, pl.ds(off + QB, QB)] = d_query.astype(BF)
            acc_ref[mine, pl.ds(off, WINDOW)] += dot(query, d_scores, 1, 1)
            acc_ref[width + h * HD : width + (h + 1) * HD, pl.ds(off, WINDOW)] += dot(
                d_rows, probs.astype(BF), 1, 1
            )
        return carry

    lax.fori_loop(0, rows // QB, block, 0)
    out_ref[width:, :] = acc_ref[...].astype(BF)


def attn_bwd(heads, slopes, se, qkv, kv, dctx):
    rows = se.shape[1]
    elements = heads * rows * WINDOW
    return pl.pallas_call(
        functools.partial(attn_bwd_kernel, heads),
        out_shape=jax.ShapeDtypeStruct(qkv.shape, BF),
        in_specs=[smem()] + [pl.BlockSpec(memory_space=pltpu.VMEM)] * 4,
        out_specs=pl.BlockSpec(memory_space=pltpu.VMEM),
        scratch_shapes=[pltpu.VMEM((2 * heads * HD, qkv.shape[1]), F32)],
        compiler_params=params(),
        cost_estimate=cost(elements * HD * 40, qkv.size * 4 + kv.size * 2, elements),
        name="attention_backward",
    )(slopes, se, qkv, kv, dctx)


def phi_pair(gate):
    bell = jnp.exp(gate * gate * -0.5)
    t = 1.0 / (1.0 + (0.3275911 / math.sqrt(2.0)) * jnp.abs(gate))
    poly = t * (
        0.254829592
        + t * (-0.284496736 + t * (1.421413741 + t * (-1.453152027 + t * 1.061405429)))
    )
    tail = 0.5 * poly * bell
    return jnp.where(gate >= 0.0, 1.0 - tail, tail), bell * (1.0 / math.sqrt(2.0 * math.pi))


def ff_fwd_kernel(x_ref, wg_ref, wu_ref, wd_ref, act_ref, a_ref, b_ref, keep_ref, send_ref):
    x = x_ref[...]
    hidden = wd_ref.shape[0]
    for f in range(0, hidden, 256):
        cols = slice(f, f + 256)
        gate = dot(x, wg_ref[:, cols], 1, 0)
        up = dot(x, wu_ref[:, cols], 1, 0)
        big, small = phi_pair(gate)
        gelu = gate * big
        act_ref[:, cols] = (gelu * up).astype(BF)
        a_ref[:, cols] = gelu.astype(BF)
        b_ref[:, cols] = (up * (big + gate * small)).astype(BF)
    part = dot(act_ref[...], wd_ref[...], 1, 0).astype(BF)

    @pl.when(pl.program_id(0) == 0)
    def _():
        keep_ref[...] = part

    @pl.when(pl.program_id(0) == 1)
    def _():
        send_ref[...] = part


def ff_fwd(x, wg, wu, wd):
    rows, width = x.shape
    hidden = wd.shape[0]
    half = rows // 2
    tile = pl.BlockSpec((half, hidden), lambda i: (i, 0))
    return pl.pallas_call(
        ff_fwd_kernel,
        grid=(2,),
        out_shape=[jax.ShapeDtypeStruct((rows, hidden), BF)] * 3
        + [jax.ShapeDtypeStruct((half, width), BF)] * 2,
        in_specs=[pl.BlockSpec((half, width), lambda i: (i, 0))]
        + [full((width, hidden))] * 2
        + [full((hidden, width))],
        out_specs=[tile] * 3 + [full((half, width))] * 2,
        compiler_params=params(),
        cost_estimate=cost(rows * width * hidden * 6, 12 * rows * width, 2 * rows * hidden),
        name="ff_forward",
    )(x, wg, wu, wd)


def ff_bwd_kernel(
    db_ref, a_ref, b_ref, wdt_ref, wgt_ref, wut_ref, dg_ref, du_ref, keep_ref, send_ref
):
    db = db_ref[...]
    hidden = wdt_ref.shape[1]
    for f in range(0, hidden, 256):
        cols = slice(f, f + 256)
        d_active = dot(db, wdt_ref[:, cols], 1, 0)
        dg_ref[:, cols] = (d_active * b_ref[:, cols].astype(F32)).astype(BF)
        du_ref[:, cols] = (d_active * a_ref[:, cols].astype(F32)).astype(BF)
    part = (dot(dg_ref[...], wgt_ref[...], 1, 0) + dot(du_ref[...], wut_ref[...], 1, 0)).astype(BF)

    @pl.when(pl.program_id(0) == 0)
    def _():
        keep_ref[...] = part

    @pl.when(pl.program_id(0) == 1)
    def _():
        send_ref[...] = part


def ff_bwd(db, a, b, wdt, wgt, wut):
    rows, width = db.shape
    hidden = wdt.shape[1]
    half = rows // 2
    tile = pl.BlockSpec((half, hidden), lambda i: (i, 0))
    return pl.pallas_call(
        ff_bwd_kernel,
        grid=(2,),
        out_shape=[jax.ShapeDtypeStruct((rows, hidden), BF)] * 2
        + [jax.ShapeDtypeStruct((half, width), BF)] * 2,
        in_specs=[pl.BlockSpec((half, width), lambda i: (i, 0)), tile, tile]
        + [full((width, hidden))]
        + [full((hidden, width))] * 2,
        out_specs=[tile] * 2 + [full((half, width))] * 2,
        compiler_params=params(),
        cost_estimate=cost(rows * width * hidden * 6, 12 * rows * width),
        name="ff_backward",
    )(db, a, b, wdt, wgt, wut)


def centre(pre):
    mean = jnp.mean(pre, axis=-1, keepdims=True)
    centred = pre - mean
    r = lax.rsqrt(jnp.mean(centred * centred, axis=-1, keepdims=True) + EPSILON)
    return centred * r, r


def norm_back(xhat, r, gain, grad):
    e = grad * gain
    return r * (
        e
        - jnp.mean(e, axis=-1, keepdims=True)
        - xhat * jnp.mean(e * xhat, axis=-1, keepdims=True)
    )


def ln1_kernel(x_ref, own_ref, recv_ref, gain_ref, bias_ref, pre_ref, normed_ref, low_ref):
    pre = x_ref[...].astype(F32) + (own_ref[...] + recv_ref[...].astype(F32))
    pre_ref[...] = pre
    xhat, _ = centre(pre)
    normed = xhat * gain_ref[...] + bias_ref[...]
    normed_ref[...] = normed
    low_ref[...] = normed.astype(BF)


def ln1(x, own, recv, gain, bias):
    shape = x.shape
    vm = pl.BlockSpec(memory_space=pltpu.VMEM)
    return pl.pallas_call(
        ln1_kernel,
        out_shape=[
            jax.ShapeDtypeStruct(shape, F32),
            jax.ShapeDtypeStruct(shape, F32),
            jax.ShapeDtypeStruct(shape, BF),
        ],
        in_specs=[vm] * 5,
        out_specs=[vm] * 3,
        compiler_params=params(),
        cost_estimate=cost(x.size * 10, x.size * 18),
        name="norm_one",
    )(x, own, recv, gain, bias)


def ln2_kernel(
    normed_ref, keep_ref, near_ref, far_ref, dy_ref, gain_ref, bias_ref,
    out_ref, d_ref, low_ref, grads_ref,
):
    branch = (
        keep_ref[...].astype(F32) + near_ref[...].astype(F32) + far_ref[...].astype(F32)
    )
    xhat, r = centre(normed_ref[...] + branch)
    gain = gain_ref[...]
    out_ref[...] = (xhat * gain + bias_ref[...]).astype(BF)
    dy = dy_ref[...].astype(F32)
    d = norm_back(xhat, r, gain, dy)
    d_ref[...] = d
    low_ref[...] = d.astype(BF)
    grads_ref[0:1, :] = jnp.sum(dy * xhat, axis=0, keepdims=True)
    grads_ref[1:2, :] = jnp.sum(dy, axis=0, keepdims=True)


def ln2(part, normed, keep, near, far, dy, gain, bias):
    rows, width = far.shape
    piece = pl.BlockSpec((rows, width), lambda i: (part, 0))
    first = full((rows, width))
    row = full((1, width))
    return pl.pallas_call(
        ln2_kernel,
        grid=(1,),
        out_shape=[
            jax.ShapeDtypeStruct((rows, width), BF),
            jax.ShapeDtypeStruct((rows, width), F32),
            jax.ShapeDtypeStruct((rows, width), BF),
            jax.ShapeDtypeStruct((2, width), F32),
        ],
        in_specs=[piece, first, first, first, piece, row, row],
        out_specs=[first, first, first, full((2, width))],
        compiler_params=params(),
        cost_estimate=cost(far.size * 20, far.size * 20),
        name="norm_two",
    )(normed, keep, near, far, dy, gain, bias)


def ln1_back_kernel(
    pre_ref, d2_ref, keep_ref, near_ref, far_ref, gain_ref, d_ref, low_ref, grads_ref
):
    grad = d2_ref[...] + (
        keep_ref[...].astype(F32) + near_ref[...].astype(F32) + far_ref[...].astype(F32)
    )
    xhat, r = centre(pre_ref[...])
    d = norm_back(xhat, r, gain_ref[...], grad)
    d_ref[...] = d
    low_ref[...] = d.astype(BF)
    grads_ref[0:1, :] = jnp.sum(grad * xhat, axis=0, keepdims=True)
    grads_ref[1:2, :] = jnp.sum(grad, axis=0, keepdims=True)


def ln1_back(part, pre, d2, keep, near, far, gain):
    rows, width = far.shape
    piece = pl.BlockSpec((rows, width), lambda i: (part, 0))
    first = full((rows, width))
    return pl.pallas_call(
        ln1_back_kernel,
        grid=(1,),
        out_shape=[
            jax.ShapeDtypeStruct((rows, width), F32),
            jax.ShapeDtypeStruct((rows, width), BF),
            jax.ShapeDtypeStruct((2, width), F32),
        ],
        in_specs=[piece, first, first, first, first, full((1, width))],
        out_specs=[first, first, full((2, width))],
        compiler_params=params(),
        cost_estimate=cost(far.size * 20, far.size * 20),
        name="norm_one_backward",
    )(pre, d2, keep, near, far, gain)


def swap(value, axis, bit):
    count = lax.axis_size(axis)
    return lax.ppermute(value, axis, [(i, i ^ bit) for i in range(count)])


def swap_chip_edges(value):
    count = lax.axis_size("seq") * lax.axis_size("tp")
    pairs = []
    for i in range(1, count - 1, 2):
        pairs += [(i, i + 1), (i + 1, i)]
    return lax.ppermute(value, ("seq", "tp"), pairs)


def shift_z(value, k):
    count = lax.axis_size("seq")
    return lax.ppermute(value, "seq", [(i, (i + 2 * k) % count) for i in range(count)])


def fold_kernel(place_ref, g_ref, r_ref, *out_refs):
    half = r_ref.shape[0]
    shard = out_refs[0].shape[0]
    base = place_ref[0] * half
    for k, out_ref in enumerate(out_refs):
        at = lax.rem(place_ref[1] + k, 4) * shard
        own = g_ref[pl.ds(pl.multiple_of(base + at, shard), shard), :].astype(F32)
        other = r_ref[pl.ds(pl.multiple_of(at, shard), shard), :].astype(F32)
        out_ref[...] = (own + other).astype(BF)


def fold(place, g, r):
    rows, width = r.shape
    vm = pl.BlockSpec(memory_space=pltpu.VMEM)
    return pl.pallas_call(
        fold_kernel,
        out_shape=[jax.ShapeDtypeStruct((rows // 4, width), BF)] * 4,
        in_specs=[smem(), vm, vm],
        out_specs=[vm] * 4,
        compiler_params=params(),
        cost_estimate=cost(r.size, r.size * 6),
        name="fold_half",
    )(place, g, r)


def spread_kernel(place_ref, *refs):
    out_ref = refs[-1]
    shard = refs[0].shape[0]
    for k, ref in enumerate(refs[:-1]):
        at = lax.rem(place_ref[1] + 4 - k, 4) * shard
        out_ref[pl.ds(pl.multiple_of(at, shard), shard), :] = ref[...]


def spread(place, shards):
    shard, width = shards[0].shape
    vm = pl.BlockSpec(memory_space=pltpu.VMEM)
    return pl.pallas_call(
        spread_kernel,
        out_shape=jax.ShapeDtypeStruct((4 * shard, width), BF),
        in_specs=[smem()] + [vm] * 4,
        out_specs=vm,
        compiler_params=params(),
        cost_estimate=cost(0, shard * width * 16),
        name="spread_shards",
    )(place, *shards)


def join_kernel(place_ref, own_ref, other_ref, out_ref):
    half = own_ref.shape[0]
    own = place_ref[0] * half
    out_ref[pl.ds(pl.multiple_of(own, half), half), :] = own_ref[...].astype(F32)
    out_ref[pl.ds(pl.multiple_of(half - own, half), half), :] = other_ref[...].astype(F32)


def join(place, own, other):
    half, width = own.shape
    vm = pl.BlockSpec(memory_space=pltpu.VMEM)
    return pl.pallas_call(
        join_kernel,
        out_shape=jax.ShapeDtypeStruct((2 * half, width), F32),
        in_specs=[smem(), vm, vm],
        out_specs=vm,
        compiler_params=params(),
        cost_estimate=cost(0, own.size * 12),
        name="join_halves",
    )(place, own, other)


def sum_over_seq(place, g):
    if lax.axis_size("seq") != 8:
        return lax.psum(g, "seq").astype(F32)
    half = g.shape[0] // 2
    sent = lax.dynamic_slice_in_dim(g, (1 - place[0]) * half, half, 0)
    shards = fold(place, g, swap(sent, "seq", 1))
    own = shards[0].astype(F32)
    for k in (1, 2, 3):
        own = own + shift_z(shards[k], k).astype(F32)
    own = own.astype(BF)
    whole = spread(place, [own] + [shift_z(own, k) for k in (1, 2, 3)])
    return join(place, whole, swap(whole, "seq", 1))


def sum_small(value):
    for bit in (1, 2):
        value = value + swap(value, "tp", bit)
    count = lax.axis_size("seq")
    bit = 1
    while bit < count:
        value = value + swap(value, "seq", bit)
        bit *= 2
    return value


def per_device(
    inputs, lengths, w_qkv, w_out, w_in, w_down, ln1_gain, ln1_bias, ln2_gain, ln2_bias, cotangent
):
    own_rows, width = inputs.shape
    tp_count = lax.axis_size("tp")
    head_width = w_qkv.shape[2]
    heads = head_width // HD
    chip_rows = 2 * own_rows
    tp = lax.axis_index("tp")
    seq = lax.axis_index("seq")
    core = tp & 1
    even = core == 0
    first = (seq * tp_count + 2 * (tp >> 1)) * own_rows
    place = jnp.stack([seq & 1, seq >> 1]).astype(jnp.int32)

    bounds = jnp.cumsum(lengths)[:, None]
    tokens = (first + jnp.arange(chip_rows, dtype=jnp.int32))[None, :]
    before = bounds <= tokens
    start = jnp.max(jnp.where(before, bounds, 0), axis=0)
    end = jnp.min(jnp.where(before, jnp.iinfo(jnp.int32).max, bounds), axis=0)
    se = jnp.stack([start, end]) - (first - QB)
    se = jnp.pad(se, ((0, 6), (0, 0)))
    table = jnp.asarray(slope_table(HEADS))
    slopes = lax.dynamic_slice_in_dim(table, tp * heads, heads)
    slopes_far = lax.dynamic_slice_in_dim(table, (tp ^ 2) * heads, heads)

    wt = w_qkv.transpose(0, 2, 1).reshape(3 * head_width, width)
    wt_far = swap(wt, "tp", 2)
    w_out_far = swap(w_out, "tp", 2)

    sibling = swap(inputs, "tp", 1)
    edge = swap_chip_edges(
        lax.dynamic_slice_in_dim(inputs, core * (own_rows - QB), QB, axis=0)
    )
    edge_sibling = swap(edge, "tp", 1)
    rows = jnp.concatenate(
        [
            jnp.where(even, edge, edge_sibling),
            jnp.where(even, inputs, sibling),
            jnp.where(even, sibling, inputs),
            jnp.where(even, edge_sibling, edge),
        ],
        axis=0,
    )

    wg, wu = w_in[:, 0], w_in[:, 1]
    wgt, wut, wdt = wg.T, wu.T, w_down.T

    def project(weights):
        natural = weights[head_width:].reshape(2 * heads, HD, width)
        natural = jnp.pad(natural, ((0, 0), (0, 128 - HD), (0, 0))).reshape(-1, width)
        return dot(weights, rows, 1, 1).astype(BF), dot(rows, natural, 1, 1).astype(BF)

    qkv, kv = project(wt)
    ctx = attn_fwd(heads, slopes, se, qkv, kv)
    qkv_far, kv_far = project(wt_far)
    ctx_far = attn_fwd(heads, slopes_far, se, qkv_far, kv_far)

    def attended_rows(which):
        at = which * own_rows
        near = lax.dynamic_slice_in_dim(ctx, at, own_rows, 1)
        far = lax.dynamic_slice_in_dim(ctx_far, at, own_rows, 1)
        return dot(near, w_out, 0, 0) + dot(far, w_out_far, 0, 0)

    attended_sent = swap(attended_rows(1 - core).astype(BF), "tp", 1)
    gain1, bias1 = ln1_gain[None], ln1_bias[None]
    gain2, bias2 = ln2_gain[None], ln2_bias[None]
    pre_one, normed, low = ln1(inputs, attended_rows(core), attended_sent, gain1, bias1)

    parts = 2
    piece = own_rows // parts

    def gather(value):
        pair = jnp.concatenate([value, swap(value, "tp", 2)], axis=0)
        return jnp.concatenate([pair, swap(pair, "tp", 1)], axis=0)

    def scatter(keep, sent):
        near = swap(sent, "tp", 1)
        far = (keep[piece:].astype(F32) + near[piece:].astype(F32)).astype(BF)
        return near, swap(far, "tp", 2)

    hidden_rows = [gather(low[p * piece : (p + 1) * piece]) for p in range(parts)]
    forward = [ff_fwd(hidden_rows[p], wg, wu, w_down) for p in range(parts)]
    second = []
    for p in range(parts):
        keep, sent = forward[p][3:]
        near, far = scatter(keep, sent)
        second.append(ln2(p, normed, keep, near, far, cotangent, gain2, bias2))
    layer_out = jnp.concatenate([s[0] for s in second], axis=0)
    d_branch = [gather(s[2]) for s in second]
    backward = [
        ff_bwd(d_branch[p], forward[p][1], forward[p][2], wdt, wgt, wut) for p in range(parts)
    ]
    grad_down = sum(dot(forward[p][0], d_branch[p], 0, 0) for p in range(parts)).astype(BF)
    grad_down = sum_over_seq(place, grad_down)
    first_back = []
    for p in range(parts):
        keep, sent = backward[p][2:]
        near, far = scatter(keep, sent)
        first_back.append(ln1_back(p, pre_one, second[p][1], keep, near, far, gain1))
    grad_gate = sum(dot(hidden_rows[p], backward[p][0], 0, 0) for p in range(parts))
    grad_up = sum(dot(hidden_rows[p], backward[p][1], 0, 0) for p in range(parts))
    grad_in = sum_over_seq(
        place, jnp.concatenate([grad_gate.astype(BF), grad_up.astype(BF)], axis=0)
    )
    grad_in = jnp.stack([grad_in[:width], grad_in[width:]], axis=1)
    norm_grads = sum_small(
        jnp.concatenate([sum(f[2] for f in first_back), sum(s[3] for s in second)], axis=0)
    )

    halves = [f[1] for f in first_back]
    halves_sibling = [swap(h, "tp", 1) for h in halves]
    d_attended = jnp.concatenate(
        [jnp.where(even, a, b) for a, b in zip(halves, halves_sibling)]
        + [jnp.where(even, b, a) for a, b in zip(halves, halves_sibling)],
        axis=0,
    )
    d_ctx_far = dot(w_out_far, d_attended, 1, 1).astype(BF)
    d_qkv_far = attn_bwd(heads, slopes_far, se, qkv_far, kv_far, d_ctx_far)
    far_grads = swap(
        jnp.concatenate(
            [dot(d_qkv_far, rows, 1, 0).astype(BF), dot(ctx_far, d_attended, 1, 0).astype(BF)],
            axis=0,
        ),
        "tp",
        2,
    )
    d_ctx = dot(w_out, d_attended, 1, 1).astype(BF)
    d_qkv = attn_bwd(heads, slopes, se, qkv, kv, d_ctx)
    own_grads = jnp.concatenate(
        [dot(d_qkv, rows, 1, 0), dot(ctx, d_attended, 1, 0)], axis=0
    )
    grad_attn = sum_over_seq(place, (own_grads + far_grads.astype(F32)).astype(BF))
    grad_qkv = grad_attn[: 3 * head_width].reshape(3, head_width, width).transpose(0, 2, 1)
    grad_out = grad_attn[3 * head_width :]

    half = own_rows + QB

    def window_half(which):
        at = which * half
        near = lax.dynamic_slice_in_dim(d_qkv, at, half, 1)
        far = lax.dynamic_slice_in_dim(d_qkv_far, at, half, 1)
        return dot(near, wt, 0, 0) + dot(far, wt_far, 0, 0)

    from_sibling = swap(window_half(1 - core).astype(BF), "tp", 1)
    d_half = window_half(core) + from_sibling.astype(F32)
    d_edge = swap_chip_edges(
        lax.dynamic_slice_in_dim(d_half, core * own_rows, QB, 0).astype(BF)
    )
    d_pre_one = jnp.concatenate([f[0] for f in first_back], axis=0)
    grad_input = d_pre_one + lax.dynamic_slice_in_dim(d_half, (1 - core) * QB, own_rows, 0)
    zeros = jnp.zeros((own_rows - QB, width), F32)
    d_edge = d_edge.astype(F32)
    grad_input = grad_input + jnp.where(
        even, jnp.concatenate([d_edge, zeros]), jnp.concatenate([zeros, d_edge])
    )
    return (
        layer_out,
        grad_input,
        grad_qkv,
        grad_out,
        grad_in,
        grad_down,
        norm_grads[0],
        norm_grads[1],
        norm_grads[2],
        norm_grads[3],
    )


def solution(mesh):
    in_specs = (
        P(("seq", "tp"), None),
        P(),
        P(None, None, "tp"),
        P("tp", None),
        P(None, None, "tp"),
        P("tp", None),
        P(),
        P(),
        P(),
        P(),
        P(("seq", "tp"), None),
    )
    out_specs = (
        P(("seq", "tp"), None),
        P(("seq", "tp"), None),
        P(None, None, "tp"),
        P("tp", None),
        P(None, None, "tp"),
        P("tp", None),
        P(),
        P(),
        P(),
        P(),
    )
    return jax.shard_map(
        per_device, mesh=mesh, in_specs=in_specs, out_specs=out_specs, check_vma=False
    )
```

```python
import functools
import math

import jax
import jax.numpy as jnp
import numpy as np
from jax import lax
from jax.experimental import pallas as pl
from jax.experimental.pallas import tpu as pltpu
from jax.sharding import PartitionSpec as P

HEADS = 12
HD = 64
NORM_ROWS = 16
QB = 128
WINDOW = 3 * QB
EPSILON = 1e-12
FAR = 1e30

BF = jnp.bfloat16
F32 = jnp.float32


def dot(a, b, ca, cb):
    return lax.dot_general(a, b, (((ca,), (cb,)), ((), ())), preferred_element_type=F32)


def slope_table(count):
    power_two = 2 ** int(math.floor(math.log2(count)))
    leading = [2.0 ** (-8.0 * (head + 1) / power_two) for head in range(power_two)]
    trailing = [2.0 ** (-4.0 * (2 * other + 1) / power_two) for other in range(count - power_two)]
    return np.array(leading + trailing, np.float32)


def smem():
    return pl.BlockSpec(memory_space=pltpu.SMEM)


def full(shape):
    return pl.BlockSpec(shape, lambda *_: (0,) * len(shape))


def cost(flops, moved, transcendentals=0, weight=50):
    return pl.CostEstimate(
        flops=weight * flops, bytes_accessed=weight * moved, transcendentals=transcendentals
    )


def params(mib):
    return pltpu.CompilerParams(vmem_limit_bytes=mib * 1024 * 1024)


def hbm(shape, kind=BF):
    return pltpu.HBM(shape, kind)


def after(value, *others):
    return lax.optimization_barrier((value, others))[0]


class Order:
    def __init__(self):
        self.last = ()

    def __call__(self, value):
        return after(value, *self.last)

    def note(self, value):
        self.last = (value,)
        return value


def block_distance(se_ref, off):
    start = se_ref[0:1, pl.ds(off, QB)] - off
    end = se_ref[1:2, pl.ds(off, QB)] - off
    key = lax.broadcasted_iota(jnp.int32, (WINDOW, QB), 0)
    query = lax.broadcasted_iota(jnp.int32, (WINDOW, QB), 1) + QB
    valid = (key >= start) & (key < end)
    return jnp.where(valid, jnp.abs(key - query).astype(F32), FAR)


def softmax(scores):
    shifted = jnp.exp(scores - jnp.max(scores, axis=0, keepdims=True))
    return shifted * (1.0 / jnp.sum(shifted, axis=0, keepdims=True))


def attend(slopes_ref, se_ref, rows_ref, wt_ref, ctx_ref, qkv_ref, kv_ref):
    weights = wt_ref[...].reshape(3 * HD, wt_ref.shape[2])
    for c in range(0, rows_ref.shape[0], 256):
        rows = rows_ref[c : c + 256, :]
        turned = dot(weights, rows, 1, 1).astype(BF)
        qkv_ref[:, :, c : c + 256] = turned.reshape(3, HD, 256)
        kv_ref[c : c + 256, :] = dot(rows, weights[HD:], 1, 1).astype(BF)
    slope = slopes_ref[pl.program_id(0)]
    zero = jnp.zeros((HD, QB), BF)
    starts = range(0, ctx_ref.shape[1], QB)
    scores = []
    for off in starts:
        query = qkv_ref[0, :, off + QB : off + 2 * QB] * BF(0.125)
        key = kv_ref[off : off + WINDOW, :]
        scores.append(dot(key, jnp.concatenate([query, zero], axis=0), 1, 0))
    probs = [
        softmax(x - slope * block_distance(se_ref, off)).astype(BF)
        for off, x in zip(starts, scores)
    ]
    for off, x in zip(starts, probs):
        value = qkv_ref[2, :, off : off + WINDOW]
        ctx_ref[:, off : off + QB] = dot(value, x, 1, 0).astype(BF)


def attn_near_kernel(
    place_ref, slopes_ref, se_ref, own_ref, sib_ref, edge_ref, edge_sib_ref, wt_ref,
    rows_ref, ctx_ref, qkv_ref, kv_ref,
):
    @pl.when(pl.program_id(0) == 0)
    def _():
        even = place_ref[3] == 0
        count = own_ref.shape[0]
        own, sib, edge, edge_sib = (r[...] for r in (own_ref, sib_ref, edge_ref, edge_sib_ref))
        rows_ref[0:QB, :] = jnp.where(even, edge, edge_sib)
        rows_ref[QB : QB + count, :] = jnp.where(even, own, sib)
        rows_ref[QB + count : QB + 2 * count, :] = jnp.where(even, sib, own)
        rows_ref[QB + 2 * count :, :] = jnp.where(even, edge_sib, edge)

    attend(slopes_ref, se_ref, rows_ref, wt_ref, ctx_ref, qkv_ref, kv_ref)


def attended_kernel(place_ref, near_ref, far_ref, w_out_ref, w_far_ref, own_ref, sent_ref):
    count = own_ref.shape[0]
    for ref, which in ((sent_ref, 1 - place_ref[3]), (own_ref, place_ref[3])):
        here = pl.ds(pl.multiple_of(which * count, 128), count)
        near = dot(near_ref[:, here], w_out_ref[...], 0, 0)
        ref[...] = (near + dot(far_ref[:, here], w_far_ref[...], 0, 0)).astype(ref.dtype)


def attn_fwd_outs(heads, here, count):
    shapes = [
        hbm((heads * HD, here)),
        hbm((3, heads * HD, count)),
        hbm((count, heads * 2 * HD)),
    ]
    blocks = [
        pl.BlockSpec((HD, here), lambda h: (h, 0)),
        pl.BlockSpec((3, HD, count), lambda h: (0, h, 0)),
        pl.BlockSpec((count, 2 * HD), lambda h: (0, h)),
    ]
    return shapes, blocks


def attn_cost(heads, here, count, width):
    elements = heads * here * WINDOW
    flops = elements * HD * 8 + 10 * heads * HD * count * width
    return cost(flops, count * width * 8, elements)


def attn_near(heads, place, slopes, se, own, sib, edge, edge_sib, wt):
    here, width = se.shape[1], own.shape[1]
    count = here + 2 * QB
    shapes, blocks = attn_fwd_outs(heads, here, count)
    return pl.pallas_call(
        attn_near_kernel,
        grid=(heads,),
        out_shape=[hbm((count, width))] + shapes,
        in_specs=[smem(), smem()]
        + [full(x.shape) for x in (se, own, sib, edge, edge_sib)]
        + [pl.BlockSpec((3, HD, width), lambda h: (0, h, 0))],
        out_specs=[full((count, width))] + blocks,
        compiler_params=params(20),
        cost_estimate=attn_cost(heads, here, count, width),
        name="attention_forward_near",
    )(place, slopes, se, own, sib, edge, edge_sib, wt)


def attn_far(heads, slopes, se, rows, wt):
    here, (count, width) = se.shape[1], rows.shape
    shapes, blocks = attn_fwd_outs(heads, here, count)
    return pl.pallas_call(
        attend,
        grid=(heads,),
        out_shape=shapes,
        in_specs=[smem()]
        + [full(se.shape), full(rows.shape)]
        + [pl.BlockSpec((3, HD, width), lambda h: (0, h, 0))],
        out_specs=blocks,
        compiler_params=params(20),
        cost_estimate=attn_cost(heads, here, count, width),
        name="attention_forward_far",
    )(slopes, se, rows, wt)


def attended_halves(place, near, far, w_out, w_far):
    half, width = near.shape[1] // 2, w_out.shape[1]
    vm = pl.BlockSpec(memory_space=pltpu.VMEM)
    return pl.pallas_call(
        attended_kernel,
        out_shape=[
            jax.ShapeDtypeStruct((half, width), F32),
            jax.ShapeDtypeStruct((half, width), BF),
        ],
        in_specs=[smem()] + [vm] * 4,
        out_specs=[vm] * 2,
        compiler_params=params(14),
        cost_estimate=cost(8 * near.size * width, 12 * half * width),
        name="attended_halves",
    )(place, near, far, w_out, w_far)


def head_back_kernel(head, slopes_ref, se_ref, qkv_ref, kv_ref, dctx_ref, out_ref, acc_ref):
    here = dctx_ref.shape[1]
    acc_ref[...] = jnp.zeros_like(acc_ref)
    edge = jnp.zeros((HD, QB), BF)
    out_ref[0, :, 0:QB] = edge
    out_ref[0, :, QB + here :] = edge
    slope = slopes_ref[head]
    starts = range(0, here, QB)
    pairs = []
    for off in starts:
        query = qkv_ref[0, :, off + QB : off + 2 * QB] * BF(0.125)
        d_rows = dctx_ref[:, off : off + QB]
        pairs.append(
            jnp.concatenate(
                [
                    jnp.concatenate([query, edge], axis=1),
                    jnp.concatenate([edge, d_rows], axis=1),
                ],
                axis=0,
            )
        )
    both = [dot(kv_ref[off : off + WINDOW, :], pair, 1, 0) for off, pair in zip(starts, pairs)]
    probs = [
        softmax(x[:, :QB] - slope * block_distance(se_ref, off)) for off, x in zip(starts, both)
    ]
    row_dots = [jnp.sum(x[:, QB:] * p, axis=0, keepdims=True) for x, p in zip(both, probs)]
    d_scores = [
        (p * (x[:, QB:] - row_dot)).astype(BF) for x, p, row_dot in zip(both, probs, row_dots)
    ]
    probs = [p.astype(BF) for p in probs]
    for off, d in zip(starts, d_scores):
        d_query = dot(qkv_ref[1, :, off : off + WINDOW], d, 1, 0) * 0.125
        out_ref[0, :, off + QB : off + 2 * QB] = d_query.astype(BF)
    sums = [
        dot(pair, jnp.concatenate([d, p], axis=1), 1, 1)
        for pair, d, p in zip(pairs, d_scores, probs)
    ]
    for off, x in zip(starts, sums):
        acc_ref[:, off : off + WINDOW] += x
    out_ref[1, :, :] = acc_ref[0:HD, :].astype(BF)
    out_ref[2, :, :] = acc_ref[HD:, :].astype(BF)


def head_back(head, slopes, se, qkv, kv, dctx):
    here, count = se.shape[1], qkv.shape[2]
    elements = here * WINDOW
    return pl.pallas_call(
        functools.partial(head_back_kernel, head),
        grid=(1,),
        out_shape=hbm((3, HD, count)),
        in_specs=[
            smem(),
            full(se.shape),
            pl.BlockSpec((3, HD, count), lambda i: (0, head, 0)),
            pl.BlockSpec((count, 2 * HD), lambda i: (0, head)),
            pl.BlockSpec((HD, here), lambda i: (head, 0)),
        ],
        out_specs=full((3, HD, count)),
        scratch_shapes=[pltpu.VMEM((2 * HD, count), F32)],
        compiler_params=params(12),
        cost_estimate=cost(elements * HD * 24, count * HD * 18, elements),
        name="attention_backward_head",
    )(slopes, se, qkv, kv, dctx)


def stack_heads(refs, all_ref):
    heads = len(refs)
    for h, ref in enumerate(refs):
        for part in range(3):
            at = (part * heads + h) * HD
            all_ref[at : at + HD, :] = ref[part]


def qkv_grad_kernel(*refs):
    (*heads, rows_ref, out_ref, all_ref) = refs
    stack_heads(heads, all_ref)
    for c in range(0, out_ref.shape[1], 256):
        out_ref[:, c : c + 256] = dot(all_ref[...], rows_ref[:, c : c + 256], 1, 0).astype(BF)


def qkv_grad(heads, rows):
    count, width = rows.shape
    size = len(heads) * 3 * HD
    vm = pl.BlockSpec(memory_space=pltpu.VMEM)
    return pl.pallas_call(
        qkv_grad_kernel,
        out_shape=jax.ShapeDtypeStruct((size, width), BF),
        in_specs=[vm] * (len(heads) + 1),
        out_specs=vm,
        scratch_shapes=[pltpu.VMEM((size, count), BF)],
        compiler_params=params(12),
        cost_estimate=cost(2 * size * count * width, count * width * 4),
        name="projection_gradient",
    )(*heads, rows)


def gather_back_kernel(
    place_ref, ctx_ref, own_ref, sib_ref, norms_ref, norms_sib_ref, w_out_ref, w_far_ref,
    datt_ref, grad_ref, dctx_ref, dctx_far_ref,
):
    even = place_ref[3] == 0
    half = datt_ref.shape[0] // 2
    own, sib = own_ref[...], sib_ref[...]
    datt_ref[0:half, :] = jnp.where(even, own, sib)
    datt_ref[half:, :] = jnp.where(even, sib, own)
    for c in range(0, 2 * half, 256):
        rows = datt_ref[c : c + 256, :]
        dctx_far_ref[:, c : c + 256] = dot(w_far_ref[...], rows, 1, 1).astype(BF)
        dctx_ref[:, c : c + 256] = dot(w_out_ref[...], rows, 1, 1).astype(BF)
    count = ctx_ref.shape[0]
    grad_ref[0:count, :] = dot(ctx_ref[...], datt_ref[...], 1, 0).astype(BF)
    norms = norms_ref[...].astype(F32) + norms_sib_ref[...].astype(F32)
    grad_ref[count:, :] = norms.astype(BF)


def gather_back(place, ctx, own, sib, norms, norms_sib, w_out, w_far):
    half, width = own.shape
    vm = pl.BlockSpec(memory_space=pltpu.VMEM)
    return pl.pallas_call(
        gather_back_kernel,
        out_shape=[
            hbm((2 * half, width)),
            jax.ShapeDtypeStruct((ctx.shape[0] + NORM_ROWS, width), BF),
            jax.ShapeDtypeStruct(ctx.shape, BF),
            jax.ShapeDtypeStruct(ctx.shape, BF),
        ],
        in_specs=[smem()] + [vm] * 7,
        out_specs=[vm] * 4,
        compiler_params=params(16),
        cost_estimate=cost(6 * ctx.size * width, 12 * half * width),
        name="gather_d_attended",
    )(place, ctx, own, sib, norms, norms_sib, w_out, w_far)


def phi_pair(gate):
    bell = jnp.exp(gate * gate * -0.5)
    t = 1.0 / (1.0 + (0.3275911 / math.sqrt(2.0)) * jnp.abs(gate))
    poly = t * (
        0.254829592
        + t * (-0.284496736 + t * (1.421413741 + t * (-1.453152027 + t * 1.061405429)))
    )
    tail = 0.5 * poly * bell
    return jnp.where(gate >= 0.0, 1.0 - tail, tail), bell * (1.0 / math.sqrt(2.0 * math.pi))


def take_rows(refs, out_ref):
    for step, ref in enumerate(refs):

        @pl.when(pl.program_id(0) == step)
        def _():
            out_ref[...] = ref[...]


def give_rows(part, keep_ref, send_ref):
    for step, ref in enumerate((keep_ref, send_ref)):

        @pl.when(pl.program_id(0) == step)
        def _():
            ref[...] = part


def ff_fwd_kernel(
    x0_ref, x1_ref, wg_ref, wu_ref, wd_ref,
    x_ref, act_ref, a_ref, b_ref, keep_ref, send_ref,
):
    take_rows((x0_ref, x1_ref), x_ref)
    x = x_ref[...]
    for f in range(0, wd_ref.shape[0], 256):
        cols = slice(f, f + 256)
        gate = dot(x, wg_ref[:, cols], 1, 0)
        up = dot(x, wu_ref[:, cols], 1, 0)
        big, small = phi_pair(gate)
        gelu = gate * big
        act_ref[:, cols] = (gelu * up).astype(BF)
        a_ref[:, cols] = gelu.astype(BF)
        b_ref[:, cols] = (up * (big + gate * small)).astype(BF)
    give_rows(dot(act_ref[...], wd_ref[...], 1, 0).astype(BF), keep_ref, send_ref)


def ff_fwd(pieces, wg, wu, wd):
    half, width = pieces[0].shape
    hidden = wd.shape[0]
    rows = 2 * half
    tile = pl.BlockSpec((half, hidden), lambda i: (i, 0))
    return pl.pallas_call(
        ff_fwd_kernel,
        grid=(2,),
        out_shape=[hbm((rows, width))]
        + [hbm((rows, hidden))] * 3
        + [jax.ShapeDtypeStruct((half, width), BF)] * 2,
        in_specs=[full((half, width))] * 2 + [full((width, hidden))] * 2 + [full((hidden, width))],
        out_specs=[pl.BlockSpec((half, width), lambda i: (i, 0))]
        + [tile] * 3
        + [full((half, width))] * 2,
        compiler_params=params(20),
        cost_estimate=cost(rows * width * hidden * 6, 12 * rows * width, 2 * rows * hidden),
        name="ff_forward",
    )(*pieces, wg, wu, wd)


def ff_bwd_kernel(
    d0_ref, d1_ref, a_ref, b_ref, wd_ref, wg_ref, wu_ref,
    db_ref, dg_ref, du_ref, keep_ref, send_ref,
):
    take_rows((d0_ref, d1_ref), db_ref)
    db = db_ref[...]
    for f in range(0, wd_ref.shape[0], 256):
        cols = slice(f, f + 256)
        d_active = dot(db, wd_ref[cols, :], 1, 1)
        dg_ref[:, cols] = (d_active * b_ref[:, cols].astype(F32)).astype(BF)
        du_ref[:, cols] = (d_active * a_ref[:, cols].astype(F32)).astype(BF)
    part = dot(dg_ref[...], wg_ref[...], 1, 1) + dot(du_ref[...], wu_ref[...], 1, 1)
    give_rows(part.astype(BF), keep_ref, send_ref)


def ff_bwd(pieces, a, b, wd, wg, wu):
    half, width = pieces[0].shape
    hidden = wd.shape[0]
    rows = 2 * half
    tile = pl.BlockSpec((half, hidden), lambda i: (i, 0))
    return pl.pallas_call(
        ff_bwd_kernel,
        grid=(2,),
        out_shape=[hbm((rows, width))]
        + [hbm((rows, hidden))] * 2
        + [jax.ShapeDtypeStruct((half, width), BF)] * 2,
        in_specs=[full((half, width))] * 2
        + [tile, tile]
        + [full((hidden, width))]
        + [full((width, hidden))] * 2,
        out_specs=[pl.BlockSpec((half, width), lambda i: (i, 0))]
        + [tile] * 2
        + [full((half, width))] * 2,
        compiler_params=params(20),
        cost_estimate=cost(rows * width * hidden * 6, 12 * rows * width),
        name="ff_backward",
    )(*pieces, a, b, wd, wg, wu)


def centre(pre):
    mean = jnp.mean(pre, axis=-1, keepdims=True)
    centred = pre - mean
    r = lax.rsqrt(jnp.mean(centred * centred, axis=-1, keepdims=True) + EPSILON)
    return centred * r, r


def norm_back(xhat, r, gain, grad):
    e = grad * gain
    return r * (
        e
        - jnp.mean(e, axis=-1, keepdims=True)
        - xhat * jnp.mean(e * xhat, axis=-1, keepdims=True)
    )


def ln1_kernel(x_ref, own_ref, recv_ref, gain_ref, bias_ref, pre_ref, normed_ref, low_ref):
    pre = x_ref[...].astype(F32) + (own_ref[...] + recv_ref[...].astype(F32))
    pre_ref[...] = pre
    xhat, _ = centre(pre)
    normed = xhat * gain_ref[...] + bias_ref[...]
    normed_ref[...] = normed
    low_ref[...] = normed.astype(BF)


def ln1(x, own, recv, gain, bias):
    shape = x.shape
    vm = pl.BlockSpec(memory_space=pltpu.VMEM)
    return pl.pallas_call(
        ln1_kernel,
        out_shape=[
            jax.ShapeDtypeStruct(shape, F32),
            jax.ShapeDtypeStruct(shape, F32),
            jax.ShapeDtypeStruct(shape, BF),
        ],
        in_specs=[vm] * 5,
        out_specs=[vm] * 3,
        compiler_params=params(14),
        cost_estimate=cost(x.size * 10, x.size * 18),
        name="norm_one",
    )(x, own, recv, gain, bias)


def ln2_kernel(
    normed_ref, keep_ref, near_ref, far_ref, dy_ref, gain_ref, bias_ref,
    out_ref, d_ref, low_ref, grads_ref,
):
    branch = (
        keep_ref[...].astype(F32) + near_ref[...].astype(F32) + far_ref[...].astype(F32)
    )
    xhat, r = centre(normed_ref[...] + branch)
    gain = gain_ref[...]
    out_ref[...] = (xhat * gain + bias_ref[...]).astype(BF)
    dy = dy_ref[...].astype(F32)
    d = norm_back(xhat, r, gain, dy)
    d_ref[...] = d
    low_ref[...] = d.astype(BF)
    grads_ref[0:1, :] = jnp.sum(dy * xhat, axis=0, keepdims=True)
    grads_ref[1:2, :] = jnp.sum(dy, axis=0, keepdims=True)


def ln2(normed, keep, near, far, dy, gain, bias):
    shape = far.shape
    vm = pl.BlockSpec(memory_space=pltpu.VMEM)
    return pl.pallas_call(
        ln2_kernel,
        out_shape=[
            jax.ShapeDtypeStruct(shape, BF),
            jax.ShapeDtypeStruct(shape, F32),
            jax.ShapeDtypeStruct(shape, BF),
            jax.ShapeDtypeStruct((2, shape[1]), F32),
        ],
        in_specs=[vm] * 7,
        out_specs=[vm] * 4,
        compiler_params=params(16),
        cost_estimate=cost(far.size * 20, far.size * 20),
        name="norm_two",
    )(normed, keep, near, far, dy, gain, bias)


def ln1_back_kernel(
    pre_ref, d2_ref, keep_ref, near_ref, far_ref, gain_ref, grads_two_ref,
    d_ref, low_ref, norms_ref,
):
    grad = d2_ref[...] + (
        keep_ref[...].astype(F32) + near_ref[...].astype(F32) + far_ref[...].astype(F32)
    )
    xhat, r = centre(pre_ref[...])
    d = norm_back(xhat, r, gain_ref[...], grad)
    d_ref[...] = d
    width = d.shape[1]
    low_ref[...] = d.astype(BF)
    norms_ref[...] = jnp.concatenate(
        [
            jnp.sum(grad * xhat, axis=0, keepdims=True),
            jnp.sum(grad, axis=0, keepdims=True),
            grads_two_ref[...],
            jnp.zeros((NORM_ROWS - 4, width), F32),
        ],
        axis=0,
    ).astype(BF)


def ln1_back(pre, d2, keep, near, far, gain, grads_two):
    shape = far.shape
    vm = pl.BlockSpec(memory_space=pltpu.VMEM)
    return pl.pallas_call(
        ln1_back_kernel,
        out_shape=[
            jax.ShapeDtypeStruct(shape, F32),
            jax.ShapeDtypeStruct(shape, BF),
            jax.ShapeDtypeStruct((NORM_ROWS, shape[1]), BF),
        ],
        in_specs=[vm] * 7,
        out_specs=[vm] * 3,
        compiler_params=params(16),
        cost_estimate=cost(far.size * 20, far.size * 20),
        name="norm_one_backward",
    )(pre, d2, keep, near, far, gain, grads_two)


def swap(value, axis, bit):
    count = lax.axis_size(axis)
    return lax.ppermute(value, axis, [(i, i ^ bit) for i in range(count)])


def swap_chip_edges(value):
    count = lax.axis_size("seq") * lax.axis_size("tp")
    pairs = []
    for i in range(1, count - 1, 2):
        pairs += [(i, i + 1), (i + 1, i)]
    return lax.ppermute(value, ("seq", "tp"), pairs)


def fold_kernel(dims, place_ref, own_ref, recv_ref, keep_ref, send_ref):
    rows, half = recv_ref.shape[0], keep_ref.shape[0]
    base = place_ref[dims[0]] * rows
    cut = place_ref[dims[1]] * half
    for ref, at in ((keep_ref, cut), (send_ref, half - cut)):
        own = own_ref[pl.ds(pl.multiple_of(base + at, NORM_ROWS), half), :].astype(F32)
        recv = recv_ref[pl.ds(pl.multiple_of(at, NORM_ROWS), half), :].astype(F32)
        ref[...] = (own + recv).astype(BF)


def fold(place, dims, own, recv):
    rows, width = recv.shape
    vm = pl.BlockSpec(memory_space=pltpu.VMEM)
    return pl.pallas_call(
        functools.partial(fold_kernel, dims),
        out_shape=[jax.ShapeDtypeStruct((rows // 2, width), BF)] * 2,
        in_specs=[smem(), vm, vm],
        out_specs=[vm] * 2,
        compiler_params=params(10),
        cost_estimate=cost(recv.size, recv.size * 6),
        name="fold_half",
    )(place, own, recv)


def join_kernel(dim, place_ref, own_ref, recv_ref, out_ref):
    first = place_ref[dim] == 0
    half = own_ref.shape[0]
    own, recv = own_ref[...], recv_ref[...]
    out_ref[0:half, :] = jnp.where(first, own, recv).astype(out_ref.dtype)
    out_ref[half:, :] = jnp.where(first, recv, own).astype(out_ref.dtype)


def join(place, dim, own, recv, kind=BF):
    half, width = own.shape
    vm = pl.BlockSpec(memory_space=pltpu.VMEM)
    return pl.pallas_call(
        functools.partial(join_kernel, dim),
        out_shape=jax.ShapeDtypeStruct((2 * half, width), kind),
        in_specs=[smem(), vm, vm],
        out_specs=vm,
        compiler_params=params(10),
        cost_estimate=cost(0, own.size * 12),
        name="join_halves",
    )(place, own, recv)


def finish_a_kernel(dim, place_ref, own_ref, recv_ref, _, out_ref):
    join_kernel(dim, place_ref, own_ref, recv_ref, out_ref)


def finish_a(place, dim, own, recv, later):
    half, width = own.shape
    return pl.pallas_call(
        functools.partial(finish_a_kernel, dim),
        grid=(1,),
        out_shape=jax.ShapeDtypeStruct(later.shape, F32),
        in_specs=[smem()]
        + [full((half, width))] * 2
        + [pl.BlockSpec(memory_space=pl.ANY)],
        out_specs=pl.BlockSpec((2 * half, width), lambda i: (0, 0)),
        input_output_aliases={3: 0},
        compiler_params=params(10),
        cost_estimate=cost(0, own.size * 12),
        name="finish_attention_gradient_a",
    )(place, own, recv, later)


def finish_b_kernel(dim, place_ref, own_ref, recv_ref, qkv_ref, out_ref, norm_ref):
    first = place_ref[dim] == 0
    own, recv = own_ref[...], recv_ref[...]
    step = own.shape[0] // 2
    count = step - NORM_ROWS
    low = jnp.where(first, own, recv).astype(F32)
    high = jnp.where(first, recv, own).astype(F32)
    for ref, rows in ((qkv_ref, low), (out_ref, high)):
        ref[0:count, :] = rows[0:count]
        ref[count:, :] = rows[step : step + count]
    norm_ref[...] = low[count : count + 4]


def finish_b(place, dim, own, recv, rows):
    half, width = own.shape
    rest = half - 2 * NORM_ROWS
    return pl.pallas_call(
        functools.partial(finish_b_kernel, dim),
        grid=(1,),
        out_shape=[
            jax.ShapeDtypeStruct((rows, width), F32),
            jax.ShapeDtypeStruct((rest, width), F32),
            jax.ShapeDtypeStruct((4, width), F32),
        ],
        in_specs=[smem()] + [full((half, width))] * 2,
        out_specs=[
            pl.BlockSpec((rest, width), lambda i: (rows // rest - 1, 0)),
            full((rest, width)),
            full((4, width)),
        ],
        compiler_params=params(10),
        cost_estimate=cost(0, own.size * 12),
        name="finish_attention_gradient_b",
    )(place, own, recv)


def cut_kernel(place_ref, own_ref, far_ref, out_ref, a_ref, b_ref, sent_a_ref, sent_b_ref):
    half = a_ref.shape[0]
    total = own_ref[...].astype(F32) + far_ref[...].astype(F32)
    a_ref[...] = total[:half].astype(BF)
    value = total[half:].astype(BF)
    step = b_ref.shape[0] // 4
    count = step - NORM_ROWS
    for i in range(4):
        at = (i % 2) * count
        source = value if i < 2 else out_ref
        b_ref[i * step : i * step + count, :] = source[at : at + count, :]
        b_ref[i * step + count : (i + 1) * step, :] = out_ref[2 * count :, :]
    for ref, sent_ref in ((a_ref, sent_a_ref), (b_ref, sent_b_ref)):
        count = sent_ref.shape[0]
        at = (1 - place_ref[0]) * count
        sent_ref[...] = ref[pl.ds(pl.multiple_of(at, NORM_ROWS), count), :]


def cut(place, own, far, out):
    width = own.shape[1]
    half = (own.shape[0] + out.shape[0] - NORM_ROWS) // 2
    more = half + 4 * NORM_ROWS
    vm = pl.BlockSpec(memory_space=pltpu.VMEM)
    return pl.pallas_call(
        cut_kernel,
        out_shape=[
            jax.ShapeDtypeStruct((count, width), BF) for count in (half, more, half // 2, more // 2)
        ],
        in_specs=[smem()] + [vm] * 3,
        out_specs=[vm] * 4,
        compiler_params=params(16),
        cost_estimate=cost(own.size, own.size * 8),
        name="add_far_shard",
    )(place, own, far, out)


def out_grad_kernel(ctx_ref, datt_ref, own_ref, far_ref, out_ref):
    count = ctx_ref.shape[0]
    near = dot(ctx_ref[...], datt_ref[...], 1, 0)
    out_ref[0:count, :] = (near + far_ref[0:count, :].astype(F32)).astype(BF)
    norms = own_ref[count:, :].astype(F32) + far_ref[count:, :].astype(F32)
    out_ref[count:, :] = norms.astype(BF)


def out_grad(ctx, datt, own, far):
    vm = pl.BlockSpec(memory_space=pltpu.VMEM)
    return pl.pallas_call(
        out_grad_kernel,
        out_shape=jax.ShapeDtypeStruct(far.shape, BF),
        in_specs=[vm] * 4,
        out_specs=vm,
        compiler_params=params(14),
        cost_estimate=cost(2 * ctx.size * datt.shape[1], datt.size * 2),
        name="out_gradient",
    )(ctx, datt, own, far)


class SeqSum:
    def __init__(self, place, order, dims, g, sent=None, last=None):
        self.place, self.order, self.dims, self.value = place, order, dims, g
        self.last = last or (lambda *halves: join(*halves, F32))
        self.stage = 1
        if lax.axis_size("seq") != 8:
            whole = lax.psum(g, "seq")
            half = g.shape[0] // 2
            zero = jnp.zeros_like(place)
            self.result = self.last(zero, 0, whole[:half], whole[half:])
            return
        if sent is None:
            half = g.shape[0] // 2
            sent = lax.dynamic_slice_in_dim(g, (1 - place[dims[0]]) * half, half, 0)
        self.send(0, sent)

    def send(self, dim, value):
        self.moving = swap(value, "seq", 1 << self.dims[dim])

    def step(self):
        stage, place, order, dims = self.stage, self.place, self.order, self.dims
        self.stage += 1
        if lax.axis_size("seq") != 8:
            return
        value, moved = order(self.value), self.moving
        if stage == 1:
            self.value, sent = fold(place, dims[:2], value, moved)
            order.note(sent)
            self.send(1, sent)
        elif stage in (2, 3):
            self.value = order.note(add(value, moved))
            self.send(2 if stage == 2 else 1, self.value)
        elif stage == 4:
            self.value = order.note(join(place, dims[1], value, moved))
            self.send(0, self.value)
        elif stage == 5:
            self.result = self.last(place, dims[0], value, moved)
            order.note(jax.tree.leaves(self.result)[-1])


def add_kernel(a_ref, b_ref, out_ref):
    out_ref[...] = (a_ref[...].astype(F32) + b_ref[...].astype(F32)).astype(BF)


def add(a, b, part=0, parts=1):
    rows, width = a.shape[0] // parts, a.shape[1]
    piece = pl.BlockSpec((rows, width), lambda i: (part, 0))
    return pl.pallas_call(
        add_kernel,
        grid=(1,),
        out_shape=jax.ShapeDtypeStruct((rows, width), BF),
        in_specs=[piece] * 2,
        out_specs=full((rows, width)),
        compiler_params=params(10),
        cost_estimate=cost(rows * width, rows * width * 6),
        name="add_pair",
    )(a, b)


def input_grad_kernel(place_ref, *refs):
    (*heads, wt_ref, wt_far_ref, own_ref, sent_ref, near_ref, far_ref) = refs
    stack_heads(heads[: len(heads) // 2], near_ref)
    stack_heads(heads[len(heads) // 2 :], far_ref)
    half = own_ref.shape[0]
    for ref, which in ((sent_ref, 1 - place_ref[3]), (own_ref, place_ref[3])):
        here = pl.ds(pl.multiple_of(which * half, 128), half)
        total = dot(near_ref[:, here], wt_ref[...], 0, 0)
        ref[...] = (total + dot(far_ref[:, here], wt_far_ref[...], 0, 0)).astype(ref.dtype)


def input_grad(place, near, far, wt, wt_far):
    count = near[0].shape[2]
    half, (size, width) = count // 2, wt.shape
    vm = pl.BlockSpec(memory_space=pltpu.VMEM)
    return pl.pallas_call(
        input_grad_kernel,
        out_shape=[
            jax.ShapeDtypeStruct((half, width), F32),
            jax.ShapeDtypeStruct((half, width), BF),
        ],
        in_specs=[smem()] + [vm] * (2 * len(near) + 2),
        out_specs=[vm] * 2,
        scratch_shapes=[pltpu.VMEM((size, count), BF)] * 2,
        compiler_params=params(20),
        cost_estimate=cost(4 * size * count * width, 12 * half * width),
        name="input_gradient",
    )(place, *near, *far, wt, wt_far)


def input_rows_kernel(place_ref, own_ref, recv_ref, pre_ref, out_ref, edge_ref):
    count, edge = out_ref.shape[0], edge_ref.shape[0]
    core = place_ref[3]
    at = pl.ds(pl.multiple_of(core * count, edge), edge)
    edge_ref[...] = (own_ref[at, :] + recv_ref[at, :].astype(F32)).astype(BF)
    at = pl.ds(pl.multiple_of((1 - core) * edge, edge), count)
    out_ref[...] = pre_ref[...] + (own_ref[at, :] + recv_ref[at, :].astype(F32))


def input_rows(place, own, recv, pre):
    vm = pl.BlockSpec(memory_space=pltpu.VMEM)
    return pl.pallas_call(
        input_rows_kernel,
        out_shape=[
            jax.ShapeDtypeStruct(pre.shape, F32),
            jax.ShapeDtypeStruct((QB, pre.shape[1]), BF),
        ],
        in_specs=[smem()] + [vm] * 3,
        out_specs=[vm] * 2,
        compiler_params=params(16),
        cost_estimate=cost(pre.size * 2, pre.size * 16),
        name="input_gradient_rows",
    )(place, own, recv, pre)


def input_edge_kernel(place_ref, rows_ref, edge_ref, out_ref):
    out_ref[...] = rows_ref[...]
    edge = edge_ref.shape[0]
    start = place_ref[3] * (rows_ref.shape[0] - edge)
    at = pl.ds(pl.multiple_of(start, edge), edge)
    out_ref[at, :] = rows_ref[at, :] + edge_ref[...].astype(F32)


def input_edge(place, rows, edge):
    vm = pl.BlockSpec(memory_space=pltpu.VMEM)
    return pl.pallas_call(
        input_edge_kernel,
        out_shape=jax.ShapeDtypeStruct(rows.shape, F32),
        in_specs=[smem()] + [vm] * 2,
        out_specs=vm,
        compiler_params=params(14),
        cost_estimate=cost(rows.size, rows.size * 10),
        name="input_gradient_edge",
    )(place, rows, edge)


def per_device(
    inputs, lengths, w_qkv, w_out, w_in, w_down, ln1_gain, ln1_bias, ln2_gain, ln2_bias, cotangent
):
    own_rows, width = inputs.shape
    tp_count = lax.axis_size("tp")
    head_width = w_qkv.shape[2]
    heads = head_width // HD
    chip_rows = 2 * own_rows
    tp = lax.axis_index("tp")
    seq = lax.axis_index("seq")
    core = tp & 1
    even = core == 0
    first = (seq * tp_count + 2 * (tp >> 1)) * own_rows
    place = jnp.stack([seq & 1, (seq >> 1) & 1, (seq >> 2) & 1, core]).astype(jnp.int32)

    bounds = jnp.cumsum(lengths)[:, None]
    tokens = (first + jnp.arange(chip_rows, dtype=jnp.int32))[None, :]
    before = bounds <= tokens
    start = jnp.max(jnp.where(before, bounds, 0), axis=0)
    end = jnp.min(jnp.where(before, jnp.iinfo(jnp.int32).max, bounds), axis=0)
    se = jnp.stack([start, end]) - (first - QB)
    se = jnp.pad(se, ((0, 6), (0, 0)))
    table = jnp.asarray(slope_table(HEADS))
    slopes = lax.dynamic_slice_in_dim(table, tp * heads, heads)
    slopes_far = lax.dynamic_slice_in_dim(table, (tp ^ 2) * heads, heads)

    wt = w_qkv.transpose(0, 2, 1).reshape(3 * head_width, width)
    wt_far = swap(wt, "tp", 2)

    sibling = swap(inputs, "tp", 1)
    edge = swap_chip_edges(
        lax.dynamic_slice_in_dim(inputs, core * (own_rows - QB), QB, axis=0)
    )
    edge_sibling = swap(edge, "tp", 1)
    rows, ctx, qkv, kv = attn_near(
        heads, place, slopes, se, inputs, sibling, edge, edge_sibling,
        wt.reshape(3, head_width, width),
    )
    w_out_far = swap(after(w_out, ctx), "tp", 2)
    ctx_far, qkv_far, kv_far = attn_far(
        heads, slopes_far, se, rows, wt_far.reshape(3, head_width, width)
    )
    attended, attended_sent = attended_halves(place, ctx, ctx_far, w_out, w_out_far)
    attended_sent = swap(attended_sent, "tp", 1)
    gain1, bias1 = ln1_gain[None], ln1_bias[None]
    gain2, bias2 = ln2_gain[None], ln2_bias[None]
    pre_one, normed, low = ln1(inputs, attended, attended_sent, gain1, bias1)

    order = Order()
    w_in_late = after(w_in, low)
    wg, wu = w_in_late[:, 0], w_in_late[:, 1]

    def both_ways(own, work, between=lambda near_out: None):
        far = swap(own, "tp", 2)
        near_out = work(0, own, order(swap(own, "tp", 1)))
        near_keep, near_send = near_out[-2:]
        order.note(near_send)
        recv = swap(near_send, "tp", 1)
        between(near_out)
        far = order(far)
        far_out = work(1, far, swap(far, "tp", 1))
        far_keep, far_send = far_out[-2:]
        order.note(far_send)
        from_sibling = swap(far_send, "tp", 1)
        far_sum = order.note(add(order(far_keep), from_sibling))
        return (near_out, far_out), (near_keep, recv, swap(far_sum, "tp", 2))

    order.note(low)
    forward, parts = both_ways(low, lambda i, a, b: ff_fwd((a, b), wg, wu, w_down))
    layer_out, d_pre_two, d_branch, grads_two = ln2(
        normed, order(parts[0]), *parts[1:], cotangent, gain2, bias2
    )
    order.note(d_branch)

    grads = {}

    def weight_grad(name, x, d):
        i = 1 if name in grads else 0
        part = dot(order(forward[i][x]), d, 0, 0)
        if i:
            part = (grads[name] + part).astype(BF)
        grads[name] = order.note(part)

    def grads_between(out):
        weight_grad("down", 1, out[0])
        weight_grad("up", 0, out[2])
        weight_grad("gate", 0, out[1])

    backward, parts = both_ways(
        d_branch,
        lambda i, a, b: ff_bwd((a, b), forward[i][2], forward[i][3], w_down, wg, wu),
        grads_between,
    )
    weight_grad("down", 1, backward[1][0])
    down = SeqSum(place, order, (0, 1, 2), grads["down"])
    weight_grad("up", 0, backward[1][2])
    up = SeqSum(place, order, (1, 0, 2), grads["up"])
    weight_grad("gate", 0, backward[1][1])
    gate = SeqSum(place, order, (0, 1, 2), grads["gate"])
    d_pre_one, half, norms = ln1_back(
        pre_one, d_pre_two, order(parts[0]), *parts[1:], gain1, grads_two
    )
    order.note(half)
    half_sibling = swap(half, "tp", 1)

    down.step()
    d_attended, sent_out, d_ctx, d_ctx_far = gather_back(
        place, order(ctx_far), half, half_sibling, norms, swap(norms, "tp", 1), w_out, w_out_far
    )
    order.note(d_ctx_far)
    far_out = swap(sent_out, "tp", 2)

    def one_head(h, far):
        kept = (slopes_far, se, qkv_far, kv_far) if far else (slopes, se, qkv, kv)
        return order.note(head_back(h, *kept, order(d_ctx_far if far else d_ctx)))

    d_far = [one_head(h, True) for h in range(heads)]
    far_qkv = order.note(qkv_grad(d_far, order(rows)))
    far_qkv = swap(far_qkv, "tp", 2)
    down.step()
    grad_out = order.note(out_grad(ctx, order(d_attended), sent_out, far_out))
    up.step()
    gate.step()
    d_near = [one_head(h, False) for h in range(2)]
    up.step()
    d_near += [one_head(h, False) for h in range(2, heads)]
    own_qkv = order.note(qkv_grad(d_near, order(rows)))
    down.step()
    total_a, total_b, sent_a, sent_b = cut(place, order(own_qkv), far_qkv, grad_out)
    order.note(sent_b)
    rows_qkv = own_qkv.shape[0]
    attn_b = SeqSum(
        place, order, (0, 1, 2), total_b, sent_b, lambda *h: finish_b(*h, rows_qkv)
    )
    attn_a = SeqSum(
        place, order, (0, 1, 2), total_a, sent_a, lambda *h: finish_a(*h, attn_b.result[0])
    )
    gate.step()
    down.step()
    attn_b.step()
    up.step()
    gate.step()
    window_own, window_sent = input_grad(place, [order(d_near[0]), *d_near[1:]], d_far, wt, wt_far)
    order.note(window_sent)
    window_sent = swap(window_sent, "tp", 1)
    attn_a.step()
    attn_b.step()
    gate.step()
    grad_rows, d_edge = input_rows(place, order(window_own), window_sent, d_pre_one)
    order.note(d_edge)
    d_edge = swap_chip_edges(d_edge)
    attn_a.step()
    attn_b.step()
    attn_a.step()
    up.step()
    attn_b.step()
    down.step()
    attn_a.step()
    grad_input = order.note(input_edge(place, order(grad_rows), d_edge))
    gate.step()
    attn_b.step()
    up.step()
    attn_a.step()
    assert all(unit.stage == 6 for unit in (down, gate, up, attn_a, attn_b))
    grad_down = down.result
    grad_in = jnp.stack([gate.result, up.result], axis=1)
    _, grad_out, norm_grads = attn_b.result
    grad_qkv = attn_a.result
    grad_qkv = grad_qkv.reshape(3, head_width, width).transpose(0, 2, 1)
    return (
        layer_out,
        grad_input,
        grad_qkv,
        grad_out,
        grad_in,
        grad_down,
        norm_grads[0],
        norm_grads[1],
        norm_grads[2],
        norm_grads[3],
    )


def solution(mesh):
    in_specs = (
        P(("seq", "tp"), None),
        P(),
        P(None, None, "tp"),
        P("tp", None),
        P(None, None, "tp"),
        P("tp", None),
        P(),
        P(),
        P(),
        P(),
        P(("seq", "tp"), None),
    )
    out_specs = (
        P(("seq", "tp"), None),
        P(("seq", "tp"), None),
        P(None, None, "tp"),
        P("tp", None),
        P(None, None, "tp"),
        P("tp", None),
        P(),
        P(),
        P(),
        P(),
    )
    return jax.shard_map(
        per_device, mesh=mesh, in_specs=in_specs, out_specs=out_specs, check_vma=False
    )
```

```python
import functools
import math

import jax
import jax.numpy as jnp
import numpy as np
from jax import lax
from jax.experimental import pallas as pl
from jax.experimental.pallas import tpu as pltpu
from jax.sharding import PartitionSpec as P

HEADS = 12
HD = 64
NORM_ROWS = 16
QB = 128
WINDOW = 3 * QB
EPSILON = 1e-12
FAR = 1e30

BF = jnp.bfloat16
F32 = jnp.float32


def dot(a, b, ca, cb):
    return lax.dot_general(a, b, (((ca,), (cb,)), ((), ())), preferred_element_type=F32)


def slope_table(count):
    power_two = 2 ** int(math.floor(math.log2(count)))
    leading = [2.0 ** (-8.0 * (head + 1) / power_two) for head in range(power_two)]
    trailing = [2.0 ** (-4.0 * (2 * other + 1) / power_two) for other in range(count - power_two)]
    return np.array(leading + trailing, np.float32)


def smem():
    return pl.BlockSpec(memory_space=pltpu.SMEM)


def full(shape):
    return pl.BlockSpec(shape, lambda *_: (0,) * len(shape))


def cost(flops, moved, transcendentals=0):
    return pl.CostEstimate(
        flops=flops // 1000,
        bytes_accessed=moved // 1000,
        transcendentals=transcendentals // 1000,
    )


def params(mib):
    return pltpu.CompilerParams(vmem_limit_bytes=mib * 1024 * 1024)


def out(shape, kind=BF):
    return jax.ShapeDtypeStruct(shape, kind)


def vmem(count):
    return [pl.BlockSpec(memory_space=pltpu.VMEM)] * count


def after(value, *others):
    return lax.optimization_barrier((value, others))[0]


class Order:
    def __init__(self):
        self.last = ()

    def __call__(self, value):
        return after(value, *self.last)

    def note(self, value):
        self.last = (value,)
        return value


def block_distance(se_ref, off):
    start = se_ref[0:1, pl.ds(off, QB)] - off
    end = se_ref[1:2, pl.ds(off, QB)] - off
    key = lax.broadcasted_iota(jnp.int32, (WINDOW, QB), 0)
    query = lax.broadcasted_iota(jnp.int32, (WINDOW, QB), 1) + QB
    valid = (key >= start) & (key < end)
    return jnp.where(valid, jnp.abs(key - query).astype(F32), FAR)


def softmax(scores):
    shifted = jnp.exp(scores - jnp.max(scores, axis=0, keepdims=True))
    return shifted * (1.0 / jnp.sum(shifted, axis=0, keepdims=True))


def attend(heads, slopes_ref, se_ref, rows_ref, wt_ref, ctx_ref, qkv_ref, kv_ref):
    zero = jnp.zeros((HD, QB), BF)
    starts = range(0, ctx_ref.shape[1], QB)
    for h in range(heads):
        mine = slice(h * HD, (h + 1) * HD)
        pair = slice(h * 2 * HD, (h + 1) * 2 * HD)
        weights = wt_ref[:, mine, :].reshape(3 * HD, wt_ref.shape[2])
        for c in range(0, rows_ref.shape[0], 256):
            rows = rows_ref[c : c + 256, :]
            turned = dot(weights, rows, 1, 1).astype(BF)
            qkv_ref[:, mine, c : c + 256] = turned.reshape(3, HD, 256)
            kv_ref[c : c + 256, pair] = dot(rows, weights[HD:], 1, 1).astype(BF)
        scores = []
        for off in starts:
            query = qkv_ref[0, mine, off + QB : off + 2 * QB] * BF(0.125)
            key = kv_ref[off : off + WINDOW, pair]
            scores.append(dot(key, jnp.concatenate([query, zero], axis=0), 1, 0))
        probs = [
            softmax(x - slopes_ref[h] * block_distance(se_ref, off)).astype(BF)
            for off, x in zip(starts, scores)
        ]
        for off, x in zip(starts, probs):
            value = qkv_ref[2, mine, off : off + WINDOW]
            ctx_ref[mine, off : off + QB] = dot(value, x, 1, 0).astype(BF)


def attn_near_kernel(
    heads, place_ref, slopes_ref, se_ref, own_ref, sib_ref, edge_ref, edge_sib_ref, wt_ref,
    rows_ref, ctx_ref, qkv_ref, kv_ref,
):
    even = place_ref[4] == 0
    count = own_ref.shape[0]
    own, sib, edge, edge_sib = (r[...] for r in (own_ref, sib_ref, edge_ref, edge_sib_ref))
    rows_ref[0:QB, :] = jnp.where(even, edge, edge_sib)
    rows_ref[QB : QB + count, :] = jnp.where(even, own, sib)
    rows_ref[QB + count : QB + 2 * count, :] = jnp.where(even, sib, own)
    rows_ref[QB + 2 * count :, :] = jnp.where(even, edge_sib, edge)
    attend(heads, slopes_ref, se_ref, rows_ref, wt_ref, ctx_ref, qkv_ref, kv_ref)


def attended_kernel(place_ref, near_ref, far_ref, w_out_ref, w_far_ref, own_ref, sent_ref):
    count = own_ref.shape[0]
    for ref, which in ((sent_ref, 1 - place_ref[4]), (own_ref, place_ref[4])):
        here = pl.ds(pl.multiple_of(which * count, 128), count)
        near = dot(near_ref[:, here], w_out_ref[...], 0, 0)
        ref[...] = (near + dot(far_ref[:, here], w_far_ref[...], 0, 0)).astype(ref.dtype)


def attn_fwd_outs(heads, here, count):
    return [
        out((heads * HD, here)),
        out((3, heads * HD, count)),
        out((count, heads * 2 * HD)),
    ]


def attn_cost(heads, here, count, width):
    elements = heads * here * WINDOW
    flops = elements * HD * 8 + 10 * heads * HD * count * width
    return cost(flops, count * width * 8, elements)


def attn_near(heads, place, slopes, se, own, sib, edge, edge_sib, wt):
    here, width = se.shape[1], own.shape[1]
    count = here + 2 * QB
    return pl.pallas_call(
        functools.partial(attn_near_kernel, heads),
        out_shape=[out((count, width))] + attn_fwd_outs(heads, here, count),
        in_specs=[smem(), smem()] + vmem(6),
        out_specs=vmem(4),
        compiler_params=params(16),
        cost_estimate=attn_cost(heads, here, count, width),
        name="attention_forward_near",
    )(place, slopes, se, own, sib, edge, edge_sib, wt)


def attn_far(heads, slopes, se, rows, wt):
    here, (count, width) = se.shape[1], rows.shape
    return pl.pallas_call(
        functools.partial(attend, heads),
        out_shape=attn_fwd_outs(heads, here, count),
        in_specs=[smem()] + vmem(3),
        out_specs=vmem(3),
        compiler_params=params(16),
        cost_estimate=attn_cost(heads, here, count, width),
        name="attention_forward_far",
    )(slopes, se, rows, wt)


def attended_halves(place, near, far, w_out, w_far):
    half, width = near.shape[1] // 2, w_out.shape[1]
    vm = pl.BlockSpec(memory_space=pltpu.VMEM)
    return pl.pallas_call(
        attended_kernel,
        out_shape=[
            jax.ShapeDtypeStruct((half, width), F32),
            jax.ShapeDtypeStruct((half, width), BF),
        ],
        in_specs=[smem()] + [vm] * 4,
        out_specs=[vm] * 2,
        compiler_params=params(12),
        cost_estimate=cost(8 * near.size * width, 12 * half * width),
        name="attended_halves",
    )(place, near, far, w_out, w_far)


def head_back_kernel(head, slopes_ref, se_ref, qkv_ref, kv_ref, dctx_ref, out_ref, acc_ref):
    here = dctx_ref.shape[1]
    mine = slice(head * HD, (head + 1) * HD)
    keys = slice(head * 2 * HD, (head + 1) * 2 * HD)
    acc_ref[...] = jnp.zeros_like(acc_ref)
    edge = jnp.zeros((HD, QB), BF)
    out_ref[0, :, 0:QB] = edge
    out_ref[0, :, QB + here :] = edge
    slope = slopes_ref[head]
    starts = range(0, here, QB)
    pairs = []
    for off in starts:
        query = qkv_ref[0, mine, off + QB : off + 2 * QB] * BF(0.125)
        d_rows = dctx_ref[mine, off : off + QB]
        pairs.append(
            jnp.concatenate(
                [
                    jnp.concatenate([query, edge], axis=1),
                    jnp.concatenate([edge, d_rows], axis=1),
                ],
                axis=0,
            )
        )
    both = [dot(kv_ref[off : off + WINDOW, keys], pair, 1, 0) for off, pair in zip(starts, pairs)]
    probs = [
        softmax(x[:, :QB] - slope * block_distance(se_ref, off)) for off, x in zip(starts, both)
    ]
    row_dots = [jnp.sum(x[:, QB:] * p, axis=0, keepdims=True) for x, p in zip(both, probs)]
    d_scores = [
        (p * (x[:, QB:] - row_dot)).astype(BF) for x, p, row_dot in zip(both, probs, row_dots)
    ]
    probs = [p.astype(BF) for p in probs]
    for off, d in zip(starts, d_scores):
        d_query = dot(qkv_ref[1, mine, off : off + WINDOW], d, 1, 0) * 0.125
        out_ref[0, :, off + QB : off + 2 * QB] = d_query.astype(BF)
    sums = [
        dot(pair, jnp.concatenate([d, p], axis=1), 1, 1)
        for pair, d, p in zip(pairs, d_scores, probs)
    ]
    for off, x in zip(starts, sums):
        acc_ref[:, off : off + WINDOW] += x
    out_ref[1, :, :] = acc_ref[0:HD, :].astype(BF)
    out_ref[2, :, :] = acc_ref[HD:, :].astype(BF)


def head_back(head, slopes, se, qkv, kv, dctx):
    here, count = se.shape[1], qkv.shape[2]
    elements = here * WINDOW
    return pl.pallas_call(
        functools.partial(head_back_kernel, head),
        out_shape=out((3, HD, count)),
        in_specs=[smem()] + vmem(4),
        out_specs=vmem(1)[0],
        scratch_shapes=[pltpu.VMEM((2 * HD, count), F32)],
        compiler_params=params(12),
        cost_estimate=cost(elements * HD * 24, count * HD * 18, elements),
        name="attention_backward_head",
    )(slopes, se, qkv, kv, dctx)


def stack_heads(refs, all_ref):
    heads = len(refs)
    for h, ref in enumerate(refs):
        for part in range(3):
            at = (part * heads + h) * HD
            all_ref[at : at + HD, :] = ref[part]


def qkv_grad_kernel(heads, *refs):
    (rows_ref, *out_refs, all_ref) = refs[heads:]
    stack_heads(refs[:heads], all_ref)
    for c in range(0, rows_ref.shape[1], 256):
        total = dot(all_ref[...], rows_ref[:, c : c + 256], 1, 0).astype(BF)
        at = 0
        for ref in out_refs:
            ref[:, c : c + 256] = total[at : at + ref.shape[0]]
            at += ref.shape[0]


def qkv_grad(heads, rows, parts=(3,)):
    count, width = rows.shape
    size = len(heads) * HD
    return pl.pallas_call(
        functools.partial(qkv_grad_kernel, len(heads)),
        out_shape=[out((part * size, width)) for part in parts],
        in_specs=vmem(len(heads) + 1),
        out_specs=vmem(len(parts)),
        scratch_shapes=[pltpu.VMEM((3 * size, count), BF)],
        compiler_params=params(12),
        cost_estimate=cost(6 * size * count * width, count * width * 4),
        name="projection_gradient",
    )(*heads, rows)


def gather_back_kernel(
    place_ref, ctx_ref, own_ref, sib_ref, norms_ref, norms_sib_ref, w_out_ref, w_far_ref,
    datt_ref, grad_ref, dctx_ref, dctx_far_ref,
):
    even = place_ref[4] == 0
    half = datt_ref.shape[0] // 2
    own, sib = own_ref[...], sib_ref[...]
    datt_ref[0:half, :] = jnp.where(even, own, sib)
    datt_ref[half:, :] = jnp.where(even, sib, own)
    for c in range(0, 2 * half, 256):
        rows = datt_ref[c : c + 256, :]
        dctx_far_ref[:, c : c + 256] = dot(w_far_ref[...], rows, 1, 1).astype(BF)
        dctx_ref[:, c : c + 256] = dot(w_out_ref[...], rows, 1, 1).astype(BF)
    count = ctx_ref.shape[0]
    grad_ref[0:count, :] = dot(ctx_ref[...], datt_ref[...], 1, 0).astype(BF)
    norms = norms_ref[...].astype(F32) + norms_sib_ref[...].astype(F32)
    grad_ref[count:, :] = norms.astype(BF)


def gather_back(place, ctx, own, sib, norms, norms_sib, w_out, w_far):
    half, width = own.shape
    vm = pl.BlockSpec(memory_space=pltpu.VMEM)
    return pl.pallas_call(
        gather_back_kernel,
        out_shape=[
            out((2 * half, width)),
            jax.ShapeDtypeStruct((ctx.shape[0] + NORM_ROWS, width), BF),
            jax.ShapeDtypeStruct(ctx.shape, BF),
            jax.ShapeDtypeStruct(ctx.shape, BF),
        ],
        in_specs=[smem()] + [vm] * 7,
        out_specs=[vm] * 4,
        compiler_params=params(16),
        cost_estimate=cost(6 * ctx.size * width, 12 * half * width),
        name="gather_d_attended",
    )(place, ctx, own, sib, norms, norms_sib, w_out, w_far)


def phi_pair(gate):
    bell = jnp.exp(gate * gate * -0.5)
    t = 1.0 / (1.0 + (0.3275911 / math.sqrt(2.0)) * jnp.abs(gate))
    poly = t * (
        0.254829592
        + t * (-0.284496736 + t * (1.421413741 + t * (-1.453152027 + t * 1.061405429)))
    )
    tail = 0.5 * poly * bell
    return jnp.where(gate >= 0.0, 1.0 - tail, tail), bell * (1.0 / math.sqrt(2.0 * math.pi))


def ff_fwd_kernel(
    x0_ref, x1_ref, wg_ref, wu_ref, wd_ref, x_ref, act_ref, a_ref, b_ref, keep_ref, send_ref
):
    half = x0_ref.shape[0]
    for i, (source, target) in enumerate(((x0_ref, keep_ref), (x1_ref, send_ref))):
        rows = slice(i * half, (i + 1) * half)
        x = source[...]
        x_ref[rows, :] = x
        for f in range(0, wd_ref.shape[0], 256):
            cols = slice(f, f + 256)
            gate = dot(x, wg_ref[:, cols], 1, 0)
            up = dot(x, wu_ref[:, cols], 1, 0)
            big, small = phi_pair(gate)
            gelu = gate * big
            act_ref[rows, cols] = (gelu * up).astype(BF)
            a_ref[rows, cols] = gelu.astype(BF)
            b_ref[rows, cols] = (up * (big + gate * small)).astype(BF)
        target[...] = dot(act_ref[rows, :], wd_ref[...], 1, 0).astype(BF)


def ff_fwd(pieces, wg, wu, wd):
    half, width = pieces[0].shape
    hidden = wd.shape[0]
    rows = 2 * half
    return pl.pallas_call(
        ff_fwd_kernel,
        out_shape=[out((rows, width))] + [out((rows, hidden))] * 3 + [out((half, width))] * 2,
        in_specs=vmem(5),
        out_specs=vmem(6),
        compiler_params=params(16),
        cost_estimate=cost(rows * width * hidden * 6, 12 * rows * width, 2 * rows * hidden),
        name="ff_forward",
    )(*pieces, wg, wu, wd)


def ff_bwd_kernel(
    d0_ref, d1_ref, a_ref, b_ref, wd_ref, wg_ref, wu_ref,
    db_ref, dg_ref, du_ref, keep_ref, send_ref,
):
    half = d0_ref.shape[0]
    for i, (source, target) in enumerate(((d0_ref, keep_ref), (d1_ref, send_ref))):
        rows = slice(i * half, (i + 1) * half)
        db = source[...]
        db_ref[rows, :] = db
        for f in range(0, wd_ref.shape[0], 256):
            cols = slice(f, f + 256)
            d_active = dot(db, wd_ref[cols, :], 1, 1)
            dg_ref[rows, cols] = (d_active * b_ref[rows, cols].astype(F32)).astype(BF)
            du_ref[rows, cols] = (d_active * a_ref[rows, cols].astype(F32)).astype(BF)
        part = dot(dg_ref[rows, :], wg_ref[...], 1, 1) + dot(du_ref[rows, :], wu_ref[...], 1, 1)
        target[...] = part.astype(BF)


def ff_bwd(pieces, a, b, wd, wg, wu):
    half, width = pieces[0].shape
    hidden = wd.shape[0]
    rows = 2 * half
    return pl.pallas_call(
        ff_bwd_kernel,
        out_shape=[out((rows, width))] + [out((rows, hidden))] * 2 + [out((half, width))] * 2,
        in_specs=vmem(7),
        out_specs=vmem(5),
        compiler_params=params(16),
        cost_estimate=cost(rows * width * hidden * 6, 12 * rows * width),
        name="ff_backward",
    )(*pieces, a, b, wd, wg, wu)


def weight_near_kernel(a_ref, d_ref, out_ref):
    out_ref[...] = dot(a_ref[...], d_ref[...], 0, 0)


def weight_near(a, d):
    size = (a.shape[1], d.shape[1])
    return pl.pallas_call(
        weight_near_kernel,
        out_shape=out(size, F32),
        in_specs=vmem(2),
        out_specs=vmem(1)[0],
        compiler_params=params(16),
        cost_estimate=cost(2 * a.size * d.shape[1], a.size * 8),
        name="weight_gradient_near",
    )(a, d)


def weight_far_kernel(dim, place_ref, acc_ref, a_ref, d_ref, out_ref, sent_ref):
    out_ref[...] = (acc_ref[...] + dot(a_ref[...], d_ref[...], 0, 0)).astype(BF)
    half = sent_ref.shape[0]
    at = (1 - place_ref[dim]) * half
    sent_ref[...] = out_ref[pl.ds(pl.multiple_of(at, half), half), :]


def weight_far(place, dim, acc, a, d):
    rows, width = acc.shape
    return pl.pallas_call(
        functools.partial(weight_far_kernel, dim),
        out_shape=[out((rows, width)), out((rows // 2, width))],
        in_specs=[smem()] + vmem(3),
        out_specs=vmem(2),
        compiler_params=params(16),
        cost_estimate=cost(2 * a.size * d.shape[1], a.size * 12),
        name="weight_gradient_far",
    )(place, acc, a, d)


def centre(pre):
    mean = jnp.mean(pre, axis=-1, keepdims=True)
    centred = pre - mean
    r = lax.rsqrt(jnp.mean(centred * centred, axis=-1, keepdims=True) + EPSILON)
    return centred * r, r


def norm_back(xhat, r, gain, grad):
    e = grad * gain
    return r * (
        e
        - jnp.mean(e, axis=-1, keepdims=True)
        - xhat * jnp.mean(e * xhat, axis=-1, keepdims=True)
    )


def ln1_kernel(x_ref, own_ref, recv_ref, gain_ref, bias_ref, pre_ref, normed_ref, low_ref):
    pre = x_ref[...].astype(F32) + (own_ref[...] + recv_ref[...].astype(F32))
    pre_ref[...] = pre
    xhat, _ = centre(pre)
    normed = xhat * gain_ref[...] + bias_ref[...]
    normed_ref[...] = normed
    low_ref[...] = normed.astype(BF)


def ln1(x, own, recv, gain, bias):
    shape = x.shape
    vm = pl.BlockSpec(memory_space=pltpu.VMEM)
    return pl.pallas_call(
        ln1_kernel,
        out_shape=[
            jax.ShapeDtypeStruct(shape, F32),
            jax.ShapeDtypeStruct(shape, F32),
            jax.ShapeDtypeStruct(shape, BF),
        ],
        in_specs=[vm] * 5,
        out_specs=[vm] * 3,
        compiler_params=params(12),
        cost_estimate=cost(x.size * 10, x.size * 18),
        name="norm_one",
    )(x, own, recv, gain, bias)


def ln2_kernel(
    normed_ref, keep_ref, near_ref, far_ref, dy_ref, gain_ref, bias_ref,
    out_ref, d_ref, low_ref, grads_ref,
):
    branch = (
        keep_ref[...].astype(F32) + near_ref[...].astype(F32) + far_ref[...].astype(F32)
    )
    xhat, r = centre(normed_ref[...] + branch)
    gain = gain_ref[...]
    out_ref[...] = (xhat * gain + bias_ref[...]).astype(BF)
    dy = dy_ref[...].astype(F32)
    d = norm_back(xhat, r, gain, dy)
    d_ref[...] = d
    low_ref[...] = d.astype(BF)
    grads_ref[0:1, :] = jnp.sum(dy * xhat, axis=0, keepdims=True)
    grads_ref[1:2, :] = jnp.sum(dy, axis=0, keepdims=True)


def ln2(normed, keep, near, far, dy, gain, bias):
    shape = far.shape
    vm = pl.BlockSpec(memory_space=pltpu.VMEM)
    return pl.pallas_call(
        ln2_kernel,
        out_shape=[
            jax.ShapeDtypeStruct(shape, BF),
            jax.ShapeDtypeStruct(shape, F32),
            jax.ShapeDtypeStruct(shape, BF),
            jax.ShapeDtypeStruct((2, shape[1]), F32),
        ],
        in_specs=[vm] * 7,
        out_specs=[vm] * 4,
        compiler_params=params(16),
        cost_estimate=cost(far.size * 20, far.size * 20),
        name="norm_two",
    )(normed, keep, near, far, dy, gain, bias)


def ln1_back_kernel(
    pre_ref, d2_ref, keep_ref, near_ref, far_ref, gain_ref, grads_two_ref,
    d_ref, low_ref, norms_ref,
):
    grad = d2_ref[...] + (
        keep_ref[...].astype(F32) + near_ref[...].astype(F32) + far_ref[...].astype(F32)
    )
    xhat, r = centre(pre_ref[...])
    d = norm_back(xhat, r, gain_ref[...], grad)
    d_ref[...] = d
    width = d.shape[1]
    low_ref[...] = d.astype(BF)
    norms_ref[...] = jnp.concatenate(
        [
            jnp.sum(grad * xhat, axis=0, keepdims=True),
            jnp.sum(grad, axis=0, keepdims=True),
            grads_two_ref[...],
            jnp.zeros((NORM_ROWS - 4, width), F32),
        ],
        axis=0,
    ).astype(BF)


def ln1_back(pre, d2, keep, near, far, gain, grads_two):
    shape = far.shape
    vm = pl.BlockSpec(memory_space=pltpu.VMEM)
    return pl.pallas_call(
        ln1_back_kernel,
        out_shape=[
            jax.ShapeDtypeStruct(shape, F32),
            jax.ShapeDtypeStruct(shape, BF),
            jax.ShapeDtypeStruct((NORM_ROWS, shape[1]), BF),
        ],
        in_specs=[vm] * 7,
        out_specs=[vm] * 3,
        compiler_params=params(16),
        cost_estimate=cost(far.size * 20, far.size * 20),
        name="norm_one_backward",
    )(pre, d2, keep, near, far, gain, grads_two)


def swap(value, axis, bit):
    count = lax.axis_size(axis)
    return lax.ppermute(value, axis, [(i, i ^ bit) for i in range(count)])


def swap_chip_edges(value):
    count = lax.axis_size("seq") * lax.axis_size("tp")
    pairs = []
    for i in range(1, count - 1, 2):
        pairs += [(i, i + 1), (i + 1, i)]
    return lax.ppermute(value, ("seq", "tp"), pairs)


def fold_kernel(dims, place_ref, own_ref, recv_ref, keep_ref, send_ref):
    rows, half = recv_ref.shape[0], keep_ref.shape[0]
    base = place_ref[dims[0]] * rows
    cut = place_ref[dims[1]] * half
    for ref, at in ((keep_ref, cut), (send_ref, half - cut)):
        own = own_ref[pl.ds(pl.multiple_of(base + at, NORM_ROWS), half), :].astype(F32)
        recv = recv_ref[pl.ds(pl.multiple_of(at, NORM_ROWS), half), :].astype(F32)
        ref[...] = (own + recv).astype(BF)


def fold(place, dims, own, recv):
    rows, width = recv.shape
    vm = pl.BlockSpec(memory_space=pltpu.VMEM)
    return pl.pallas_call(
        functools.partial(fold_kernel, dims),
        out_shape=[jax.ShapeDtypeStruct((rows // 2, width), BF)] * 2,
        in_specs=[smem(), vm, vm],
        out_specs=[vm] * 2,
        compiler_params=params(10),
        cost_estimate=cost(recv.size, recv.size * 6),
        name="fold_half",
    )(place, own, recv)


def join_kernel(dim, place_ref, own_ref, recv_ref, out_ref):
    first = place_ref[dim] == 0
    half = own_ref.shape[0]
    own, recv = own_ref[...], recv_ref[...]
    out_ref[0:half, :] = jnp.where(first, own, recv).astype(out_ref.dtype)
    out_ref[half:, :] = jnp.where(first, recv, own).astype(out_ref.dtype)


def join(place, dim, own, recv, kind=BF):
    half, width = own.shape
    vm = pl.BlockSpec(memory_space=pltpu.VMEM)
    return pl.pallas_call(
        functools.partial(join_kernel, dim),
        out_shape=jax.ShapeDtypeStruct((2 * half, width), kind),
        in_specs=[smem(), vm, vm],
        out_specs=vm,
        compiler_params=params(10),
        cost_estimate=cost(0, own.size * 12),
        name="join_halves",
    )(place, own, recv)


def finish_in_kernel(dims, place_ref, g_ref, g_recv_ref, u_ref, u_recv_ref, out_ref):
    half = g_ref.shape[0]
    for i, (own_ref, recv_ref) in enumerate(((g_ref, g_recv_ref), (u_ref, u_recv_ref))):
        first = place_ref[dims[i]] == 0
        own, recv = own_ref[...], recv_ref[...]
        out_ref[0:half, i, :] = jnp.where(first, own, recv).astype(F32)
        out_ref[half:, i, :] = jnp.where(first, recv, own).astype(F32)


def finish_in(place, gate, up):
    half, width = gate[1].shape
    return pl.pallas_call(
        functools.partial(finish_in_kernel, (gate[0], up[0])),
        out_shape=out((2 * half, 2, width), F32),
        in_specs=[smem()] + vmem(4),
        out_specs=vmem(1)[0],
        compiler_params=params(16),
        cost_estimate=cost(0, gate[1].size * 24),
        name="finish_w_in_gradient",
    )(place, *gate[1:], *up[1:])


def finish_a_kernel(dim, place_ref, own_ref, recv_ref, _, out_ref):
    join_kernel(dim, place_ref, own_ref, recv_ref, out_ref)


def finish_a(place, dim, own, recv, later):
    half, width = own.shape
    return pl.pallas_call(
        functools.partial(finish_a_kernel, dim),
        grid=(1,),
        out_shape=jax.ShapeDtypeStruct(later.shape, F32),
        in_specs=[smem()]
        + [full((half, width))] * 2
        + [pl.BlockSpec(memory_space=pl.ANY)],
        out_specs=pl.BlockSpec((2 * half, width), lambda i: (0, 0)),
        input_output_aliases={3: 0},
        compiler_params=params(10),
        cost_estimate=cost(0, own.size * 12),
        name="finish_attention_gradient_a",
    )(place, own, recv, later)


def finish_b_kernel(dim, place_ref, own_ref, recv_ref, qkv_ref, out_ref, norm_ref):
    first = place_ref[dim] == 0
    own, recv = own_ref[...], recv_ref[...]
    step = own.shape[0] // 2
    count = step - NORM_ROWS
    low = jnp.where(first, own, recv).astype(F32)
    high = jnp.where(first, recv, own).astype(F32)
    for ref, rows in ((qkv_ref, low), (out_ref, high)):
        ref[0:count, :] = rows[0:count]
        ref[count:, :] = rows[step : step + count]
    norm_ref[...] = low[count : count + 4]


def finish_b(place, dim, own, recv, rows):
    half, width = own.shape
    rest = half - 2 * NORM_ROWS
    return pl.pallas_call(
        functools.partial(finish_b_kernel, dim),
        grid=(1,),
        out_shape=[
            jax.ShapeDtypeStruct((rows, width), F32),
            jax.ShapeDtypeStruct((rest, width), F32),
            jax.ShapeDtypeStruct((4, width), F32),
        ],
        in_specs=[smem()] + [full((half, width))] * 2,
        out_specs=[
            pl.BlockSpec((rest, width), lambda i: (rows // rest - 1, 0)),
            full((rest, width)),
            full((4, width)),
        ],
        compiler_params=params(10),
        cost_estimate=cost(0, own.size * 12),
        name="finish_attention_gradient_b",
    )(place, own, recv)


def send_half(place_ref, dim, ref, sent_ref):
    count = sent_ref.shape[0]
    at = (1 - place_ref[dim]) * count
    sent_ref[...] = ref[pl.ds(pl.multiple_of(at, NORM_ROWS), count), :]


def cut_a_kernel(dim, place_ref, own_ref, far_ref, a_ref, sent_ref):
    half = a_ref.shape[0]
    total = own_ref[0:half, :].astype(F32) + far_ref[...].astype(F32)
    a_ref[...] = total.astype(BF)
    send_half(place_ref, dim, a_ref, sent_ref)


def cut_a(place, dim, own, far):
    rows, width = far.shape
    return pl.pallas_call(
        functools.partial(cut_a_kernel, dim),
        out_shape=[out((rows, width)), out((rows // 2, width))],
        in_specs=[smem()] + vmem(2),
        out_specs=vmem(2),
        compiler_params=params(12),
        cost_estimate=cost(far.size, far.size * 8),
        name="add_far_shard_a",
    )(place, own, far)


def cut_b_kernel(dim, place_ref, own_ref, far_ref, out_ref, b_ref, sent_ref):
    rows = far_ref.shape[0]
    start = own_ref.shape[0] - rows
    value = (own_ref[start:, :].astype(F32) + far_ref[...].astype(F32)).astype(BF)
    step = b_ref.shape[0] // 4
    count = step - NORM_ROWS
    for i in range(4):
        at = (i % 2) * count
        source = value if i < 2 else out_ref
        b_ref[i * step : i * step + count, :] = source[at : at + count, :]
        b_ref[i * step + count : (i + 1) * step, :] = out_ref[2 * count :, :]
    send_half(place_ref, dim, b_ref, sent_ref)


def cut_b(place, dim, own, far, out_rows):
    width = own.shape[1]
    rows = far.shape[0] + out_rows.shape[0] + 3 * NORM_ROWS
    return pl.pallas_call(
        functools.partial(cut_b_kernel, dim),
        out_shape=[out((rows, width)), out((rows // 2, width))],
        in_specs=[smem()] + vmem(3),
        out_specs=vmem(2),
        compiler_params=params(12),
        cost_estimate=cost(far.size, far.size * 8),
        name="add_far_shard_b",
    )(place, own, far, out_rows)


def out_grad_kernel(ctx_ref, datt_ref, own_ref, far_ref, out_ref):
    count = ctx_ref.shape[0]
    near = dot(ctx_ref[...], datt_ref[...], 1, 0)
    out_ref[0:count, :] = (near + far_ref[0:count, :].astype(F32)).astype(BF)
    norms = own_ref[count:, :].astype(F32) + far_ref[count:, :].astype(F32)
    out_ref[count:, :] = norms.astype(BF)


def out_grad(ctx, datt, own, far):
    vm = pl.BlockSpec(memory_space=pltpu.VMEM)
    return pl.pallas_call(
        out_grad_kernel,
        out_shape=jax.ShapeDtypeStruct(far.shape, BF),
        in_specs=[vm] * 4,
        out_specs=vm,
        compiler_params=params(12),
        cost_estimate=cost(2 * ctx.size * datt.shape[1], datt.size * 2),
        name="out_gradient",
    )(ctx, datt, own, far)


class SeqSum:
    def __init__(self, place, order, dims, g, sent=None, last=None):
        self.place, self.order, self.dims, self.value = place, order, dims, g
        self.last = last
        self.stage = 1
        self.pairwise = lax.axis_size("seq") == 8
        if not self.pairwise:
            whole = lax.psum(g, "seq")
            half = g.shape[0] // 2
            self.dims = (len(dims),)
            self.value, self.moving = whole[:half], whole[half:]
            return
        if sent is None:
            half = g.shape[0] // 2
            sent = lax.dynamic_slice_in_dim(g, (1 - place[dims[0]]) * half, half, 0)
        self.send(0, sent)

    def send(self, dim, value):
        self.moving = swap(value, "seq", 1 << self.dims[dim])

    def step(self):
        stage, place, order, dims = self.stage, self.place, self.order, self.dims
        self.stage += 1
        if not self.pairwise and stage < 5:
            return
        value, moved = self.value, self.moving
        if stage < 5 or self.last is not None:
            value = order(value)
        if stage == 1:
            self.value, sent = fold(place, dims[:2], value, moved)
            order.note(sent)
            self.send(1, sent)
        elif stage in (2, 3):
            self.value = order.note(add(value, moved))
            self.send(2 if stage == 2 else 1, self.value)
        elif stage == 4:
            self.value = order.note(join(place, dims[1], value, moved))
            self.send(0, self.value)
        elif stage == 5:
            if self.last is None:
                self.result = (dims[0], self.value, moved)
                return
            self.result = self.last(place, dims[0], value, moved)
            order.note(jax.tree.leaves(self.result)[-1])


def add_kernel(a_ref, b_ref, out_ref):
    out_ref[...] = (a_ref[...].astype(F32) + b_ref[...].astype(F32)).astype(BF)


def add(a, b):
    return pl.pallas_call(
        add_kernel,
        out_shape=out(a.shape),
        in_specs=vmem(2),
        out_specs=vmem(1)[0],
        compiler_params=params(10),
        cost_estimate=cost(a.size, a.size * 6),
        name="add_pair",
    )(a, b)


def input_grad_kernel(place_ref, *refs):
    (*heads, wt_ref, wt_far_ref, own_ref, sent_ref, near_ref, far_ref) = refs
    stack_heads(heads[: len(heads) // 2], near_ref)
    stack_heads(heads[len(heads) // 2 :], far_ref)
    half = own_ref.shape[0]
    for ref, which in ((sent_ref, 1 - place_ref[4]), (own_ref, place_ref[4])):
        here = pl.ds(pl.multiple_of(which * half, 128), half)
        total = dot(near_ref[:, here], wt_ref[...], 0, 0)
        ref[...] = (total + dot(far_ref[:, here], wt_far_ref[...], 0, 0)).astype(ref.dtype)


def input_grad(place, near, far, wt, wt_far):
    count = near[0].shape[2]
    half, (size, width) = count // 2, wt.shape
    vm = pl.BlockSpec(memory_space=pltpu.VMEM)
    return pl.pallas_call(
        input_grad_kernel,
        out_shape=[
            jax.ShapeDtypeStruct((half, width), F32),
            jax.ShapeDtypeStruct((half, width), BF),
        ],
        in_specs=[smem()] + [vm] * (2 * len(near) + 2),
        out_specs=[vm] * 2,
        scratch_shapes=[pltpu.VMEM((size, count), BF)] * 2,
        compiler_params=params(16),
        cost_estimate=cost(4 * size * count * width, 12 * half * width),
        name="input_gradient",
    )(place, *near, *far, wt, wt_far)


def input_rows_kernel(place_ref, own_ref, recv_ref, pre_ref, out_ref, edge_ref):
    count, edge = out_ref.shape[0], edge_ref.shape[0]
    core = place_ref[4]
    at = pl.ds(pl.multiple_of(core * count, edge), edge)
    edge_ref[...] = (own_ref[at, :] + recv_ref[at, :].astype(F32)).astype(BF)
    at = pl.ds(pl.multiple_of((1 - core) * edge, edge), count)
    out_ref[...] = pre_ref[...] + (own_ref[at, :] + recv_ref[at, :].astype(F32))


def input_rows(place, own, recv, pre):
    vm = pl.BlockSpec(memory_space=pltpu.VMEM)
    return pl.pallas_call(
        input_rows_kernel,
        out_shape=[
            jax.ShapeDtypeStruct(pre.shape, F32),
            jax.ShapeDtypeStruct((QB, pre.shape[1]), BF),
        ],
        in_specs=[smem()] + [vm] * 3,
        out_specs=[vm] * 2,
        compiler_params=params(16),
        cost_estimate=cost(pre.size * 2, pre.size * 16),
        name="input_gradient_rows",
    )(place, own, recv, pre)


def input_edge_kernel(place_ref, rows_ref, edge_ref, out_ref):
    out_ref[...] = rows_ref[...]
    edge = edge_ref.shape[0]
    start = place_ref[4] * (rows_ref.shape[0] - edge)
    at = pl.ds(pl.multiple_of(start, edge), edge)
    out_ref[at, :] = rows_ref[at, :] + edge_ref[...].astype(F32)


def input_edge(place, rows, edge):
    vm = pl.BlockSpec(memory_space=pltpu.VMEM)
    return pl.pallas_call(
        input_edge_kernel,
        out_shape=jax.ShapeDtypeStruct(rows.shape, F32),
        in_specs=[smem()] + [vm] * 2,
        out_specs=vm,
        compiler_params=params(12),
        cost_estimate=cost(rows.size, rows.size * 10),
        name="input_gradient_edge",
    )(place, rows, edge)


def per_device(
    inputs, lengths, w_qkv, w_out, w_in, w_down, ln1_gain, ln1_bias, ln2_gain, ln2_bias, cotangent
):
    own_rows, width = inputs.shape
    tp_count = lax.axis_size("tp")
    head_width = w_qkv.shape[2]
    heads = head_width // HD
    chip_rows = 2 * own_rows
    tp = lax.axis_index("tp")
    seq = lax.axis_index("seq")
    core = tp & 1
    even = core == 0
    first = (seq * tp_count + 2 * (tp >> 1)) * own_rows
    place = jnp.stack([seq & 1, (seq >> 1) & 1, (seq >> 2) & 1, 0 * core, core]).astype(jnp.int32)

    bounds = jnp.cumsum(lengths)[:, None]
    tokens = (first + jnp.arange(chip_rows, dtype=jnp.int32))[None, :]
    before = bounds <= tokens
    start = jnp.max(jnp.where(before, bounds, 0), axis=0)
    end = jnp.min(jnp.where(before, jnp.iinfo(jnp.int32).max, bounds), axis=0)
    se = jnp.stack([start, end]) - (first - QB)
    se = jnp.pad(se, ((0, 6), (0, 0)))
    table = jnp.asarray(slope_table(HEADS))
    slopes = lax.dynamic_slice_in_dim(table, tp * heads, heads)
    slopes_far = lax.dynamic_slice_in_dim(table, (tp ^ 2) * heads, heads)

    wt = w_qkv.transpose(0, 2, 1).reshape(3 * head_width, width)
    wt_far = swap(wt, "tp", 2)

    sibling = swap(inputs, "tp", 1)
    edge = swap_chip_edges(
        lax.dynamic_slice_in_dim(inputs, core * (own_rows - QB), QB, axis=0)
    )
    edge_sibling = swap(edge, "tp", 1)
    rows, ctx, qkv, kv = attn_near(
        heads, place, slopes, se, inputs, sibling, edge, edge_sibling,
        wt.reshape(3, head_width, width),
    )
    w_out_far = swap(after(w_out, ctx), "tp", 2)
    ctx_far, qkv_far, kv_far = attn_far(
        heads, slopes_far, se, rows, wt_far.reshape(3, head_width, width)
    )
    attended, attended_sent = attended_halves(place, ctx, ctx_far, w_out, w_out_far)
    attended_sent = swap(attended_sent, "tp", 1)
    gain1, bias1 = ln1_gain[None], ln1_bias[None]
    gain2, bias2 = ln2_gain[None], ln2_bias[None]
    pre_one, normed, low = ln1(inputs, attended, attended_sent, gain1, bias1)

    order = Order()
    w_in_late = after(w_in, low)
    wg, wu = w_in_late[:, 0], w_in_late[:, 1]

    def both_ways(own, work, between=lambda near_out: None):
        far = swap(own, "tp", 2)
        near_out = work(0, own, order(swap(own, "tp", 1)))
        near_keep, near_send = near_out[-2:]
        order.note(near_send)
        recv = swap(near_send, "tp", 1)
        between(near_out)
        far = order(far)
        far_out = work(1, far, swap(far, "tp", 1))
        far_keep, far_send = far_out[-2:]
        order.note(far_send)
        from_sibling = swap(far_send, "tp", 1)
        far_sum = order.note(add(order(far_keep), from_sibling))
        return (near_out, far_out), (near_keep, recv, swap(far_sum, "tp", 2))

    order.note(low)
    forward, parts = both_ways(low, lambda i, a, b: ff_fwd((a, b), wg, wu, w_down))
    layer_out, d_pre_two, d_branch, grads_two = ln2(
        normed, order(parts[0]), *parts[1:], cotangent, gain2, bias2
    )
    order.note(d_branch)

    weight_near_parts = []

    def grads_between(near_out):
        for x, d in weight_pairs:
            part = weight_near(order(forward[0][x]), near_out[d])
            weight_near_parts.append(order.note(part))

    weight_pairs = ((1, 0), (0, 2), (0, 1))
    backward, parts = both_ways(
        d_branch,
        lambda i, a, b: ff_bwd((a, b), forward[i][2], forward[i][3], w_down, wg, wu),
        grads_between,
    )

    def join_whole(*halves):
        return join(*halves, F32)

    def weight_sum(which, dims):
        x, d = weight_pairs[which]
        total, sent = weight_far(
            place, dims[0], weight_near_parts[which], order(forward[1][x]), backward[1][d]
        )
        order.note(sent)
        return SeqSum(place, order, dims, total, sent, None if which else join_whole)

    d_far, d_near = [], []

    def one_head(h, far):
        kept = (slopes_far, se, qkv_far, kv_far) if far else (slopes, se, qkv, kv)
        return order.note(head_back(h, *kept, order(d_ctx_far if far else d_ctx)))

    down = weight_sum(0, (0, 1, 2))
    up = weight_sum(1, (1, 0, 2))
    gate = weight_sum(2, (0, 1, 2))
    d_pre_one, half, norms = ln1_back(
        pre_one, d_pre_two, order(parts[0]), *parts[1:], gain1, grads_two
    )
    order.note(half)
    half_sibling = swap(half, "tp", 1)
    norms_sibling = swap(norms, "tp", 1)
    down.step()
    up.step()
    d_attended, sent_out, d_ctx, d_ctx_far = gather_back(
        place, order(ctx_far), half, half_sibling, norms, norms_sibling, w_out, w_out_far
    )
    order.note(d_ctx_far)
    far_out = swap(sent_out, "tp", 2)
    d_near.append(one_head(0, False))
    down.step()
    d_far.append(one_head(0, True))
    d_far.append(one_head(1, True))
    d_near.append(one_head(1, False))
    gate.step()
    d_far.append(one_head(2, True))
    up.step()
    grad_out = order.note(out_grad(ctx, order(d_attended), sent_out, far_out))
    far_qk, far_v = qkv_grad(d_far, order(rows), (2, 1))
    order.note(far_v)
    far_v = swap(far_v, "tp", 2)
    far_qk = swap(far_qk, "tp", 2)
    down.step()
    d_near.append(one_head(2, False))
    (own_qkv,) = qkv_grad(d_near, order(rows))
    order.note(own_qkv)
    window_own, window_sent = input_grad(
        place, [order(d_near[0]), *d_near[1:]], d_far, wt, wt_far
    )
    order.note(window_sent)
    window_sent = swap(window_sent, "tp", 1)
    down.step()
    up.step()
    total, sent = cut_a(place, 0, order(own_qkv), far_qk)
    order.note(sent)
    attn_a = SeqSum(place, order, (0, 1, 2), total, sent, lambda *h: finish_a(*h, attn_b.result[0]))
    total, sent = cut_b(place, 1, order(own_qkv), far_v, grad_out)
    order.note(sent)
    attn_b = SeqSum(
        place, order, (1, 0, 2), total, sent, lambda *h: finish_b(*h, own_qkv.shape[0])
    )
    gate.step()
    attn_a.step()
    attn_b.step()
    down.step()
    gate.step()
    attn_a.step()
    grad_rows, d_edge = input_rows(place, order(window_own), window_sent, d_pre_one)
    order.note(d_edge)
    d_edge = swap_chip_edges(d_edge)
    attn_b.step()
    up.step()
    grad_input = order.note(input_edge(place, order(grad_rows), d_edge))
    attn_a.step()
    gate.step()
    attn_b.step()
    attn_b.step()
    attn_a.step()
    up.step()
    attn_b.step()
    gate.step()
    attn_a.step()
    grad_in = order.note(
        finish_in(order(place), gate.result, up.result)
    )
    assert all(unit.stage == 6 for unit in (down, gate, up, attn_a, attn_b))
    grad_down = down.result
    _, grad_out, norm_grads = attn_b.result
    grad_qkv = attn_a.result
    grad_qkv = grad_qkv.reshape(3, head_width, width).transpose(0, 2, 1)
    return (
        layer_out,
        grad_input,
        grad_qkv,
        grad_out,
        grad_in,
        grad_down,
        norm_grads[0],
        norm_grads[1],
        norm_grads[2],
        norm_grads[3],
    )


def solution(mesh):
    in_specs = (
        P(("seq", "tp"), None),
        P(),
        P(None, None, "tp"),
        P("tp", None),
        P(None, None, "tp"),
        P("tp", None),
        P(),
        P(),
        P(),
        P(),
        P(("seq", "tp"), None),
    )
    out_specs = (
        P(("seq", "tp"), None),
        P(("seq", "tp"), None),
        P(None, None, "tp"),
        P("tp", None),
        P(None, None, "tp"),
        P("tp", None),
        P(),
        P(),
        P(),
        P(),
    )
    return jax.shard_map(
        per_device, mesh=mesh, in_specs=in_specs, out_specs=out_specs, check_vma=False
    )
```

```python
import functools
import math

import jax
import jax.numpy as jnp
import numpy as np
from jax import lax
from jax.experimental import pallas as pl
from jax.experimental.pallas import tpu as pltpu
from jax.sharding import PartitionSpec as P

HEADS = 12
HD = 64
PIECES = 2
NORM_ROWS = 16
QB = 128
WINDOW = 3 * QB
EPSILON = 1e-12
FAR = 1e30

BF = jnp.bfloat16
F32 = jnp.float32


def dot(a, b, ca, cb):
    return lax.dot_general(a, b, (((ca,), (cb,)), ((), ())), preferred_element_type=F32)


def slope_table(count):
    power_two = 2 ** int(math.floor(math.log2(count)))
    leading = [2.0 ** (-8.0 * (head + 1) / power_two) for head in range(power_two)]
    trailing = [2.0 ** (-4.0 * (2 * other + 1) / power_two) for other in range(count - power_two)]
    return np.array(leading + trailing, np.float32)


def smem():
    return pl.BlockSpec(memory_space=pltpu.SMEM)


def full(shape):
    return pl.BlockSpec(shape, lambda *_: (0,) * len(shape))


def cost(flops, moved, transcendentals=0):
    return pl.CostEstimate(
        flops=flops // 1000,
        bytes_accessed=moved // 1000,
        transcendentals=transcendentals // 1000,
    )


def params(mib):
    return pltpu.CompilerParams(vmem_limit_bytes=mib * 1024 * 1024)


def out(shape, kind=BF):
    return jax.ShapeDtypeStruct(shape, kind)


def vmem(count):
    return [pl.BlockSpec(memory_space=pltpu.VMEM)] * count


def after(value, *others):
    return lax.optimization_barrier((value, others))[0]


class Order:
    def __init__(self):
        self.last = ()

    def __call__(self, value):
        return after(value, *self.last)

    def note(self, value):
        self.last = (value,)
        return value


def block_distance(se_ref, off):
    start = se_ref[0:1, pl.ds(off, QB)] - off
    end = se_ref[1:2, pl.ds(off, QB)] - off
    key = lax.broadcasted_iota(jnp.int32, (WINDOW, QB), 0)
    query = lax.broadcasted_iota(jnp.int32, (WINDOW, QB), 1) + QB
    valid = (key >= start) & (key < end)
    return jnp.where(valid, jnp.abs(key - query).astype(F32), FAR)


def softmax(scores):
    shifted = jnp.exp(scores - jnp.max(scores, axis=0, keepdims=True))
    return shifted * (1.0 / jnp.sum(shifted, axis=0, keepdims=True))


def attend(heads, slopes_ref, se_ref, rows_ref, wt_ref, ctx_ref, qkv_ref, kv_ref):
    zero = jnp.zeros((HD, QB), BF)
    starts = range(0, ctx_ref.shape[1], QB)
    for h in range(heads):
        mine = slice(h * HD, (h + 1) * HD)
        pair = slice(h * 2 * HD, (h + 1) * 2 * HD)
        weights = wt_ref[:, mine, :].reshape(3 * HD, wt_ref.shape[2])
        for c in range(0, rows_ref.shape[0], 256):
            rows = rows_ref[c : c + 256, :]
            turned = dot(weights, rows, 1, 1).astype(BF)
            qkv_ref[:, mine, c : c + 256] = turned.reshape(3, HD, 256)
            kv_ref[c : c + 256, pair] = dot(rows, weights[HD:], 1, 1).astype(BF)
        scores = []
        for off in starts:
            query = qkv_ref[0, mine, off + QB : off + 2 * QB] * BF(0.125)
            key = kv_ref[off : off + WINDOW, pair]
            scores.append(dot(key, jnp.concatenate([query, zero], axis=0), 1, 0))
        probs = [
            softmax(x - slopes_ref[h] * block_distance(se_ref, off)).astype(BF)
            for off, x in zip(starts, scores)
        ]
        for off, x in zip(starts, probs):
            value = qkv_ref[2, mine, off : off + WINDOW]
            ctx_ref[mine, off : off + QB] = dot(value, x, 1, 0).astype(BF)


def attn_near_kernel(
    heads, place_ref, slopes_ref, se_ref, own_ref, sib_ref, edge_ref, edge_sib_ref, wt_ref,
    rows_ref, ctx_ref, qkv_ref, kv_ref,
):
    even = place_ref[4] == 0
    count = own_ref.shape[0]
    own, sib, edge, edge_sib = (r[...] for r in (own_ref, sib_ref, edge_ref, edge_sib_ref))
    rows_ref[0:QB, :] = jnp.where(even, edge, edge_sib)
    rows_ref[QB : QB + count, :] = jnp.where(even, own, sib)
    rows_ref[QB + count : QB + 2 * count, :] = jnp.where(even, sib, own)
    rows_ref[QB + 2 * count :, :] = jnp.where(even, edge_sib, edge)
    attend(heads, slopes_ref, se_ref, rows_ref, wt_ref, ctx_ref, qkv_ref, kv_ref)


def attended_kernel(place_ref, near_ref, far_ref, w_out_ref, w_far_ref, own_ref, sent_ref):
    count = own_ref.shape[0]
    for ref, which in ((sent_ref, 1 - place_ref[4]), (own_ref, place_ref[4])):
        here = pl.ds(pl.multiple_of(which * count, 128), count)
        near = dot(near_ref[:, here], w_out_ref[...], 0, 0)
        ref[...] = (near + dot(far_ref[:, here], w_far_ref[...], 0, 0)).astype(ref.dtype)


def attn_fwd_outs(heads, here, count):
    return [
        out((heads * HD, here)),
        out((3, heads * HD, count)),
        out((count, heads * 2 * HD)),
    ]


def attn_cost(heads, here, count, width):
    elements = heads * here * WINDOW
    flops = elements * HD * 8 + 10 * heads * HD * count * width
    return cost(flops, count * width * 8, elements)


def attn_near(heads, place, slopes, se, own, sib, edge, edge_sib, wt):
    here, width = se.shape[1], own.shape[1]
    count = here + 2 * QB
    return pl.pallas_call(
        functools.partial(attn_near_kernel, heads),
        out_shape=[out((count, width))] + attn_fwd_outs(heads, here, count),
        in_specs=[smem(), smem()] + vmem(6),
        out_specs=vmem(4),
        compiler_params=params(16),
        cost_estimate=attn_cost(heads, here, count, width),
        name="attention_forward_near",
    )(place, slopes, se, own, sib, edge, edge_sib, wt)


def attn_far(heads, slopes, se, rows, wt):
    here, (count, width) = se.shape[1], rows.shape
    return pl.pallas_call(
        functools.partial(attend, heads),
        out_shape=attn_fwd_outs(heads, here, count),
        in_specs=[smem()] + vmem(3),
        out_specs=vmem(3),
        compiler_params=params(16),
        cost_estimate=attn_cost(heads, here, count, width),
        name="attention_forward_far",
    )(slopes, se, rows, wt)


def attended_halves(place, near, far, w_out, w_far):
    half, width = near.shape[1] // 2, w_out.shape[1]
    vm = pl.BlockSpec(memory_space=pltpu.VMEM)
    return pl.pallas_call(
        attended_kernel,
        out_shape=[
            jax.ShapeDtypeStruct((half, width), F32),
            jax.ShapeDtypeStruct((half, width), BF),
        ],
        in_specs=[smem()] + [vm] * 4,
        out_specs=[vm] * 2,
        compiler_params=params(12),
        cost_estimate=cost(8 * near.size * width, 12 * half * width),
        name="attended_halves",
    )(place, near, far, w_out, w_far)


def head_back_kernel(head, slopes_ref, se_ref, qkv_ref, kv_ref, dctx_ref, out_ref, acc_ref):
    here = dctx_ref.shape[1]
    mine = slice(head * HD, (head + 1) * HD)
    keys = slice(head * 2 * HD, (head + 1) * 2 * HD)
    acc_ref[...] = jnp.zeros_like(acc_ref)
    edge = jnp.zeros((HD, QB), BF)
    out_ref[0, :, 0:QB] = edge
    out_ref[0, :, QB + here :] = edge
    slope = slopes_ref[head]
    starts = range(0, here, QB)
    pairs = []
    for off in starts:
        query = qkv_ref[0, mine, off + QB : off + 2 * QB] * BF(0.125)
        d_rows = dctx_ref[mine, off : off + QB]
        pairs.append(
            jnp.concatenate(
                [
                    jnp.concatenate([query, edge], axis=1),
                    jnp.concatenate([edge, d_rows], axis=1),
                ],
                axis=0,
            )
        )
    both = [dot(kv_ref[off : off + WINDOW, keys], pair, 1, 0) for off, pair in zip(starts, pairs)]
    probs = [
        softmax(x[:, :QB] - slope * block_distance(se_ref, off)) for off, x in zip(starts, both)
    ]
    row_dots = [jnp.sum(x[:, QB:] * p, axis=0, keepdims=True) for x, p in zip(both, probs)]
    d_scores = [
        (p * (x[:, QB:] - row_dot)).astype(BF) for x, p, row_dot in zip(both, probs, row_dots)
    ]
    probs = [p.astype(BF) for p in probs]
    for off, d in zip(starts, d_scores):
        d_query = dot(qkv_ref[1, mine, off : off + WINDOW], d, 1, 0) * 0.125
        out_ref[0, :, off + QB : off + 2 * QB] = d_query.astype(BF)
    sums = [
        dot(pair, jnp.concatenate([d, p], axis=1), 1, 1)
        for pair, d, p in zip(pairs, d_scores, probs)
    ]
    for off, x in zip(starts, sums):
        acc_ref[:, off : off + WINDOW] += x
    out_ref[1, :, :] = acc_ref[0:HD, :].astype(BF)
    out_ref[2, :, :] = acc_ref[HD:, :].astype(BF)


def head_back(head, slopes, se, qkv, kv, dctx):
    here, count = se.shape[1], qkv.shape[2]
    elements = here * WINDOW
    return pl.pallas_call(
        functools.partial(head_back_kernel, head),
        out_shape=out((3, HD, count)),
        in_specs=[smem()] + vmem(4),
        out_specs=vmem(1)[0],
        scratch_shapes=[pltpu.VMEM((2 * HD, count), F32)],
        compiler_params=params(12),
        cost_estimate=cost(elements * HD * 24, count * HD * 18, elements),
        name="attention_backward_head",
    )(slopes, se, qkv, kv, dctx)


def stack_heads(refs, all_ref):
    heads = len(refs)
    for h, ref in enumerate(refs):
        for part in range(3):
            at = (part * heads + h) * HD
            all_ref[at : at + HD, :] = ref[part]


def qkv_grad_kernel(heads, *refs):
    (rows_ref, *out_refs, all_ref) = refs[heads:]
    stack_heads(refs[:heads], all_ref)
    for c in range(0, rows_ref.shape[1], 256):
        total = dot(all_ref[...], rows_ref[:, c : c + 256], 1, 0).astype(BF)
        at = 0
        for ref in out_refs:
            ref[:, c : c + 256] = total[at : at + ref.shape[0]]
            at += ref.shape[0]


def qkv_grad(heads, rows, parts=(3,)):
    count, width = rows.shape
    size = len(heads) * HD
    return pl.pallas_call(
        functools.partial(qkv_grad_kernel, len(heads)),
        out_shape=[out((part * size, width)) for part in parts],
        in_specs=vmem(len(heads) + 1),
        out_specs=vmem(len(parts)),
        scratch_shapes=[pltpu.VMEM((3 * size, count), BF)],
        compiler_params=params(12),
        cost_estimate=cost(6 * size * count * width, count * width * 4),
        name="projection_gradient",
    )(*heads, rows)


def gather_back_kernel(
    place_ref, ctx_ref, own_ref, sib_ref, norms_ref, norms_sib_ref, w_out_ref, w_far_ref,
    datt_ref, grad_ref, dctx_ref, dctx_far_ref,
):
    even = place_ref[4] == 0
    half = datt_ref.shape[0] // 2
    own, sib = own_ref[...], sib_ref[...]
    datt_ref[0:half, :] = jnp.where(even, own, sib)
    datt_ref[half:, :] = jnp.where(even, sib, own)
    for c in range(0, 2 * half, 256):
        rows = datt_ref[c : c + 256, :]
        dctx_far_ref[:, c : c + 256] = dot(w_far_ref[...], rows, 1, 1).astype(BF)
        dctx_ref[:, c : c + 256] = dot(w_out_ref[...], rows, 1, 1).astype(BF)
    count = ctx_ref.shape[0]
    grad_ref[0:count, :] = dot(ctx_ref[...], datt_ref[...], 1, 0).astype(BF)
    norms = norms_ref[...].astype(F32) + norms_sib_ref[...].astype(F32)
    grad_ref[count:, :] = norms.astype(BF)


def gather_back(place, ctx, own, sib, norms, norms_sib, w_out, w_far):
    half, width = own.shape
    vm = pl.BlockSpec(memory_space=pltpu.VMEM)
    return pl.pallas_call(
        gather_back_kernel,
        out_shape=[
            out((2 * half, width)),
            jax.ShapeDtypeStruct((ctx.shape[0] + NORM_ROWS, width), BF),
            jax.ShapeDtypeStruct(ctx.shape, BF),
            jax.ShapeDtypeStruct(ctx.shape, BF),
        ],
        in_specs=[smem()] + [vm] * 7,
        out_specs=[vm] * 4,
        compiler_params=params(16),
        cost_estimate=cost(6 * ctx.size * width, 12 * half * width),
        name="gather_d_attended",
    )(place, ctx, own, sib, norms, norms_sib, w_out, w_far)


def phi_pair(gate):
    bell = jnp.exp(gate * gate * -0.5)
    t = 1.0 / (1.0 + (0.3275911 / math.sqrt(2.0)) * jnp.abs(gate))
    poly = t * (
        0.254829592
        + t * (-0.284496736 + t * (1.421413741 + t * (-1.453152027 + t * 1.061405429)))
    )
    tail = 0.5 * poly * bell
    return jnp.where(gate >= 0.0, 1.0 - tail, tail), bell * (1.0 / math.sqrt(2.0 * math.pi))


def ff_fwd_kernel(
    x0_ref, x1_ref, wg_ref, wu_ref, wd_ref, x_ref, act_ref, a_ref, b_ref, keep_ref, send_ref
):
    half = x0_ref.shape[0]
    for i, (source, target) in enumerate(((x0_ref, keep_ref), (x1_ref, send_ref))):
        rows = slice(i * half, (i + 1) * half)
        x = source[...]
        x_ref[rows, :] = x
        for f in range(0, wd_ref.shape[0], 256):
            cols = slice(f, f + 256)
            gate = dot(x, wg_ref[:, cols], 1, 0)
            up = dot(x, wu_ref[:, cols], 1, 0)
            big, small = phi_pair(gate)
            gelu = gate * big
            act_ref[rows, cols] = (gelu * up).astype(BF)
            a_ref[rows, cols] = gelu.astype(BF)
            b_ref[rows, cols] = (up * (big + gate * small)).astype(BF)
        target[...] = dot(act_ref[rows, :], wd_ref[...], 1, 0).astype(BF)


def ff_fwd(pieces, wg, wu, wd):
    half, width = pieces[0].shape
    hidden = wd.shape[0]
    rows = 2 * half
    return pl.pallas_call(
        ff_fwd_kernel,
        out_shape=[out((rows, width))] + [out((rows, hidden))] * 3 + [out((half, width))] * 2,
        in_specs=vmem(5),
        out_specs=vmem(6),
        compiler_params=params(16),
        cost_estimate=cost(rows * width * hidden * 6, 12 * rows * width, 2 * rows * hidden),
        name="ff_forward",
    )(*pieces, wg, wu, wd)


def ff_bwd_kernel(
    d0_ref, d1_ref, a_ref, b_ref, wd_ref, wg_ref, wu_ref,
    db_ref, dg_ref, du_ref, keep_ref, send_ref,
):
    half = d0_ref.shape[0]
    for i, (source, target) in enumerate(((d0_ref, keep_ref), (d1_ref, send_ref))):
        rows = slice(i * half, (i + 1) * half)
        db = source[...]
        db_ref[rows, :] = db
        for f in range(0, wd_ref.shape[0], 256):
            cols = slice(f, f + 256)
            d_active = dot(db, wd_ref[cols, :], 1, 1)
            dg_ref[rows, cols] = (d_active * b_ref[rows, cols].astype(F32)).astype(BF)
            du_ref[rows, cols] = (d_active * a_ref[rows, cols].astype(F32)).astype(BF)
        part = dot(dg_ref[rows, :], wg_ref[...], 1, 1) + dot(du_ref[rows, :], wu_ref[...], 1, 1)
        target[...] = part.astype(BF)


def ff_bwd(pieces, a, b, wd, wg, wu):
    half, width = pieces[0].shape
    hidden = wd.shape[0]
    rows = 2 * half
    return pl.pallas_call(
        ff_bwd_kernel,
        out_shape=[out((rows, width))] + [out((rows, hidden))] * 2 + [out((half, width))] * 2,
        in_specs=vmem(7),
        out_specs=vmem(5),
        compiler_params=params(16),
        cost_estimate=cost(rows * width * hidden * 6, 12 * rows * width),
        name="ff_backward",
    )(*pieces, a, b, wd, wg, wu)


def weight_near_kernel(a_ref, d_ref, out_ref):
    out_ref[...] = dot(a_ref[...], d_ref[...], 0, 0)


def weight_near(a, d):
    size = (a.shape[1], d.shape[1])
    return pl.pallas_call(
        weight_near_kernel,
        out_shape=out(size, F32),
        in_specs=vmem(2),
        out_specs=vmem(1)[0],
        compiler_params=params(16),
        cost_estimate=cost(2 * a.size * d.shape[1], a.size * 8),
        name="weight_gradient_near",
    )(a, d)


def weight_far_kernel(dim, place_ref, acc_ref, *refs):
    pairs, (out_ref, sent_ref) = refs[:-2], refs[-2:]
    a = jnp.concatenate([ref[...] for ref in pairs[0::2]], axis=0)
    d = jnp.concatenate([ref[...] for ref in pairs[1::2]], axis=0)
    out_ref[...] = (acc_ref[...] + dot(a, d, 0, 0)).astype(BF)
    half = sent_ref.shape[0]
    at = (1 - place_ref[dim]) * half
    sent_ref[...] = out_ref[pl.ds(pl.multiple_of(at, half), half), :]


def weight_far(place, dim, acc, *pairs):
    rows, width = acc.shape
    return pl.pallas_call(
        functools.partial(weight_far_kernel, dim),
        out_shape=[out((rows, width)), out((rows // 2, width))],
        in_specs=[smem()] + vmem(1 + len(pairs)),
        out_specs=vmem(2),
        compiler_params=params(16),
        cost_estimate=cost(2 * acc.size * rows, acc.size * 12),
        name="weight_gradient_far",
    )(place, acc, *pairs)


def centre(pre):
    mean = jnp.mean(pre, axis=-1, keepdims=True)
    centred = pre - mean
    r = lax.rsqrt(jnp.mean(centred * centred, axis=-1, keepdims=True) + EPSILON)
    return centred * r, r


def norm_back(xhat, r, gain, grad):
    e = grad * gain
    return r * (
        e
        - jnp.mean(e, axis=-1, keepdims=True)
        - xhat * jnp.mean(e * xhat, axis=-1, keepdims=True)
    )


def store_pieces(value, refs):
    refs[0][...] = value
    at = 0
    for ref in refs[1:]:
        ref[...] = value[at : at + ref.shape[0]]
        at += ref.shape[0]


def far_rows(refs):
    return jnp.concatenate([ref[...].astype(F32) for ref in refs], axis=0)


def ln1_kernel(
    x_ref, own_ref, recv_ref, gain_ref, bias_ref, pre_ref, normed_ref, *low_refs
):
    pre = x_ref[...].astype(F32) + (own_ref[...] + recv_ref[...].astype(F32))
    pre_ref[...] = pre
    xhat, _ = centre(pre)
    normed = xhat * gain_ref[...] + bias_ref[...]
    normed_ref[...] = normed
    store_pieces(normed.astype(BF), low_refs)


def ln1(x, own, recv, gain, bias):
    shape = x.shape
    vm = pl.BlockSpec(memory_space=pltpu.VMEM)
    return pl.pallas_call(
        ln1_kernel,
        out_shape=[
            out(shape, F32),
            out(shape, F32),
            out(shape),
            *[out((shape[0] // PIECES, shape[1]))] * PIECES,
        ],
        in_specs=[vm] * 5,
        out_specs=[vm] * (3 + PIECES),
        compiler_params=params(12),
        cost_estimate=cost(x.size * 10, x.size * 18),
        name="norm_one",
    )(x, own, recv, gain, bias)


def ln2_kernel(
    normed_ref, keep_ref, near_ref, dy_ref, gain_ref, bias_ref, *refs
):
    out_ref, d_ref, grads_ref, *low_refs = refs[PIECES:]
    branch = keep_ref[...].astype(F32) + near_ref[...].astype(F32) + far_rows(refs[:PIECES])
    xhat, r = centre(normed_ref[...] + branch)
    gain = gain_ref[...]
    out_ref[...] = (xhat * gain + bias_ref[...]).astype(BF)
    dy = dy_ref[...].astype(F32)
    d = norm_back(xhat, r, gain, dy)
    d_ref[...] = d
    store_pieces(d.astype(BF), low_refs)
    grads_ref[0:1, :] = jnp.sum(dy * xhat, axis=0, keepdims=True)
    grads_ref[1:2, :] = jnp.sum(dy, axis=0, keepdims=True)


def ln2(normed, keep, near, far, dy, gain, bias):
    shape = normed.shape
    return pl.pallas_call(
        ln2_kernel,
        out_shape=[
            out(shape),
            out(shape, F32),
            out((2, shape[1]), F32),
            out(shape),
            *[out((shape[0] // PIECES, shape[1]))] * PIECES,
        ],
        in_specs=vmem(6 + PIECES),
        out_specs=vmem(4 + PIECES),
        compiler_params=params(16),
        cost_estimate=cost(normed.size * 20, normed.size * 20),
        name="norm_two",
    )(normed, keep, near, dy, gain, bias, *far)


def ln1_back_kernel(
    pre_ref, d2_ref, keep_ref, near_ref, gain_ref, grads_two_ref, *refs
):
    d_ref, low_ref, norms_ref = refs[PIECES:]
    grad = d2_ref[...] + (
        keep_ref[...].astype(F32) + near_ref[...].astype(F32) + far_rows(refs[:PIECES])
    )
    xhat, r = centre(pre_ref[...])
    d = norm_back(xhat, r, gain_ref[...], grad)
    d_ref[...] = d
    width = d.shape[1]
    low_ref[...] = d.astype(BF)
    norms_ref[...] = jnp.concatenate(
        [
            jnp.sum(grad * xhat, axis=0, keepdims=True),
            jnp.sum(grad, axis=0, keepdims=True),
            grads_two_ref[...],
            jnp.zeros((NORM_ROWS - 4, width), F32),
        ],
        axis=0,
    ).astype(BF)


def ln1_back(pre, d2, keep, near, far, gain, grads_two):
    shape = pre.shape
    return pl.pallas_call(
        ln1_back_kernel,
        out_shape=[out(shape, F32), out(shape), out((NORM_ROWS, shape[1]))],
        in_specs=vmem(6 + PIECES),
        out_specs=vmem(3),
        compiler_params=params(16),
        cost_estimate=cost(pre.size * 20, pre.size * 20),
        name="norm_one_backward",
    )(pre, d2, keep, near, gain, grads_two, *far)


def swap(value, axis, bit):
    count = lax.axis_size(axis)
    return lax.ppermute(value, axis, [(i, i ^ bit) for i in range(count)])


def swap_chip_edges(value):
    count = lax.axis_size("seq") * lax.axis_size("tp")
    pairs = []
    for i in range(1, count - 1, 2):
        pairs += [(i, i + 1), (i + 1, i)]
    return lax.ppermute(value, ("seq", "tp"), pairs)


def fold_kernel(dims, place_ref, own_ref, recv_ref, keep_ref, send_ref):
    rows, half = recv_ref.shape[0], keep_ref.shape[0]
    base = place_ref[dims[0]] * rows
    cut = place_ref[dims[1]] * half
    for ref, at in ((keep_ref, cut), (send_ref, half - cut)):
        own = own_ref[pl.ds(pl.multiple_of(base + at, NORM_ROWS), half), :].astype(F32)
        recv = recv_ref[pl.ds(pl.multiple_of(at, NORM_ROWS), half), :].astype(F32)
        ref[...] = (own + recv).astype(BF)


def fold(place, dims, own, recv):
    rows, width = recv.shape
    vm = pl.BlockSpec(memory_space=pltpu.VMEM)
    return pl.pallas_call(
        functools.partial(fold_kernel, dims),
        out_shape=[jax.ShapeDtypeStruct((rows // 2, width), BF)] * 2,
        in_specs=[smem(), vm, vm],
        out_specs=[vm] * 2,
        compiler_params=params(10),
        cost_estimate=cost(recv.size, recv.size * 6),
        name="fold_half",
    )(place, own, recv)


def join_kernel(dim, place_ref, own_ref, recv_ref, out_ref):
    first = place_ref[dim] == 0
    half = own_ref.shape[0]
    own, recv = own_ref[...], recv_ref[...]
    out_ref[0:half, :] = jnp.where(first, own, recv).astype(out_ref.dtype)
    out_ref[half:, :] = jnp.where(first, recv, own).astype(out_ref.dtype)


def join(place, dim, own, recv, kind=BF):
    half, width = own.shape
    vm = pl.BlockSpec(memory_space=pltpu.VMEM)
    return pl.pallas_call(
        functools.partial(join_kernel, dim),
        out_shape=jax.ShapeDtypeStruct((2 * half, width), kind),
        in_specs=[smem(), vm, vm],
        out_specs=vm,
        compiler_params=params(10),
        cost_estimate=cost(0, own.size * 12),
        name="join_halves",
    )(place, own, recv)


def finish_in_kernel(dims, place_ref, g_ref, g_recv_ref, u_ref, u_recv_ref, out_ref):
    half = g_ref.shape[0]
    for i, (own_ref, recv_ref) in enumerate(((g_ref, g_recv_ref), (u_ref, u_recv_ref))):
        first = place_ref[dims[i]] == 0
        own, recv = own_ref[...], recv_ref[...]
        out_ref[0:half, i, :] = jnp.where(first, own, recv).astype(F32)
        out_ref[half:, i, :] = jnp.where(first, recv, own).astype(F32)


def finish_in(place, gate, up):
    half, width = gate[1].shape
    return pl.pallas_call(
        functools.partial(finish_in_kernel, (gate[0], up[0])),
        out_shape=out((2 * half, 2, width), F32),
        in_specs=[smem()] + vmem(4),
        out_specs=vmem(1)[0],
        compiler_params=params(16),
        cost_estimate=cost(0, gate[1].size * 24),
        name="finish_w_in_gradient",
    )(place, *gate[1:], *up[1:])


def finish_a_kernel(dim, place_ref, own_ref, recv_ref, _, out_ref):
    join_kernel(dim, place_ref, own_ref, recv_ref, out_ref)


def finish_a(place, dim, own, recv, later):
    half, width = own.shape
    return pl.pallas_call(
        functools.partial(finish_a_kernel, dim),
        grid=(1,),
        out_shape=jax.ShapeDtypeStruct(later.shape, F32),
        in_specs=[smem()]
        + [full((half, width))] * 2
        + [pl.BlockSpec(memory_space=pl.ANY)],
        out_specs=pl.BlockSpec((2 * half, width), lambda i: (0, 0)),
        input_output_aliases={3: 0},
        compiler_params=params(10),
        cost_estimate=cost(0, own.size * 12),
        name="finish_attention_gradient_a",
    )(place, own, recv, later)


def finish_b_kernel(dim, place_ref, own_ref, recv_ref, qkv_ref, out_ref, norm_ref):
    first = place_ref[dim] == 0
    own, recv = own_ref[...], recv_ref[...]
    step = own.shape[0] // 2
    count = step - NORM_ROWS
    low = jnp.where(first, own, recv).astype(F32)
    high = jnp.where(first, recv, own).astype(F32)
    for ref, rows in ((qkv_ref, low), (out_ref, high)):
        ref[0:count, :] = rows[0:count]
        ref[count:, :] = rows[step : step + count]
    norm_ref[...] = low[count : count + 4]


def finish_b(place, dim, own, recv, rows):
    half, width = own.shape
    rest = half - 2 * NORM_ROWS
    return pl.pallas_call(
        functools.partial(finish_b_kernel, dim),
        grid=(1,),
        out_shape=[
            jax.ShapeDtypeStruct((rows, width), F32),
            jax.ShapeDtypeStruct((rest, width), F32),
            jax.ShapeDtypeStruct((4, width), F32),
        ],
        in_specs=[smem()] + [full((half, width))] * 2,
        out_specs=[
            pl.BlockSpec((rest, width), lambda i: (rows // rest - 1, 0)),
            full((rest, width)),
            full((4, width)),
        ],
        compiler_params=params(10),
        cost_estimate=cost(0, own.size * 12),
        name="finish_attention_gradient_b",
    )(place, own, recv)


def send_half(place_ref, dim, ref, sent_ref):
    count = sent_ref.shape[0]
    at = (1 - place_ref[dim]) * count
    sent_ref[...] = ref[pl.ds(pl.multiple_of(at, NORM_ROWS), count), :]


def cut_a_kernel(dim, place_ref, own_ref, far_ref, a_ref, sent_ref):
    half = a_ref.shape[0]
    total = own_ref[0:half, :].astype(F32) + far_ref[...].astype(F32)
    a_ref[...] = total.astype(BF)
    send_half(place_ref, dim, a_ref, sent_ref)


def cut_a(place, dim, own, far):
    rows, width = far.shape
    return pl.pallas_call(
        functools.partial(cut_a_kernel, dim),
        out_shape=[out((rows, width)), out((rows // 2, width))],
        in_specs=[smem()] + vmem(2),
        out_specs=vmem(2),
        compiler_params=params(12),
        cost_estimate=cost(far.size, far.size * 8),
        name="add_far_shard_a",
    )(place, own, far)


def cut_b_kernel(dim, place_ref, own_ref, far_ref, out_ref, b_ref, sent_ref):
    rows = far_ref.shape[0]
    start = own_ref.shape[0] - rows
    value = (own_ref[start:, :].astype(F32) + far_ref[...].astype(F32)).astype(BF)
    step = b_ref.shape[0] // 4
    count = step - NORM_ROWS
    for i in range(4):
        at = (i % 2) * count
        source = value if i < 2 else out_ref
        b_ref[i * step : i * step + count, :] = source[at : at + count, :]
        b_ref[i * step + count : (i + 1) * step, :] = out_ref[2 * count :, :]
    send_half(place_ref, dim, b_ref, sent_ref)


def cut_b(place, dim, own, far, out_rows):
    width = own.shape[1]
    rows = far.shape[0] + out_rows.shape[0] + 3 * NORM_ROWS
    return pl.pallas_call(
        functools.partial(cut_b_kernel, dim),
        out_shape=[out((rows, width)), out((rows // 2, width))],
        in_specs=[smem()] + vmem(3),
        out_specs=vmem(2),
        compiler_params=params(12),
        cost_estimate=cost(far.size, far.size * 8),
        name="add_far_shard_b",
    )(place, own, far, out_rows)


def out_grad_kernel(ctx_ref, datt_ref, own_ref, far_ref, out_ref):
    count = ctx_ref.shape[0]
    near = dot(ctx_ref[...], datt_ref[...], 1, 0)
    out_ref[0:count, :] = (near + far_ref[0:count, :].astype(F32)).astype(BF)
    norms = own_ref[count:, :].astype(F32) + far_ref[count:, :].astype(F32)
    out_ref[count:, :] = norms.astype(BF)


def out_grad(ctx, datt, own, far):
    vm = pl.BlockSpec(memory_space=pltpu.VMEM)
    return pl.pallas_call(
        out_grad_kernel,
        out_shape=jax.ShapeDtypeStruct(far.shape, BF),
        in_specs=[vm] * 4,
        out_specs=vm,
        compiler_params=params(12),
        cost_estimate=cost(2 * ctx.size * datt.shape[1], datt.size * 2),
        name="out_gradient",
    )(ctx, datt, own, far)


class SeqSum:
    def __init__(self, place, order, dims, g, sent=None, last=None):
        self.place, self.order, self.dims, self.value = place, order, dims, g
        self.last = last
        self.stage = 1
        self.pairwise = lax.axis_size("seq") == 8
        if not self.pairwise:
            whole = lax.psum(g, "seq")
            half = g.shape[0] // 2
            self.dims = (len(dims),)
            self.value, self.moving = whole[:half], whole[half:]
            return
        if sent is None:
            half = g.shape[0] // 2
            sent = lax.dynamic_slice_in_dim(g, (1 - place[dims[0]]) * half, half, 0)
        self.send(0, sent)

    def send(self, dim, value):
        self.moving = swap(value, "seq", 1 << self.dims[dim])

    def step(self):
        stage, place, order, dims = self.stage, self.place, self.order, self.dims
        self.stage += 1
        if not self.pairwise and stage < 5:
            return
        value, moved = self.value, self.moving
        if stage < 5 or self.last is not None:
            value = order(value)
        if stage == 1:
            self.value, sent = fold(place, dims[:2], value, moved)
            order.note(sent)
            self.send(1, sent)
        elif stage in (2, 3):
            self.value = order.note(add(value, moved))
            self.send(2 if stage == 2 else 1, self.value)
        elif stage == 4:
            self.value = order.note(join(place, dims[1], value, moved))
            self.send(0, self.value)
        elif stage == 5:
            if self.last is None:
                self.result = (dims[0], self.value, moved)
                return
            self.result = self.last(place, dims[0], value, moved)
            order.note(jax.tree.leaves(self.result)[-1])


def add_kernel(a_ref, b_ref, out_ref):
    out_ref[...] = (a_ref[...].astype(F32) + b_ref[...].astype(F32)).astype(BF)


def add(a, b):
    return pl.pallas_call(
        add_kernel,
        out_shape=out(a.shape),
        in_specs=vmem(2),
        out_specs=vmem(1)[0],
        compiler_params=params(10),
        cost_estimate=cost(a.size, a.size * 6),
        name="add_pair",
    )(a, b)


def input_grad_kernel(place_ref, *refs):
    (*heads, wt_ref, wt_far_ref, own_ref, sent_ref, near_ref, far_ref) = refs
    stack_heads(heads[: len(heads) // 2], near_ref)
    stack_heads(heads[len(heads) // 2 :], far_ref)
    half = own_ref.shape[0]
    for ref, which in ((sent_ref, 1 - place_ref[4]), (own_ref, place_ref[4])):
        here = pl.ds(pl.multiple_of(which * half, 128), half)
        total = dot(near_ref[:, here], wt_ref[...], 0, 0)
        ref[...] = (total + dot(far_ref[:, here], wt_far_ref[...], 0, 0)).astype(ref.dtype)


def input_grad(place, near, far, wt, wt_far):
    count = near[0].shape[2]
    half, (size, width) = count // 2, wt.shape
    vm = pl.BlockSpec(memory_space=pltpu.VMEM)
    return pl.pallas_call(
        input_grad_kernel,
        out_shape=[
            jax.ShapeDtypeStruct((half, width), F32),
            jax.ShapeDtypeStruct((half, width), BF),
        ],
        in_specs=[smem()] + [vm] * (2 * len(near) + 2),
        out_specs=[vm] * 2,
        scratch_shapes=[pltpu.VMEM((size, count), BF)] * 2,
        compiler_params=params(16),
        cost_estimate=cost(4 * size * count * width, 12 * half * width),
        name="input_gradient",
    )(place, *near, *far, wt, wt_far)


def input_rows_kernel(place_ref, own_ref, recv_ref, pre_ref, out_ref, edge_ref):
    count, edge = out_ref.shape[0], edge_ref.shape[0]
    core = place_ref[4]
    at = pl.ds(pl.multiple_of(core * count, edge), edge)
    edge_ref[...] = (own_ref[at, :] + recv_ref[at, :].astype(F32)).astype(BF)
    at = pl.ds(pl.multiple_of((1 - core) * edge, edge), count)
    out_ref[...] = pre_ref[...] + (own_ref[at, :] + recv_ref[at, :].astype(F32))


def input_rows(place, own, recv, pre):
    vm = pl.BlockSpec(memory_space=pltpu.VMEM)
    return pl.pallas_call(
        input_rows_kernel,
        out_shape=[
            jax.ShapeDtypeStruct(pre.shape, F32),
            jax.ShapeDtypeStruct((QB, pre.shape[1]), BF),
        ],
        in_specs=[smem()] + [vm] * 3,
        out_specs=[vm] * 2,
        compiler_params=params(16),
        cost_estimate=cost(pre.size * 2, pre.size * 16),
        name="input_gradient_rows",
    )(place, own, recv, pre)


def input_edge_kernel(place_ref, rows_ref, edge_ref, out_ref):
    out_ref[...] = rows_ref[...]
    edge = edge_ref.shape[0]
    start = place_ref[4] * (rows_ref.shape[0] - edge)
    at = pl.ds(pl.multiple_of(start, edge), edge)
    out_ref[at, :] = rows_ref[at, :] + edge_ref[...].astype(F32)


def input_edge(place, rows, edge):
    vm = pl.BlockSpec(memory_space=pltpu.VMEM)
    return pl.pallas_call(
        input_edge_kernel,
        out_shape=jax.ShapeDtypeStruct(rows.shape, F32),
        in_specs=[smem()] + [vm] * 2,
        out_specs=vm,
        compiler_params=params(12),
        cost_estimate=cost(rows.size, rows.size * 10),
        name="input_gradient_edge",
    )(place, rows, edge)


def per_device(
    inputs, lengths, w_qkv, w_out, w_in, w_down, ln1_gain, ln1_bias, ln2_gain, ln2_bias, cotangent
):
    own_rows, width = inputs.shape
    tp_count = lax.axis_size("tp")
    head_width = w_qkv.shape[2]
    heads = head_width // HD
    chip_rows = 2 * own_rows
    tp = lax.axis_index("tp")
    seq = lax.axis_index("seq")
    core = tp & 1
    even = core == 0
    first = (seq * tp_count + 2 * (tp >> 1)) * own_rows
    place = jnp.stack([seq & 1, (seq >> 1) & 1, (seq >> 2) & 1, 0 * core, core]).astype(jnp.int32)

    bounds = jnp.cumsum(lengths)[:, None]
    tokens = (first + jnp.arange(chip_rows, dtype=jnp.int32))[None, :]
    before = bounds <= tokens
    start = jnp.max(jnp.where(before, bounds, 0), axis=0)
    end = jnp.min(jnp.where(before, jnp.iinfo(jnp.int32).max, bounds), axis=0)
    se = jnp.stack([start, end]) - (first - QB)
    se = jnp.pad(se, ((0, 6), (0, 0)))
    table = jnp.asarray(slope_table(HEADS))
    slopes = lax.dynamic_slice_in_dim(table, tp * heads, heads)
    slopes_far = lax.dynamic_slice_in_dim(table, (tp ^ 2) * heads, heads)

    wt = w_qkv.transpose(0, 2, 1).reshape(3 * head_width, width)
    wt_far = swap(wt, "tp", 2)

    sibling = swap(inputs, "tp", 1)
    edge = swap_chip_edges(
        lax.dynamic_slice_in_dim(inputs, core * (own_rows - QB), QB, axis=0)
    )
    edge_sibling = swap(edge, "tp", 1)
    rows, ctx, qkv, kv = attn_near(
        heads, place, slopes, se, inputs, sibling, edge, edge_sibling,
        wt.reshape(3, head_width, width),
    )
    w_out_far = swap(after(w_out, ctx), "tp", 2)
    ctx_far, qkv_far, kv_far = attn_far(
        heads, slopes_far, se, rows, wt_far.reshape(3, head_width, width)
    )
    attended, attended_sent = attended_halves(place, ctx, ctx_far, w_out, w_out_far)
    attended_sent = swap(attended_sent, "tp", 1)
    gain1, bias1 = ln1_gain[None], ln1_bias[None]
    gain2, bias2 = ln2_gain[None], ln2_bias[None]
    pre_one, normed, low, *low_pieces = ln1(inputs, attended, attended_sent, gain1, bias1)

    order = Order()
    w_in_late = after(w_in, low)
    wg, wu = w_in_late[:, 0], w_in_late[:, 1]

    def both_ways(own, pieces, work, between=lambda near_out: None):
        far = [swap(piece, "tp", 2) for piece in pieces]
        near_out = work(0, own, order(swap(own, "tp", 1)))
        near_keep, near_send = near_out[-2:]
        order.note(near_send)
        recv = swap(near_send, "tp", 1)
        between(near_out)
        far = [order(rows) for rows in far]
        far_sibling = [swap(rows, "tp", 1) for rows in far]
        outs, sums = [near_out], []
        for rows, rows_sibling in zip(far, far_sibling):
            outs.append(work(len(outs), order(rows), rows_sibling))
            order.note(outs[-1][-1])
        from_sibling = [swap(o[-1], "tp", 1) for o in outs[1:]]
        for i, (o, theirs) in enumerate(zip(outs[1:], from_sibling)):
            total = order.note(add(order(o[-2]), theirs))
            sums.append(swap(total, "tp", 2))
        return outs, (near_keep, recv, sums)

    order.note(low)
    forward, parts = both_ways(
        low, low_pieces, lambda i, a, b: ff_fwd((a, b), wg, wu, w_down)
    )
    layer_out, d_pre_two, grads_two, d_branch, *d_branch_pieces = ln2(
        normed, order(parts[0]), *parts[1:], cotangent, gain2, bias2
    )
    order.note(d_branch)

    weight_near_parts = []

    def grads_between(near_out):
        for x, d in weight_pairs:
            part = weight_near(order(forward[0][x]), near_out[d])
            weight_near_parts.append(order.note(part))

    weight_pairs = ((1, 0), (0, 2), (0, 1))
    backward, parts = both_ways(
        d_branch,
        d_branch_pieces,
        lambda i, a, b: ff_bwd((a, b), forward[i][2], forward[i][3], w_down, wg, wu),
        grads_between,
    )

    def join_whole(*halves):
        return join(*halves, F32)

    def weight_sum(which, dims):
        x, d = weight_pairs[which]
        pairs = [t for f, b in zip(forward[1:], backward[1:]) for t in (f[x], b[d])]
        total, sent = weight_far(
            place, dims[0], order(weight_near_parts[which]), *pairs
        )
        order.note(sent)
        return SeqSum(place, order, dims, total, sent, None if which else join_whole)

    d_far, d_near = [], []

    def one_head(h, far):
        kept = (slopes_far, se, qkv_far, kv_far) if far else (slopes, se, qkv, kv)
        return order.note(head_back(h, *kept, order(d_ctx_far if far else d_ctx)))

    down = weight_sum(0, (0, 1, 2))
    up = weight_sum(1, (0, 1, 2))
    gate = weight_sum(2, (1, 0, 2))
    d_pre_one, half, norms = ln1_back(
        pre_one, d_pre_two, order(parts[0]), *parts[1:], gain1, grads_two
    )
    order.note(half)
    half_sibling = swap(half, "tp", 1)
    norms_sibling = swap(norms, "tp", 1)
    down.step()
    gate.step()
    d_attended, sent_out, d_ctx, d_ctx_far = gather_back(
        place, order(ctx_far), half, half_sibling, norms, norms_sibling, w_out, w_out_far
    )
    order.note(d_ctx_far)
    far_out = swap(sent_out, "tp", 2)
    d_far.append(one_head(0, True))
    down.step()
    d_far.append(one_head(1, True))
    grad_out = order.note(out_grad(ctx, order(d_attended), sent_out, far_out))
    up.step()
    d_far.append(one_head(2, True))
    far_qk, far_v = qkv_grad(d_far, order(rows), (2, 1))
    order.note(far_v)
    far_v = swap(far_v, "tp", 2)
    far_qk = swap(far_qk, "tp", 2)
    gate.step()
    d_near.append(one_head(0, False))
    down.step()
    d_near.append(one_head(1, False))
    up.step()
    d_near.append(one_head(2, False))
    (own_qkv,) = qkv_grad(d_near, order(rows))
    order.note(own_qkv)
    total, sent = cut_b(place, 0, order(own_qkv), far_v, grad_out)
    order.note(sent)
    attn_b = SeqSum(
        place, order, (0, 1, 2), total, sent, lambda *h: finish_b(*h, own_qkv.shape[0])
    )
    gate.step()
    window_own, window_sent = input_grad(
        place, [order(d_near[0]), *d_near[1:]], d_far, wt, wt_far
    )
    order.note(window_sent)
    window_sent = swap(window_sent, "tp", 1)
    down.step()
    total, sent = cut_a(place, 1, order(own_qkv), far_qk)
    order.note(sent)
    attn_a = SeqSum(place, order, (1, 0, 2), total, sent, lambda *h: finish_a(*h, attn_b.result[0]))
    attn_b.step()
    up.step()
    attn_b.step()
    attn_a.step()
    gate.step()
    down.step()
    attn_a.step()
    up.step()
    attn_b.step()
    attn_a.step()
    attn_b.step()
    attn_a.step()
    grad_rows, d_edge = input_rows(place, order(window_own), window_sent, d_pre_one)
    order.note(d_edge)
    d_edge = swap_chip_edges(d_edge)
    gate.step()
    up.step()
    grad_in = order.note(
        finish_in(order(place), gate.result, up.result)
    )
    attn_b.step()
    grad_input = order.note(input_edge(place, order(grad_rows), d_edge))
    attn_a.step()
    assert all(unit.stage == 6 for unit in (down, gate, up, attn_a, attn_b))
    grad_down = down.result
    _, grad_out, norm_grads = attn_b.result
    grad_qkv = attn_a.result
    grad_qkv = grad_qkv.reshape(3, head_width, width).transpose(0, 2, 1)
    return (
        layer_out,
        grad_input,
        grad_qkv,
        grad_out,
        grad_in,
        grad_down,
        norm_grads[0],
        norm_grads[1],
        norm_grads[2],
        norm_grads[3],
    )


def solution(mesh):
    in_specs = (
        P(("seq", "tp"), None),
        P(),
        P(None, None, "tp"),
        P("tp", None),
        P(None, None, "tp"),
        P("tp", None),
        P(),
        P(),
        P(),
        P(),
        P(("seq", "tp"), None),
    )
    out_specs = (
        P(("seq", "tp"), None),
        P(("seq", "tp"), None),
        P(None, None, "tp"),
        P("tp", None),
        P(None, None, "tp"),
        P("tp", None),
        P(),
        P(),
        P(),
        P(),
    )
    return jax.shard_map(
        per_device, mesh=mesh, in_specs=in_specs, out_specs=out_specs, check_vma=False
    )
```

```python
import functools
import math

import jax
import jax.numpy as jnp
import numpy as np
from jax import lax
from jax.experimental import pallas as pl
from jax.experimental.pallas import tpu as pltpu
from jax.sharding import PartitionSpec as P

HEADS = 12
HD = 64
PIECES = 2
NORM_ROWS = 16
QB = 128
WINDOW = 3 * QB
EPSILON = 1e-12
FAR = 1e30

BF = jnp.bfloat16
F32 = jnp.float32


def dot(a, b, ca, cb):
    return lax.dot_general(a, b, (((ca,), (cb,)), ((), ())), preferred_element_type=F32)


def slope_table(count):
    power_two = 2 ** int(math.floor(math.log2(count)))
    leading = [2.0 ** (-8.0 * (head + 1) / power_two) for head in range(power_two)]
    trailing = [2.0 ** (-4.0 * (2 * other + 1) / power_two) for other in range(count - power_two)]
    return np.array(leading + trailing, np.float32)


def smem():
    return pl.BlockSpec(memory_space=pltpu.SMEM)


def full(shape):
    return pl.BlockSpec(shape, lambda *_: (0,) * len(shape))


def cost(flops, moved, transcendentals=0):
    return pl.CostEstimate(
        flops=flops // 1000,
        bytes_accessed=moved // 1000,
        transcendentals=transcendentals // 1000,
    )


def params(mib):
    return pltpu.CompilerParams(vmem_limit_bytes=mib * 1024 * 1024)


def out(shape, kind=BF):
    return jax.ShapeDtypeStruct(shape, kind)


def vmem(count):
    return [pl.BlockSpec(memory_space=pltpu.VMEM)] * count


def after(value, *others):
    return lax.optimization_barrier((value, others))[0]


class Order:
    def __init__(self):
        self.last = ()

    def __call__(self, value):
        return after(value, *self.last)

    def note(self, value):
        self.last = (value,)
        return value


def block_distance(se_ref, off):
    start = se_ref[0:1, pl.ds(off, QB)] - off
    end = se_ref[1:2, pl.ds(off, QB)] - off
    key = lax.broadcasted_iota(jnp.int32, (WINDOW, QB), 0)
    query = lax.broadcasted_iota(jnp.int32, (WINDOW, QB), 1) + QB
    valid = (key >= start) & (key < end)
    return jnp.where(valid, jnp.abs(key - query).astype(F32), FAR)


def softmax(scores):
    shifted = jnp.exp(scores - jnp.max(scores, axis=0, keepdims=True))
    return shifted * (1.0 / jnp.sum(shifted, axis=0, keepdims=True))


def attend(heads, slopes_ref, se_ref, rows_ref, wt_ref, ctx_ref, qkv_ref, kv_ref):
    zero = jnp.zeros((HD, QB), BF)
    starts = range(0, ctx_ref.shape[1], QB)
    weights = wt_ref[...].reshape(3 * heads * HD, wt_ref.shape[2])
    pairs = jnp.concatenate(
        [wt_ref[part, h * HD : (h + 1) * HD, :] for h in range(heads) for part in (1, 2)], axis=0
    )
    for c in range(0, rows_ref.shape[0], 256):
        rows = rows_ref[c : c + 256, :]
        turned = dot(weights, rows, 1, 1).astype(BF)
        qkv_ref[:, :, c : c + 256] = turned.reshape(3, heads * HD, 256)
        kv_ref[c : c + 256, :] = dot(rows, pairs, 1, 1).astype(BF)
    for h in range(heads):
        mine = slice(h * HD, (h + 1) * HD)
        pair = slice(h * 2 * HD, (h + 1) * 2 * HD)
        scores = []
        for off in starts:
            query = qkv_ref[0, mine, off + QB : off + 2 * QB] * BF(0.125)
            key = kv_ref[off : off + WINDOW, pair]
            scores.append(dot(key, jnp.concatenate([query, zero], axis=0), 1, 0))
        probs = [
            softmax(x - slopes_ref[h] * block_distance(se_ref, off)).astype(BF)
            for off, x in zip(starts, scores)
        ]
        for off, x in zip(starts, probs):
            value = qkv_ref[2, mine, off : off + WINDOW]
            ctx_ref[mine, off : off + QB] = dot(value, x, 1, 0).astype(BF)


def attn_near_kernel(
    heads, place_ref, slopes_ref, se_ref, own_ref, sib_ref, edge_ref, edge_sib_ref, wt_ref,
    rows_ref, ctx_ref, qkv_ref, kv_ref,
):
    even = place_ref[4] == 0
    count = own_ref.shape[0]
    own, sib, edge, edge_sib = (r[...] for r in (own_ref, sib_ref, edge_ref, edge_sib_ref))
    rows_ref[0:QB, :] = jnp.where(even, edge, edge_sib)
    rows_ref[QB : QB + count, :] = jnp.where(even, own, sib)
    rows_ref[QB + count : QB + 2 * count, :] = jnp.where(even, sib, own)
    rows_ref[QB + 2 * count :, :] = jnp.where(even, edge_sib, edge)
    attend(heads, slopes_ref, se_ref, rows_ref, wt_ref, ctx_ref, qkv_ref, kv_ref)


def attended_kernel(place_ref, ctx_ref, w_ref, *refs):
    (*sums, own_ref, sent_ref) = refs
    count = own_ref.shape[0]
    for i, (ref, which) in enumerate(((own_ref, place_ref[4]), (sent_ref, 1 - place_ref[4]))):
        here = pl.ds(pl.multiple_of(which * count, 128), count)
        total = dot(ctx_ref[:, here], w_ref[...], 0, 0)
        if sums:
            total = sums[i][...] + total
        ref[...] = total.astype(ref.dtype)


def attn_fwd_outs(heads, here, count):
    return [
        out((heads * HD, here)),
        out((3, heads * HD, count)),
        out((count, heads * 2 * HD)),
    ]


def attn_cost(heads, here, count, width):
    elements = heads * here * WINDOW
    flops = elements * HD * 8 + 10 * heads * HD * count * width
    return cost(flops, count * width * 8, elements)


def attn_near(heads, place, slopes, se, own, sib, edge, edge_sib, wt):
    here, width = se.shape[1], own.shape[1]
    count = here + 2 * QB
    return pl.pallas_call(
        functools.partial(attn_near_kernel, heads),
        out_shape=[out((count, width))] + attn_fwd_outs(heads, here, count),
        in_specs=[smem(), smem()] + vmem(6),
        out_specs=vmem(4),
        compiler_params=params(16),
        cost_estimate=attn_cost(heads, here, count, width),
        name="attention_forward_near",
    )(place, slopes, se, own, sib, edge, edge_sib, wt)


def attn_far(heads, slopes, se, rows, wt):
    here, (count, width) = se.shape[1], rows.shape
    return pl.pallas_call(
        functools.partial(attend, heads),
        out_shape=attn_fwd_outs(heads, here, count),
        in_specs=[smem()] + vmem(3),
        out_specs=vmem(3),
        compiler_params=params(16),
        cost_estimate=attn_cost(heads, here, count, width),
        name="attention_forward_far",
    )(slopes, se, rows, wt)


def attended_halves(place, ctx, w, sums=()):
    half, width = ctx.shape[1] // 2, w.shape[1]
    return pl.pallas_call(
        attended_kernel,
        out_shape=[out((half, width), F32), out((half, width), BF if sums else F32)],
        in_specs=[smem()] + vmem(2 + len(sums)),
        out_specs=vmem(2),
        compiler_params=params(12),
        cost_estimate=cost(4 * ctx.size * width, 12 * half * width),
        name="attended_halves",
    )(place, ctx, w, *sums)


def head_back_kernel(head, slopes_ref, se_ref, qkv_ref, kv_ref, dctx_ref, out_ref, acc_ref):
    here = dctx_ref.shape[1]
    mine = slice(head * HD, (head + 1) * HD)
    keys = slice(head * 2 * HD, (head + 1) * 2 * HD)
    acc_ref[...] = jnp.zeros_like(acc_ref)
    edge = jnp.zeros((HD, QB), BF)
    out_ref[0, :, 0:QB] = edge
    out_ref[0, :, QB + here :] = edge
    slope = slopes_ref[head]
    starts = range(0, here, QB)
    pairs = []
    for off in starts:
        query = qkv_ref[0, mine, off + QB : off + 2 * QB] * BF(0.125)
        d_rows = dctx_ref[mine, off : off + QB]
        pairs.append(
            jnp.concatenate(
                [
                    jnp.concatenate([query, edge], axis=1),
                    jnp.concatenate([edge, d_rows], axis=1),
                ],
                axis=0,
            )
        )
    both = [dot(kv_ref[off : off + WINDOW, keys], pair, 1, 0) for off, pair in zip(starts, pairs)]
    probs = [
        softmax(x[:, :QB] - slope * block_distance(se_ref, off)) for off, x in zip(starts, both)
    ]
    row_dots = [jnp.sum(x[:, QB:] * p, axis=0, keepdims=True) for x, p in zip(both, probs)]
    d_scores = [
        (p * (x[:, QB:] - row_dot)).astype(BF) for x, p, row_dot in zip(both, probs, row_dots)
    ]
    probs = [p.astype(BF) for p in probs]
    for off, d in zip(starts, d_scores):
        d_query = dot(qkv_ref[1, mine, off : off + WINDOW], d, 1, 0) * 0.125
        out_ref[0, :, off + QB : off + 2 * QB] = d_query.astype(BF)
    sums = [
        dot(pair, jnp.concatenate([d, p], axis=1), 1, 1)
        for pair, d, p in zip(pairs, d_scores, probs)
    ]
    for off, x in zip(starts, sums):
        acc_ref[:, off : off + WINDOW] += x
    out_ref[1, :, :] = acc_ref[0:HD, :].astype(BF)
    out_ref[2, :, :] = acc_ref[HD:, :].astype(BF)


def head_back(head, slopes, se, qkv, kv, dctx):
    here, count = se.shape[1], qkv.shape[2]
    elements = here * WINDOW
    return pl.pallas_call(
        functools.partial(head_back_kernel, head),
        out_shape=out((3, HD, count)),
        in_specs=[smem()] + vmem(4),
        out_specs=vmem(1)[0],
        scratch_shapes=[pltpu.VMEM((2 * HD, count), F32)],
        compiler_params=params(12),
        cost_estimate=cost(elements * HD * 24, count * HD * 18, elements),
        name="attention_backward_head",
    )(slopes, se, qkv, kv, dctx)


def stack_heads(refs, all_ref):
    heads = len(refs)
    for h, ref in enumerate(refs):
        for part in range(3):
            at = (part * heads + h) * HD
            all_ref[at : at + HD, :] = ref[part]


def qkv_grad_kernel(heads, *refs):
    (rows_ref, *out_refs, all_ref) = refs[heads:]
    stack_heads(refs[:heads], all_ref)
    for c in range(0, rows_ref.shape[1], 256):
        total = dot(all_ref[...], rows_ref[:, c : c + 256], 1, 0).astype(BF)
        at = 0
        for ref in out_refs:
            ref[:, c : c + 256] = total[at : at + ref.shape[0]]
            at += ref.shape[0]


def qkv_grad(heads, rows, parts=(3,)):
    count, width = rows.shape
    size = len(heads) * HD
    return pl.pallas_call(
        functools.partial(qkv_grad_kernel, len(heads)),
        out_shape=[out((part * size, width)) for part in parts],
        in_specs=vmem(len(heads) + 1),
        out_specs=vmem(len(parts)),
        scratch_shapes=[pltpu.VMEM((3 * size, count), BF)],
        compiler_params=params(12),
        cost_estimate=cost(6 * size * count * width, count * width * 4),
        name="projection_gradient",
    )(*heads, rows)


def gather_back_kernel(
    place_ref, ctx_ref, own_ref, sib_ref, norms_ref, norms_sib_ref, w_out_ref, w_far_ref,
    datt_ref, grad_ref, dctx_ref, dctx_far_ref,
):
    even = place_ref[4] == 0
    half = datt_ref.shape[0] // 2
    own, sib = own_ref[...], sib_ref[...]
    datt_ref[0:half, :] = jnp.where(even, own, sib)
    datt_ref[half:, :] = jnp.where(even, sib, own)
    for c in range(0, 2 * half, 256):
        rows = datt_ref[c : c + 256, :]
        dctx_far_ref[:, c : c + 256] = dot(w_far_ref[...], rows, 1, 1).astype(BF)
        dctx_ref[:, c : c + 256] = dot(w_out_ref[...], rows, 1, 1).astype(BF)
    count = ctx_ref.shape[0]
    grad_ref[0:count, :] = dot(ctx_ref[...], datt_ref[...], 1, 0).astype(BF)
    norms = norms_ref[...].astype(F32) + norms_sib_ref[...].astype(F32)
    grad_ref[count:, :] = norms.astype(BF)


def gather_back(place, ctx, own, sib, norms, norms_sib, w_out, w_far):
    half, width = own.shape
    vm = pl.BlockSpec(memory_space=pltpu.VMEM)
    return pl.pallas_call(
        gather_back_kernel,
        out_shape=[
            out((2 * half, width)),
            jax.ShapeDtypeStruct((ctx.shape[0] + NORM_ROWS, width), BF),
            jax.ShapeDtypeStruct(ctx.shape, BF),
            jax.ShapeDtypeStruct(ctx.shape, BF),
        ],
        in_specs=[smem()] + [vm] * 7,
        out_specs=[vm] * 4,
        compiler_params=params(16),
        cost_estimate=cost(6 * ctx.size * width, 12 * half * width),
        name="gather_d_attended",
    )(place, ctx, own, sib, norms, norms_sib, w_out, w_far)


def phi_pair(gate):
    bell = jnp.exp(gate * gate * -0.5)
    t = 1.0 / (1.0 + (0.3275911 / math.sqrt(2.0)) * jnp.abs(gate))
    poly = t * (
        0.254829592
        + t * (-0.284496736 + t * (1.421413741 + t * (-1.453152027 + t * 1.061405429)))
    )
    tail = 0.5 * poly * bell
    return jnp.where(gate >= 0.0, 1.0 - tail, tail), bell * (1.0 / math.sqrt(2.0 * math.pi))


def ff_fwd_kernel(
    x0_ref, x1_ref, wg_ref, wu_ref, wd_ref, x_ref, act_ref, a_ref, b_ref, keep_ref, send_ref
):
    half = x0_ref.shape[0]
    for i, (source, target) in enumerate(((x0_ref, keep_ref), (x1_ref, send_ref))):
        rows = slice(i * half, (i + 1) * half)
        x = source[...]
        x_ref[rows, :] = x
        for f in range(0, wd_ref.shape[0], 256):
            cols = slice(f, f + 256)
            gate = dot(x, wg_ref[:, cols], 1, 0)
            up = dot(x, wu_ref[:, cols], 1, 0)
            big, small = phi_pair(gate)
            gelu = gate * big
            act_ref[rows, cols] = (gelu * up).astype(BF)
            a_ref[rows, cols] = gelu.astype(BF)
            b_ref[rows, cols] = (up * (big + gate * small)).astype(BF)
        target[...] = dot(act_ref[rows, :], wd_ref[...], 1, 0).astype(BF)


def ff_fwd(pieces, wg, wu, wd):
    half, width = pieces[0].shape
    hidden = wd.shape[0]
    rows = 2 * half
    return pl.pallas_call(
        ff_fwd_kernel,
        out_shape=[out((rows, width))] + [out((rows, hidden))] * 3 + [out((half, width))] * 2,
        in_specs=vmem(5),
        out_specs=vmem(6),
        compiler_params=params(16),
        cost_estimate=cost(rows * width * hidden * 6, 12 * rows * width, 2 * rows * hidden),
        name="ff_forward",
    )(*pieces, wg, wu, wd)


def ff_bwd_kernel(
    d0_ref, d1_ref, a_ref, b_ref, wd_ref, wg_ref, wu_ref,
    db_ref, dg_ref, du_ref, keep_ref, send_ref,
):
    half = d0_ref.shape[0]
    for i, (source, target) in enumerate(((d0_ref, keep_ref), (d1_ref, send_ref))):
        rows = slice(i * half, (i + 1) * half)
        db = source[...]
        db_ref[rows, :] = db
        for f in range(0, wd_ref.shape[0], 256):
            cols = slice(f, f + 256)
            d_active = dot(db, wd_ref[cols, :], 1, 1)
            dg_ref[rows, cols] = (d_active * b_ref[rows, cols].astype(F32)).astype(BF)
            du_ref[rows, cols] = (d_active * a_ref[rows, cols].astype(F32)).astype(BF)
        part = dot(dg_ref[rows, :], wg_ref[...], 1, 1) + dot(du_ref[rows, :], wu_ref[...], 1, 1)
        target[...] = part.astype(BF)


def ff_bwd(pieces, a, b, wd, wg, wu):
    half, width = pieces[0].shape
    hidden = wd.shape[0]
    rows = 2 * half
    return pl.pallas_call(
        ff_bwd_kernel,
        out_shape=[out((rows, width))] + [out((rows, hidden))] * 2 + [out((half, width))] * 2,
        in_specs=vmem(7),
        out_specs=vmem(5),
        compiler_params=params(16),
        cost_estimate=cost(rows * width * hidden * 6, 12 * rows * width),
        name="ff_backward",
    )(*pieces, a, b, wd, wg, wu)


def weight_near_kernel(a_ref, d_ref, out_ref):
    out_ref[...] = dot(a_ref[...], d_ref[...], 0, 0)


def weight_near(a, d):
    size = (a.shape[1], d.shape[1])
    return pl.pallas_call(
        weight_near_kernel,
        out_shape=out(size, F32),
        in_specs=vmem(2),
        out_specs=vmem(1)[0],
        compiler_params=params(16),
        cost_estimate=cost(2 * a.size * d.shape[1], a.size * 8),
        name="weight_gradient_near",
    )(a, d)


def weight_far_kernel(dim, place_ref, acc_ref, *refs):
    pairs, (out_ref, sent_ref) = refs[:-2], refs[-2:]
    a = jnp.concatenate([ref[...] for ref in pairs[0::2]], axis=0)
    d = jnp.concatenate([ref[...] for ref in pairs[1::2]], axis=0)
    out_ref[...] = (acc_ref[...] + dot(a, d, 0, 0)).astype(BF)
    half = sent_ref.shape[0]
    at = (1 - place_ref[dim]) * half
    sent_ref[...] = out_ref[pl.ds(pl.multiple_of(at, half), half), :]


def weight_far(place, dim, acc, *pairs):
    rows, width = acc.shape
    return pl.pallas_call(
        functools.partial(weight_far_kernel, dim),
        out_shape=[out((rows, width)), out((rows // 2, width))],
        in_specs=[smem()] + vmem(1 + len(pairs)),
        out_specs=vmem(2),
        compiler_params=params(16),
        cost_estimate=cost(2 * acc.size * rows, acc.size * 12),
        name="weight_gradient_far",
    )(place, acc, *pairs)


def centre(pre):
    mean = jnp.mean(pre, axis=-1, keepdims=True)
    centred = pre - mean
    r = lax.rsqrt(jnp.mean(centred * centred, axis=-1, keepdims=True) + EPSILON)
    return centred * r, r


def norm_back(xhat, r, gain, grad):
    e = grad * gain
    return r * (
        e
        - jnp.mean(e, axis=-1, keepdims=True)
        - xhat * jnp.mean(e * xhat, axis=-1, keepdims=True)
    )


def store_pieces(value, refs):
    refs[0][...] = value
    at = 0
    for ref in refs[1:]:
        ref[...] = value[at : at + ref.shape[0]]
        at += ref.shape[0]


def far_rows(refs):
    return jnp.concatenate([ref[...].astype(F32) for ref in refs], axis=0)


def ln1_kernel(
    x_ref, own_ref, recv_ref, gain_ref, bias_ref, pre_ref, normed_ref, *low_refs
):
    pre = x_ref[...].astype(F32) + (own_ref[...] + recv_ref[...].astype(F32))
    pre_ref[...] = pre
    xhat, _ = centre(pre)
    normed = xhat * gain_ref[...] + bias_ref[...]
    normed_ref[...] = normed
    store_pieces(normed.astype(BF), low_refs)


def ln1(x, own, recv, gain, bias):
    shape = x.shape
    vm = pl.BlockSpec(memory_space=pltpu.VMEM)
    return pl.pallas_call(
        ln1_kernel,
        out_shape=[
            out(shape, F32),
            out(shape, F32),
            out(shape),
            *[out((shape[0] // PIECES, shape[1]))] * PIECES,
        ],
        in_specs=[vm] * 5,
        out_specs=[vm] * (3 + PIECES),
        compiler_params=params(12),
        cost_estimate=cost(x.size * 10, x.size * 18),
        name="norm_one",
    )(x, own, recv, gain, bias)


def ln2_kernel(
    normed_ref, keep_ref, near_ref, dy_ref, gain_ref, bias_ref, *refs
):
    out_ref, d_ref, grads_ref, *low_refs = refs[PIECES:]
    branch = keep_ref[...].astype(F32) + near_ref[...].astype(F32) + far_rows(refs[:PIECES])
    xhat, r = centre(normed_ref[...] + branch)
    gain = gain_ref[...]
    out_ref[...] = (xhat * gain + bias_ref[...]).astype(BF)
    dy = dy_ref[...].astype(F32)
    d = norm_back(xhat, r, gain, dy)
    d_ref[...] = d
    store_pieces(d.astype(BF), low_refs)
    grads_ref[0:1, :] = jnp.sum(dy * xhat, axis=0, keepdims=True)
    grads_ref[1:2, :] = jnp.sum(dy, axis=0, keepdims=True)


def ln2(normed, keep, near, far, dy, gain, bias):
    shape = normed.shape
    return pl.pallas_call(
        ln2_kernel,
        out_shape=[
            out(shape),
            out(shape, F32),
            out((2, shape[1]), F32),
            out(shape),
            *[out((shape[0] // PIECES, shape[1]))] * PIECES,
        ],
        in_specs=vmem(6 + PIECES),
        out_specs=vmem(4 + PIECES),
        compiler_params=params(16),
        cost_estimate=cost(normed.size * 20, normed.size * 20),
        name="norm_two",
    )(normed, keep, near, dy, gain, bias, *far)


def ln1_back_kernel(
    pre_ref, d2_ref, keep_ref, near_ref, gain_ref, grads_two_ref, *refs
):
    d_ref, low_ref, norms_ref = refs[PIECES:]
    grad = d2_ref[...] + (
        keep_ref[...].astype(F32) + near_ref[...].astype(F32) + far_rows(refs[:PIECES])
    )
    xhat, r = centre(pre_ref[...])
    d = norm_back(xhat, r, gain_ref[...], grad)
    d_ref[...] = d
    width = d.shape[1]
    low_ref[...] = d.astype(BF)
    norms_ref[...] = jnp.concatenate(
        [
            jnp.sum(grad * xhat, axis=0, keepdims=True),
            jnp.sum(grad, axis=0, keepdims=True),
            grads_two_ref[...],
            jnp.zeros((NORM_ROWS - 4, width), F32),
        ],
        axis=0,
    ).astype(BF)


def ln1_back(pre, d2, keep, near, far, gain, grads_two):
    shape = pre.shape
    return pl.pallas_call(
        ln1_back_kernel,
        out_shape=[out(shape, F32), out(shape), out((NORM_ROWS, shape[1]))],
        in_specs=vmem(6 + PIECES),
        out_specs=vmem(3),
        compiler_params=params(16),
        cost_estimate=cost(pre.size * 20, pre.size * 20),
        name="norm_one_backward",
    )(pre, d2, keep, near, gain, grads_two, *far)


def swap(value, axis, bit):
    count = lax.axis_size(axis)
    return lax.ppermute(value, axis, [(i, i ^ bit) for i in range(count)])


def swap_chip_edges(value):
    count = lax.axis_size("seq") * lax.axis_size("tp")
    pairs = []
    for i in range(1, count - 1, 2):
        pairs += [(i, i + 1), (i + 1, i)]
    return lax.ppermute(value, ("seq", "tp"), pairs)


def fold_kernel(dims, place_ref, own_ref, recv_ref, keep_ref, send_ref):
    rows, half = recv_ref.shape[0], keep_ref.shape[0]
    base = place_ref[dims[0]] * rows
    cut = place_ref[dims[1]] * half
    for ref, at in ((keep_ref, cut), (send_ref, half - cut)):
        own = own_ref[pl.ds(pl.multiple_of(base + at, NORM_ROWS), half), :].astype(F32)
        recv = recv_ref[pl.ds(pl.multiple_of(at, NORM_ROWS), half), :].astype(F32)
        ref[...] = (own + recv).astype(BF)


def fold(place, dims, own, recv):
    rows, width = recv.shape
    vm = pl.BlockSpec(memory_space=pltpu.VMEM)
    return pl.pallas_call(
        functools.partial(fold_kernel, dims),
        out_shape=[jax.ShapeDtypeStruct((rows // 2, width), BF)] * 2,
        in_specs=[smem(), vm, vm],
        out_specs=[vm] * 2,
        compiler_params=params(10),
        cost_estimate=cost(recv.size, recv.size * 6),
        name="fold_half",
    )(place, own, recv)


def join_kernel(dim, place_ref, own_ref, recv_ref, out_ref):
    first = place_ref[dim] == 0
    half = own_ref.shape[0]
    own, recv = own_ref[...], recv_ref[...]
    out_ref[0:half, :] = jnp.where(first, own, recv).astype(out_ref.dtype)
    out_ref[half:, :] = jnp.where(first, recv, own).astype(out_ref.dtype)


def join(place, dim, own, recv, kind=BF):
    half, width = own.shape
    vm = pl.BlockSpec(memory_space=pltpu.VMEM)
    return pl.pallas_call(
        functools.partial(join_kernel, dim),
        out_shape=jax.ShapeDtypeStruct((2 * half, width), kind),
        in_specs=[smem(), vm, vm],
        out_specs=vm,
        compiler_params=params(10),
        cost_estimate=cost(0, own.size * 12),
        name="join_halves",
    )(place, own, recv)


def finish_in_kernel(dims, place_ref, g_ref, g_recv_ref, u_ref, u_recv_ref, out_ref):
    half = g_ref.shape[0]
    for i, (own_ref, recv_ref) in enumerate(((g_ref, g_recv_ref), (u_ref, u_recv_ref))):
        first = place_ref[dims[i]] == 0
        own, recv = own_ref[...], recv_ref[...]
        out_ref[0:half, i, :] = jnp.where(first, own, recv).astype(F32)
        out_ref[half:, i, :] = jnp.where(first, recv, own).astype(F32)


def finish_in(place, gate, up):
    half, width = gate[1].shape
    return pl.pallas_call(
        functools.partial(finish_in_kernel, (gate[0], up[0])),
        out_shape=out((2 * half, 2, width), F32),
        in_specs=[smem()] + vmem(4),
        out_specs=vmem(1)[0],
        compiler_params=params(16),
        cost_estimate=cost(0, gate[1].size * 24),
        name="finish_w_in_gradient",
    )(place, *gate[1:], *up[1:])


def finish_a_kernel(dim, place_ref, own_ref, recv_ref, _, out_ref):
    join_kernel(dim, place_ref, own_ref, recv_ref, out_ref)


def finish_a(place, dim, own, recv, later):
    half, width = own.shape
    return pl.pallas_call(
        functools.partial(finish_a_kernel, dim),
        grid=(1,),
        out_shape=jax.ShapeDtypeStruct(later.shape, F32),
        in_specs=[smem()]
        + [full((half, width))] * 2
        + [pl.BlockSpec(memory_space=pl.ANY)],
        out_specs=pl.BlockSpec((2 * half, width), lambda i: (0, 0)),
        input_output_aliases={3: 0},
        compiler_params=params(10),
        cost_estimate=cost(0, own.size * 12),
        name="finish_attention_gradient_a",
    )(place, own, recv, later)


def finish_b_kernel(dim, place_ref, own_ref, recv_ref, qkv_ref, out_ref, norm_ref):
    first = place_ref[dim] == 0
    own, recv = own_ref[...], recv_ref[...]
    step = own.shape[0] // 2
    count = step - NORM_ROWS
    low = jnp.where(first, own, recv).astype(F32)
    high = jnp.where(first, recv, own).astype(F32)
    for ref, rows in ((qkv_ref, low), (out_ref, high)):
        ref[0:count, :] = rows[0:count]
        ref[count:, :] = rows[step : step + count]
    norm_ref[...] = low[count : count + 4]


def finish_b(place, dim, own, recv, rows):
    half, width = own.shape
    rest = half - 2 * NORM_ROWS
    return pl.pallas_call(
        functools.partial(finish_b_kernel, dim),
        grid=(1,),
        out_shape=[
            jax.ShapeDtypeStruct((rows, width), F32),
            jax.ShapeDtypeStruct((rest, width), F32),
            jax.ShapeDtypeStruct((4, width), F32),
        ],
        in_specs=[smem()] + [full((half, width))] * 2,
        out_specs=[
            pl.BlockSpec((rest, width), lambda i: (rows // rest - 1, 0)),
            full((rest, width)),
            full((4, width)),
        ],
        compiler_params=params(10),
        cost_estimate=cost(0, own.size * 12),
        name="finish_attention_gradient_b",
    )(place, own, recv)


def send_half(place_ref, dim, ref, sent_ref):
    count = sent_ref.shape[0]
    at = (1 - place_ref[dim]) * count
    sent_ref[...] = ref[pl.ds(pl.multiple_of(at, NORM_ROWS), count), :]


def cut_a_kernel(dim, place_ref, own_ref, far_ref, a_ref, sent_ref):
    half = a_ref.shape[0]
    total = own_ref[0:half, :].astype(F32) + far_ref[...].astype(F32)
    a_ref[...] = total.astype(BF)
    send_half(place_ref, dim, a_ref, sent_ref)


def cut_a(place, dim, own, far):
    rows, width = far.shape
    return pl.pallas_call(
        functools.partial(cut_a_kernel, dim),
        out_shape=[out((rows, width)), out((rows // 2, width))],
        in_specs=[smem()] + vmem(2),
        out_specs=vmem(2),
        compiler_params=params(12),
        cost_estimate=cost(far.size, far.size * 8),
        name="add_far_shard_a",
    )(place, own, far)


def cut_b_kernel(dim, place_ref, own_ref, far_ref, out_ref, b_ref, sent_ref):
    rows = far_ref.shape[0]
    start = own_ref.shape[0] - rows
    value = (own_ref[start:, :].astype(F32) + far_ref[...].astype(F32)).astype(BF)
    step = b_ref.shape[0] // 4
    count = step - NORM_ROWS
    for i in range(4):
        at = (i % 2) * count
        source = value if i < 2 else out_ref
        b_ref[i * step : i * step + count, :] = source[at : at + count, :]
        b_ref[i * step + count : (i + 1) * step, :] = out_ref[2 * count :, :]
    send_half(place_ref, dim, b_ref, sent_ref)


def cut_b(place, dim, own, far, out_rows):
    width = own.shape[1]
    rows = far.shape[0] + out_rows.shape[0] + 3 * NORM_ROWS
    return pl.pallas_call(
        functools.partial(cut_b_kernel, dim),
        out_shape=[out((rows, width)), out((rows // 2, width))],
        in_specs=[smem()] + vmem(3),
        out_specs=vmem(2),
        compiler_params=params(12),
        cost_estimate=cost(far.size, far.size * 8),
        name="add_far_shard_b",
    )(place, own, far, out_rows)


def out_grad_kernel(ctx_ref, datt_ref, own_ref, far_ref, out_ref):
    count = ctx_ref.shape[0]
    near = dot(ctx_ref[...], datt_ref[...], 1, 0)
    out_ref[0:count, :] = (near + far_ref[0:count, :].astype(F32)).astype(BF)
    norms = own_ref[count:, :].astype(F32) + far_ref[count:, :].astype(F32)
    out_ref[count:, :] = norms.astype(BF)


def out_grad(ctx, datt, own, far):
    vm = pl.BlockSpec(memory_space=pltpu.VMEM)
    return pl.pallas_call(
        out_grad_kernel,
        out_shape=jax.ShapeDtypeStruct(far.shape, BF),
        in_specs=[vm] * 4,
        out_specs=vm,
        compiler_params=params(12),
        cost_estimate=cost(2 * ctx.size * datt.shape[1], datt.size * 2),
        name="out_gradient",
    )(ctx, datt, own, far)


class SeqSum:
    def __init__(self, place, order, dims, g, sent=None, last=None):
        self.place, self.order, self.dims, self.value = place, order, dims, g
        self.last = last
        self.stage = 1
        self.pairwise = lax.axis_size("seq") == 8
        if not self.pairwise:
            whole = lax.psum(g, "seq")
            half = g.shape[0] // 2
            self.dims = (len(dims),)
            self.value, self.moving = whole[:half], whole[half:]
            return
        if sent is None:
            half = g.shape[0] // 2
            sent = lax.dynamic_slice_in_dim(g, (1 - place[dims[0]]) * half, half, 0)
        self.send(0, sent)

    def send(self, dim, value):
        self.moving = swap(value, "seq", 1 << self.dims[dim])

    def step(self):
        stage, place, order, dims = self.stage, self.place, self.order, self.dims
        self.stage += 1
        if not self.pairwise and stage < 5:
            return
        value, moved = self.value, self.moving
        if stage < 5 or self.last is not None:
            value = order(value)
        if stage == 1:
            self.value, sent = fold(place, dims[:2], value, moved)
            order.note(sent)
            self.send(1, sent)
        elif stage in (2, 3):
            self.value = order.note(add(value, moved))
            self.send(2 if stage == 2 else 1, self.value)
        elif stage == 4:
            self.value = order.note(join(place, dims[1], value, moved))
            self.send(0, self.value)
        elif stage == 5:
            if self.last is None:
                self.result = (dims[0], self.value, moved)
                return
            self.result = self.last(place, dims[0], value, moved)
            order.note(jax.tree.leaves(self.result)[-1])


def add_kernel(a_ref, b_ref, out_ref):
    out_ref[...] = (a_ref[...].astype(F32) + b_ref[...].astype(F32)).astype(BF)


def add(a, b):
    return pl.pallas_call(
        add_kernel,
        out_shape=out(a.shape),
        in_specs=vmem(2),
        out_specs=vmem(1)[0],
        compiler_params=params(10),
        cost_estimate=cost(a.size, a.size * 6),
        name="add_pair",
    )(a, b)


def input_grad_kernel(place_ref, *refs):
    (*heads, wt_ref, wt_far_ref, own_ref, sent_ref, near_ref, far_ref) = refs
    stack_heads(heads[: len(heads) // 2], near_ref)
    stack_heads(heads[len(heads) // 2 :], far_ref)
    half = own_ref.shape[0]
    for ref, which in ((sent_ref, 1 - place_ref[4]), (own_ref, place_ref[4])):
        here = pl.ds(pl.multiple_of(which * half, 128), half)
        total = dot(near_ref[:, here], wt_ref[...], 0, 0)
        ref[...] = (total + dot(far_ref[:, here], wt_far_ref[...], 0, 0)).astype(ref.dtype)


def input_grad(place, near, far, wt, wt_far):
    count = near[0].shape[2]
    half, (size, width) = count // 2, wt.shape
    vm = pl.BlockSpec(memory_space=pltpu.VMEM)
    return pl.pallas_call(
        input_grad_kernel,
        out_shape=[
            jax.ShapeDtypeStruct((half, width), F32),
            jax.ShapeDtypeStruct((half, width), BF),
        ],
        in_specs=[smem()] + [vm] * (2 * len(near) + 2),
        out_specs=[vm] * 2,
        scratch_shapes=[pltpu.VMEM((size, count), BF)] * 2,
        compiler_params=params(16),
        cost_estimate=cost(4 * size * count * width, 12 * half * width),
        name="input_gradient",
    )(place, *near, *far, wt, wt_far)


def input_rows_kernel(place_ref, own_ref, recv_ref, pre_ref, out_ref, edge_ref):
    count, edge = out_ref.shape[0], edge_ref.shape[0]
    core = place_ref[4]
    at = pl.ds(pl.multiple_of(core * count, edge), edge)
    edge_ref[...] = (own_ref[at, :] + recv_ref[at, :].astype(F32)).astype(BF)
    at = pl.ds(pl.multiple_of((1 - core) * edge, edge), count)
    out_ref[...] = pre_ref[...] + (own_ref[at, :] + recv_ref[at, :].astype(F32))


def input_rows(place, own, recv, pre):
    vm = pl.BlockSpec(memory_space=pltpu.VMEM)
    return pl.pallas_call(
        input_rows_kernel,
        out_shape=[
            jax.ShapeDtypeStruct(pre.shape, F32),
            jax.ShapeDtypeStruct((QB, pre.shape[1]), BF),
        ],
        in_specs=[smem()] + [vm] * 3,
        out_specs=[vm] * 2,
        compiler_params=params(16),
        cost_estimate=cost(pre.size * 2, pre.size * 16),
        name="input_gradient_rows",
    )(place, own, recv, pre)


def input_edge_kernel(place_ref, rows_ref, edge_ref, out_ref):
    out_ref[...] = rows_ref[...]
    edge = edge_ref.shape[0]
    start = place_ref[4] * (rows_ref.shape[0] - edge)
    at = pl.ds(pl.multiple_of(start, edge), edge)
    out_ref[at, :] = rows_ref[at, :] + edge_ref[...].astype(F32)


def input_edge(place, rows, edge):
    vm = pl.BlockSpec(memory_space=pltpu.VMEM)
    return pl.pallas_call(
        input_edge_kernel,
        out_shape=jax.ShapeDtypeStruct(rows.shape, F32),
        in_specs=[smem()] + [vm] * 2,
        out_specs=vm,
        compiler_params=params(12),
        cost_estimate=cost(rows.size, rows.size * 10),
        name="input_gradient_edge",
    )(place, rows, edge)


def per_device(
    inputs, lengths, w_qkv, w_out, w_in, w_down, ln1_gain, ln1_bias, ln2_gain, ln2_bias, cotangent
):
    own_rows, width = inputs.shape
    tp_count = lax.axis_size("tp")
    head_width = w_qkv.shape[2]
    heads = head_width // HD
    chip_rows = 2 * own_rows
    tp = lax.axis_index("tp")
    seq = lax.axis_index("seq")
    core = tp & 1
    even = core == 0
    first = (seq * tp_count + 2 * (tp >> 1)) * own_rows
    place = jnp.stack([seq & 1, (seq >> 1) & 1, (seq >> 2) & 1, 0 * core, core]).astype(jnp.int32)

    bounds = jnp.cumsum(lengths)[:, None]
    tokens = (first + jnp.arange(chip_rows, dtype=jnp.int32))[None, :]
    before = bounds <= tokens
    start = jnp.max(jnp.where(before, bounds, 0), axis=0)
    end = jnp.min(jnp.where(before, jnp.iinfo(jnp.int32).max, bounds), axis=0)
    se = jnp.stack([start, end]) - (first - QB)
    se = jnp.pad(se, ((0, 6), (0, 0)))
    table = jnp.asarray(slope_table(HEADS))
    slopes = lax.dynamic_slice_in_dim(table, tp * heads, heads)
    slopes_far = lax.dynamic_slice_in_dim(table, (tp ^ 2) * heads, heads)

    wt = w_qkv.transpose(0, 2, 1).reshape(3 * head_width, width)
    wt_far = swap(wt, "tp", 2)

    sibling = swap(inputs, "tp", 1)
    edge = swap_chip_edges(
        lax.dynamic_slice_in_dim(inputs, core * (own_rows - QB), QB, axis=0)
    )
    edge_sibling = swap(edge, "tp", 1)
    rows, ctx, qkv, kv = attn_near(
        heads, place, slopes, se, inputs, sibling, edge, edge_sibling,
        wt.reshape(3, head_width, width),
    )
    w_out_far = swap(after(w_out, ctx), "tp", 2)
    near_sums = attended_halves(place, ctx, w_out)
    ctx_far, qkv_far, kv_far = attn_far(
        heads, slopes_far, se, rows, wt_far.reshape(3, head_width, width)
    )
    attended, attended_sent = attended_halves(place, ctx_far, w_out_far, near_sums)
    attended_sent = swap(attended_sent, "tp", 1)
    gain1, bias1 = ln1_gain[None], ln1_bias[None]
    gain2, bias2 = ln2_gain[None], ln2_bias[None]
    pre_one, normed, low, *low_pieces = ln1(inputs, attended, attended_sent, gain1, bias1)

    order = Order()
    w_in_late = after(w_in, low)
    wg, wu = w_in_late[:, 0], w_in_late[:, 1]

    def both_ways(own, pieces, work, between=lambda near_out: None):
        far = [swap(piece, "tp", 2) for piece in pieces]
        near_out = work(0, own, order(swap(own, "tp", 1)))
        near_keep, near_send = near_out[-2:]
        order.note(near_send)
        recv = swap(near_send, "tp", 1)
        between(near_out)
        far = [order(rows) for rows in far]
        far_sibling = [swap(rows, "tp", 1) for rows in far]
        outs, sums = [near_out], []
        for rows, rows_sibling in zip(far, far_sibling):
            outs.append(work(len(outs), order(rows), rows_sibling))
            order.note(outs[-1][-1])
        from_sibling = [swap(o[-1], "tp", 1) for o in outs[1:]]
        for i, (o, theirs) in enumerate(zip(outs[1:], from_sibling)):
            total = order.note(add(order(o[-2]), theirs))
            sums.append(swap(total, "tp", 2))
        return outs, (near_keep, recv, sums)

    order.note(low)
    forward, parts = both_ways(
        low, low_pieces, lambda i, a, b: ff_fwd((a, b), wg, wu, w_down)
    )
    layer_out, d_pre_two, grads_two, d_branch, *d_branch_pieces = ln2(
        normed, order(parts[0]), *parts[1:], cotangent, gain2, bias2
    )
    order.note(d_branch)

    weight_near_parts = []

    def grads_between(near_out):
        for x, d in weight_pairs:
            part = weight_near(order(forward[0][x]), near_out[d])
            weight_near_parts.append(order.note(part))

    weight_pairs = ((1, 0), (0, 2), (0, 1))
    backward, parts = both_ways(
        d_branch,
        d_branch_pieces,
        lambda i, a, b: ff_bwd((a, b), forward[i][2], forward[i][3], w_down, wg, wu),
        grads_between,
    )

    def join_whole(*halves):
        return join(*halves, F32)

    def weight_sum(which, dims):
        x, d = weight_pairs[which]
        pairs = [t for f, b in zip(forward[1:], backward[1:]) for t in (f[x], b[d])]
        total, sent = weight_far(
            place, dims[0], order(weight_near_parts[which]), *pairs
        )
        order.note(sent)
        return SeqSum(place, order, dims, total, sent, None if which else join_whole)

    d_far, d_near = [], []

    def one_head(h, far):
        kept = (slopes_far, se, qkv_far, kv_far) if far else (slopes, se, qkv, kv)
        return order.note(head_back(h, *kept, order(d_ctx_far if far else d_ctx)))

    down = weight_sum(0, (0, 1, 2))
    up = weight_sum(1, (0, 1, 2))
    gate = weight_sum(2, (1, 0, 2))
    d_pre_one, half, norms = ln1_back(
        pre_one, d_pre_two, order(parts[0]), *parts[1:], gain1, grads_two
    )
    order.note(half)
    half_sibling = swap(half, "tp", 1)
    norms_sibling = swap(norms, "tp", 1)
    down.step()
    gate.step()
    d_attended, sent_out, d_ctx, d_ctx_far = gather_back(
        place, order(ctx_far), half, half_sibling, norms, norms_sibling, w_out, w_out_far
    )
    order.note(d_ctx_far)
    far_out = swap(sent_out, "tp", 2)
    d_far.append(one_head(0, True))
    down.step()
    d_far.append(one_head(1, True))
    up.step()
    d_far.append(one_head(2, True))
    grad_out = order.note(out_grad(ctx, order(d_attended), sent_out, far_out))
    gate.step()
    far_qk, far_v = qkv_grad(d_far, order(rows), (2, 1))
    order.note(far_v)
    far_v = swap(far_v, "tp", 2)
    far_qk = swap(far_qk, "tp", 2)
    d_near.append(one_head(0, False))
    down.step()
    d_near.append(one_head(1, False))
    up.step()
    d_near.append(one_head(2, False))
    (own_qkv,) = qkv_grad(d_near, order(rows))
    order.note(own_qkv)
    total, sent = cut_b(place, 0, order(own_qkv), far_v, grad_out)
    order.note(sent)
    attn_b = SeqSum(
        place, order, (0, 1, 2), total, sent, lambda *h: finish_b(*h, own_qkv.shape[0])
    )
    gate.step()
    down.step()
    attn_b.step()
    total, sent = cut_a(place, 1, order(own_qkv), far_qk)
    order.note(sent)
    attn_a = SeqSum(place, order, (1, 0, 2), total, sent, lambda *h: finish_a(*h, attn_b.result[0]))
    up.step()
    window_own, window_sent = input_grad(
        place, [order(d_near[0]), *d_near[1:]], d_far, wt, wt_far
    )
    order.note(window_sent)
    window_sent = swap(window_sent, "tp", 1)
    attn_b.step()
    attn_a.step()
    down.step()
    gate.step()
    attn_a.step()
    up.step()
    attn_b.step()
    attn_a.step()
    attn_b.step()
    attn_a.step()
    grad_rows, d_edge = input_rows(place, order(window_own), window_sent, d_pre_one)
    order.note(d_edge)
    d_edge = swap_chip_edges(d_edge)
    up.step()
    gate.step()
    grad_in = order.note(
        finish_in(order(place), gate.result, up.result)
    )
    attn_b.step()
    attn_a.step()
    grad_input = order.note(input_edge(place, order(grad_rows), d_edge))
    assert all(unit.stage == 6 for unit in (down, gate, up, attn_a, attn_b))
    grad_down = down.result
    _, grad_out, norm_grads = attn_b.result
    grad_qkv = attn_a.result
    grad_qkv = grad_qkv.reshape(3, head_width, width).transpose(0, 2, 1)
    return (
        layer_out,
        grad_input,
        grad_qkv,
        grad_out,
        grad_in,
        grad_down,
        norm_grads[0],
        norm_grads[1],
        norm_grads[2],
        norm_grads[3],
    )


def solution(mesh):
    in_specs = (
        P(("seq", "tp"), None),
        P(),
        P(None, None, "tp"),
        P("tp", None),
        P(None, None, "tp"),
        P("tp", None),
        P(),
        P(),
        P(),
        P(),
        P(("seq", "tp"), None),
    )
    out_specs = (
        P(("seq", "tp"), None),
        P(("seq", "tp"), None),
        P(None, None, "tp"),
        P("tp", None),
        P(None, None, "tp"),
        P("tp", None),
        P(),
        P(),
        P(),
        P(),
    )
    return jax.shard_map(
        per_device, mesh=mesh, in_specs=in_specs, out_specs=out_specs, check_vma=False
    )
```

```python
import functools
import math

import jax
import jax.numpy as jnp
import numpy as np
from jax import lax
from jax.experimental import pallas as pl
from jax.experimental.pallas import tpu as pltpu
from jax.sharding import PartitionSpec as P

HEADS = 12
HD = 64
PIECES = 2
NORM_ROWS = 16
QB = 128
WINDOW = 3 * QB
EPSILON = 1e-12
FAR = 1e30

BF = jnp.bfloat16
F32 = jnp.float32


def dot(a, b, ca, cb):
    return lax.dot_general(a, b, (((ca,), (cb,)), ((), ())), preferred_element_type=F32)


def slope_table(count):
    power_two = 2 ** int(math.floor(math.log2(count)))
    leading = [2.0 ** (-8.0 * (head + 1) / power_two) for head in range(power_two)]
    trailing = [2.0 ** (-4.0 * (2 * other + 1) / power_two) for other in range(count - power_two)]
    return np.array(leading + trailing, np.float32)


def smem():
    return pl.BlockSpec(memory_space=pltpu.SMEM)


def full(shape):
    return pl.BlockSpec(shape, lambda *_: (0,) * len(shape))


def cost(flops, moved, transcendentals=0):
    return pl.CostEstimate(
        flops=flops // 1000,
        bytes_accessed=moved // 1000,
        transcendentals=transcendentals // 1000,
    )


def params(mib):
    return pltpu.CompilerParams(vmem_limit_bytes=mib * 1024 * 1024)


def out(shape, kind=BF):
    return jax.ShapeDtypeStruct(shape, kind)


def vmem(count):
    return [pl.BlockSpec(memory_space=pltpu.VMEM)] * count


def after(value, *others):
    return lax.optimization_barrier((value, others))[0]


class Order:
    def __init__(self):
        self.last = ()

    def __call__(self, value):
        return after(value, *self.last)

    def note(self, value):
        self.last = (value,)
        return value


def block_distance(se_ref, off):
    start = se_ref[0:1, pl.ds(off, QB)] - off
    end = se_ref[1:2, pl.ds(off, QB)] - off
    key = lax.broadcasted_iota(jnp.int32, (WINDOW, QB), 0)
    query = lax.broadcasted_iota(jnp.int32, (WINDOW, QB), 1) + QB
    valid = (key >= start) & (key < end)
    return jnp.where(valid, jnp.abs(key - query).astype(F32), FAR)


def softmax(scores):
    shifted = jnp.exp(scores - jnp.max(scores, axis=0, keepdims=True))
    return shifted * (1.0 / jnp.sum(shifted, axis=0, keepdims=True))


def attend(heads, slopes_ref, se_ref, rows_ref, wt_ref, ctx_ref, qkv_ref, kv_ref):
    zero = jnp.zeros((HD, QB), BF)
    starts = range(0, ctx_ref.shape[1], QB)
    weights = wt_ref[...].reshape(3 * heads * HD, wt_ref.shape[2])
    pairs = jnp.concatenate(
        [wt_ref[part, h * HD : (h + 1) * HD, :] for h in range(heads) for part in (1, 2)], axis=0
    )
    for c in range(0, rows_ref.shape[0], 256):
        rows = rows_ref[c : c + 256, :]
        turned = dot(weights, rows, 1, 1).astype(BF)
        qkv_ref[:, :, c : c + 256] = turned.reshape(3, heads * HD, 256)
        kv_ref[c : c + 256, :] = dot(rows, pairs, 1, 1).astype(BF)
    for h in range(heads):
        mine = slice(h * HD, (h + 1) * HD)
        pair = slice(h * 2 * HD, (h + 1) * 2 * HD)
        scores = []
        for off in starts:
            query = qkv_ref[0, mine, off + QB : off + 2 * QB] * BF(0.125)
            key = kv_ref[off : off + WINDOW, pair]
            scores.append(dot(key, jnp.concatenate([query, zero], axis=0), 1, 0))
        probs = [
            softmax(x - slopes_ref[h] * block_distance(se_ref, off)).astype(BF)
            for off, x in zip(starts, scores)
        ]
        for off, x in zip(starts, probs):
            value = qkv_ref[2, mine, off : off + WINDOW]
            ctx_ref[mine, off : off + QB] = dot(value, x, 1, 0).astype(BF)


def attn_near_kernel(
    heads, place_ref, slopes_ref, se_ref, own_ref, sib_ref, edge_ref, edge_sib_ref, wt_ref,
    rows_ref, ctx_ref, qkv_ref, kv_ref,
):
    even = place_ref[4] == 0
    count = own_ref.shape[0]
    own, sib, edge, edge_sib = (r[...] for r in (own_ref, sib_ref, edge_ref, edge_sib_ref))
    rows_ref[0:QB, :] = jnp.where(even, edge, edge_sib)
    rows_ref[QB : QB + count, :] = jnp.where(even, own, sib)
    rows_ref[QB + count : QB + 2 * count, :] = jnp.where(even, sib, own)
    rows_ref[QB + 2 * count :, :] = jnp.where(even, edge_sib, edge)
    attend(heads, slopes_ref, se_ref, rows_ref, wt_ref, ctx_ref, qkv_ref, kv_ref)


def attended_kernel(place_ref, ctx_ref, w_ref, *refs):
    (*sums, own_ref, sent_ref) = refs
    count = own_ref.shape[0]
    for i, (ref, which) in enumerate(((own_ref, place_ref[4]), (sent_ref, 1 - place_ref[4]))):
        here = pl.ds(pl.multiple_of(which * count, 128), count)
        total = dot(ctx_ref[:, here], w_ref[...], 0, 0)
        if sums:
            total = sums[i][...] + total
        ref[...] = total.astype(ref.dtype)


def attn_fwd_outs(heads, here, count):
    return [
        out((heads * HD, here)),
        out((3, heads * HD, count)),
        out((count, heads * 2 * HD)),
    ]


def attn_cost(heads, here, count, width):
    elements = heads * here * WINDOW
    flops = elements * HD * 8 + 10 * heads * HD * count * width
    return cost(flops, count * width * 8, elements)


def attn_near(heads, place, slopes, se, own, sib, edge, edge_sib, wt):
    here, width = se.shape[1], own.shape[1]
    count = here + 2 * QB
    return pl.pallas_call(
        functools.partial(attn_near_kernel, heads),
        out_shape=[out((count, width))] + attn_fwd_outs(heads, here, count),
        in_specs=[smem(), smem()] + vmem(6),
        out_specs=vmem(4),
        compiler_params=params(16),
        cost_estimate=attn_cost(heads, here, count, width),
        name="attention_forward_near",
    )(place, slopes, se, own, sib, edge, edge_sib, wt)


def attn_far(heads, slopes, se, rows, wt):
    here, (count, width) = se.shape[1], rows.shape
    return pl.pallas_call(
        functools.partial(attend, heads),
        out_shape=attn_fwd_outs(heads, here, count),
        in_specs=[smem()] + vmem(3),
        out_specs=vmem(3),
        compiler_params=params(16),
        cost_estimate=attn_cost(heads, here, count, width),
        name="attention_forward_far",
    )(slopes, se, rows, wt)


def attended_halves(place, ctx, w, sums=()):
    half, width = ctx.shape[1] // 2, w.shape[1]
    return pl.pallas_call(
        attended_kernel,
        out_shape=[out((half, width), F32), out((half, width), BF if sums else F32)],
        in_specs=[smem()] + vmem(2 + len(sums)),
        out_specs=vmem(2),
        compiler_params=params(12),
        cost_estimate=cost(4 * ctx.size * width, 12 * half * width),
        name="attended_halves",
    )(place, ctx, w, *sums)


def head_back_kernel(head, slopes_ref, se_ref, qkv_ref, kv_ref, dctx_ref, out_ref, acc_ref):
    here = dctx_ref.shape[1]
    mine = slice(head * HD, (head + 1) * HD)
    keys = slice(head * 2 * HD, (head + 1) * 2 * HD)
    acc_ref[...] = jnp.zeros_like(acc_ref)
    edge = jnp.zeros((HD, QB), BF)
    out_ref[0, :, 0:QB] = edge
    out_ref[0, :, QB + here :] = edge
    slope = slopes_ref[head]
    starts = range(0, here, QB)
    pairs = []
    for off in starts:
        query = qkv_ref[0, mine, off + QB : off + 2 * QB] * BF(0.125)
        d_rows = dctx_ref[mine, off : off + QB]
        pairs.append(
            jnp.concatenate(
                [
                    jnp.concatenate([query, edge], axis=1),
                    jnp.concatenate([edge, d_rows], axis=1),
                ],
                axis=0,
            )
        )
    both = [dot(kv_ref[off : off + WINDOW, keys], pair, 1, 0) for off, pair in zip(starts, pairs)]
    probs = [
        softmax(x[:, :QB] - slope * block_distance(se_ref, off)) for off, x in zip(starts, both)
    ]
    row_dots = [jnp.sum(x[:, QB:] * p, axis=0, keepdims=True) for x, p in zip(both, probs)]
    d_scores = [
        (p * (x[:, QB:] - row_dot)).astype(BF) for x, p, row_dot in zip(both, probs, row_dots)
    ]
    probs = [p.astype(BF) for p in probs]
    for off, d in zip(starts, d_scores):
        d_query = dot(qkv_ref[1, mine, off : off + WINDOW], d, 1, 0) * 0.125
        out_ref[0, :, off + QB : off + 2 * QB] = d_query.astype(BF)
    sums = [
        dot(pair, jnp.concatenate([d, p], axis=1), 1, 1)
        for pair, d, p in zip(pairs, d_scores, probs)
    ]
    for off, x in zip(starts, sums):
        acc_ref[:, off : off + WINDOW] += x
    out_ref[1, :, :] = acc_ref[0:HD, :].astype(BF)
    out_ref[2, :, :] = acc_ref[HD:, :].astype(BF)


def head_back(head, slopes, se, qkv, kv, dctx):
    here, count = se.shape[1], qkv.shape[2]
    elements = here * WINDOW
    return pl.pallas_call(
        functools.partial(head_back_kernel, head),
        out_shape=out((3, HD, count)),
        in_specs=[smem()] + vmem(4),
        out_specs=vmem(1)[0],
        scratch_shapes=[pltpu.VMEM((2 * HD, count), F32)],
        compiler_params=params(12),
        cost_estimate=cost(elements * HD * 24, count * HD * 18, elements),
        name="attention_backward_head",
    )(slopes, se, qkv, kv, dctx)


def stack_heads(refs, all_ref):
    heads = len(refs)
    for h, ref in enumerate(refs):
        for part in range(3):
            at = (part * heads + h) * HD
            all_ref[at : at + HD, :] = ref[part]


def qkv_grad_kernel(heads, *refs):
    (rows_ref, *out_refs, all_ref) = refs[heads:]
    stack_heads(refs[:heads], all_ref)
    for c in range(0, rows_ref.shape[1], 256):
        total = dot(all_ref[...], rows_ref[:, c : c + 256], 1, 0).astype(BF)
        at = 0
        for ref in out_refs:
            ref[:, c : c + 256] = total[at : at + ref.shape[0]]
            at += ref.shape[0]


def qkv_grad(heads, rows, parts=(3,)):
    count, width = rows.shape
    size = len(heads) * HD
    return pl.pallas_call(
        functools.partial(qkv_grad_kernel, len(heads)),
        out_shape=[out((part * size, width)) for part in parts],
        in_specs=vmem(len(heads) + 1),
        out_specs=vmem(len(parts)),
        scratch_shapes=[pltpu.VMEM((3 * size, count), BF)],
        compiler_params=params(12),
        cost_estimate=cost(6 * size * count * width, count * width * 4),
        name="projection_gradient",
    )(*heads, rows)


def gather_back_kernel(
    place_ref, ctx_ref, own_ref, sib_ref, norms_ref, norms_sib_ref, w_out_ref, w_far_ref,
    datt_ref, grad_ref, dctx_ref, dctx_far_ref,
):
    even = place_ref[4] == 0
    half = datt_ref.shape[0] // 2
    own, sib = own_ref[...], sib_ref[...]
    datt_ref[0:half, :] = jnp.where(even, own, sib)
    datt_ref[half:, :] = jnp.where(even, sib, own)
    for c in range(0, 2 * half, 256):
        rows = datt_ref[c : c + 256, :]
        dctx_far_ref[:, c : c + 256] = dot(w_far_ref[...], rows, 1, 1).astype(BF)
        dctx_ref[:, c : c + 256] = dot(w_out_ref[...], rows, 1, 1).astype(BF)
    count = ctx_ref.shape[0]
    grad_ref[0:count, :] = dot(ctx_ref[...], datt_ref[...], 1, 0).astype(BF)
    norms = norms_ref[...].astype(F32) + norms_sib_ref[...].astype(F32)
    grad_ref[count:, :] = norms.astype(BF)


def gather_back(place, ctx, own, sib, norms, norms_sib, w_out, w_far):
    half, width = own.shape
    vm = pl.BlockSpec(memory_space=pltpu.VMEM)
    return pl.pallas_call(
        gather_back_kernel,
        out_shape=[
            out((2 * half, width)),
            jax.ShapeDtypeStruct((ctx.shape[0] + NORM_ROWS, width), BF),
            jax.ShapeDtypeStruct(ctx.shape, BF),
            jax.ShapeDtypeStruct(ctx.shape, BF),
        ],
        in_specs=[smem()] + [vm] * 7,
        out_specs=[vm] * 4,
        compiler_params=params(16),
        cost_estimate=cost(6 * ctx.size * width, 12 * half * width),
        name="gather_d_attended",
    )(place, ctx, own, sib, norms, norms_sib, w_out, w_far)


def phi_pair(gate):
    bell = jnp.exp(gate * gate * -0.5)
    t = 1.0 / (1.0 + (0.3275911 / math.sqrt(2.0)) * jnp.abs(gate))
    poly = t * (
        0.254829592
        + t * (-0.284496736 + t * (1.421413741 + t * (-1.453152027 + t * 1.061405429)))
    )
    tail = 0.5 * poly * bell
    return jnp.where(gate >= 0.0, 1.0 - tail, tail), bell * (1.0 / math.sqrt(2.0 * math.pi))


def ff_fwd_kernel(
    x0_ref, x1_ref, wg_ref, wu_ref, wd_ref, x_ref, act_ref, a_ref, b_ref, keep_ref, send_ref
):
    half = x0_ref.shape[0]
    for i, (source, target) in enumerate(((x0_ref, keep_ref), (x1_ref, send_ref))):
        rows = slice(i * half, (i + 1) * half)
        x = source[...]
        x_ref[rows, :] = x
        for f in range(0, wd_ref.shape[0], 256):
            cols = slice(f, f + 256)
            gate = dot(x, wg_ref[:, cols], 1, 0)
            up = dot(x, wu_ref[:, cols], 1, 0)
            big, small = phi_pair(gate)
            gelu = gate * big
            act_ref[rows, cols] = (gelu * up).astype(BF)
            a_ref[rows, cols] = gelu.astype(BF)
            b_ref[rows, cols] = (up * (big + gate * small)).astype(BF)
        target[...] = dot(act_ref[rows, :], wd_ref[...], 1, 0).astype(BF)


def ff_fwd(pieces, wg, wu, wd):
    half, width = pieces[0].shape
    hidden = wd.shape[0]
    rows = 2 * half
    return pl.pallas_call(
        ff_fwd_kernel,
        out_shape=[out((rows, width))] + [out((rows, hidden))] * 3 + [out((half, width))] * 2,
        in_specs=vmem(5),
        out_specs=vmem(6),
        compiler_params=params(16),
        cost_estimate=cost(rows * width * hidden * 6, 12 * rows * width, 2 * rows * hidden),
        name="ff_forward",
    )(*pieces, wg, wu, wd)


def ff_bwd_kernel(
    d0_ref, d1_ref, a_ref, b_ref, wd_ref, wg_ref, wu_ref,
    db_ref, dg_ref, du_ref, keep_ref, send_ref,
):
    half = d0_ref.shape[0]
    for i, (source, target) in enumerate(((d0_ref, keep_ref), (d1_ref, send_ref))):
        rows = slice(i * half, (i + 1) * half)
        db = source[...]
        db_ref[rows, :] = db
        for f in range(0, wd_ref.shape[0], 256):
            cols = slice(f, f + 256)
            d_active = dot(db, wd_ref[cols, :], 1, 1)
            dg_ref[rows, cols] = (d_active * b_ref[rows, cols].astype(F32)).astype(BF)
            du_ref[rows, cols] = (d_active * a_ref[rows, cols].astype(F32)).astype(BF)
        part = dot(dg_ref[rows, :], wg_ref[...], 1, 1) + dot(du_ref[rows, :], wu_ref[...], 1, 1)
        target[...] = part.astype(BF)


def ff_bwd(pieces, a, b, wd, wg, wu):
    half, width = pieces[0].shape
    hidden = wd.shape[0]
    rows = 2 * half
    return pl.pallas_call(
        ff_bwd_kernel,
        out_shape=[out((rows, width))] + [out((rows, hidden))] * 2 + [out((half, width))] * 2,
        in_specs=vmem(7),
        out_specs=vmem(5),
        compiler_params=params(16),
        cost_estimate=cost(rows * width * hidden * 6, 12 * rows * width),
        name="ff_backward",
    )(*pieces, a, b, wd, wg, wu)


def weight_near_kernel(a_ref, d_ref, out_ref):
    out_ref[...] = dot(a_ref[...], d_ref[...], 0, 0)


def weight_near(a, d):
    size = (a.shape[1], d.shape[1])
    return pl.pallas_call(
        weight_near_kernel,
        out_shape=out(size, F32),
        in_specs=vmem(2),
        out_specs=vmem(1)[0],
        compiler_params=params(16),
        cost_estimate=cost(2 * a.size * d.shape[1], a.size * 8),
        name="weight_gradient_near",
    )(a, d)


def weight_far_kernel(dim, place_ref, acc_ref, *refs):
    pairs, (out_ref, sent_ref) = refs[:-2], refs[-2:]
    a = jnp.concatenate([ref[...] for ref in pairs[0::2]], axis=0)
    d = jnp.concatenate([ref[...] for ref in pairs[1::2]], axis=0)
    out_ref[...] = (acc_ref[...] + dot(a, d, 0, 0)).astype(BF)
    half = sent_ref.shape[0]
    at = (1 - place_ref[dim]) * half
    sent_ref[...] = out_ref[pl.ds(pl.multiple_of(at, half), half), :]


def weight_far(place, dim, acc, *pairs):
    rows, width = acc.shape
    return pl.pallas_call(
        functools.partial(weight_far_kernel, dim),
        out_shape=[out((rows, width)), out((rows // 2, width))],
        in_specs=[smem()] + vmem(1 + len(pairs)),
        out_specs=vmem(2),
        compiler_params=params(16),
        cost_estimate=cost(2 * acc.size * rows, acc.size * 12),
        name="weight_gradient_far",
    )(place, acc, *pairs)


def centre(pre):
    mean = jnp.mean(pre, axis=-1, keepdims=True)
    centred = pre - mean
    r = lax.rsqrt(jnp.mean(centred * centred, axis=-1, keepdims=True) + EPSILON)
    return centred * r, r


def norm_back(xhat, r, gain, grad):
    e = grad * gain
    return r * (
        e
        - jnp.mean(e, axis=-1, keepdims=True)
        - xhat * jnp.mean(e * xhat, axis=-1, keepdims=True)
    )


def store_pieces(value, refs):
    refs[0][...] = value
    at = 0
    for ref in refs[1:]:
        ref[...] = value[at : at + ref.shape[0]]
        at += ref.shape[0]


def far_rows(refs):
    return jnp.concatenate([ref[...].astype(F32) for ref in refs], axis=0)


def ln1_kernel(
    x_ref, own_ref, recv_ref, gain_ref, bias_ref, pre_ref, normed_ref, *low_refs
):
    pre = x_ref[...].astype(F32) + (own_ref[...] + recv_ref[...].astype(F32))
    pre_ref[...] = pre
    xhat, _ = centre(pre)
    normed = xhat * gain_ref[...] + bias_ref[...]
    normed_ref[...] = normed
    store_pieces(normed.astype(BF), low_refs)


def ln1(x, own, recv, gain, bias):
    shape = x.shape
    vm = pl.BlockSpec(memory_space=pltpu.VMEM)
    return pl.pallas_call(
        ln1_kernel,
        out_shape=[
            out(shape, F32),
            out(shape, F32),
            out(shape),
            *[out((shape[0] // PIECES, shape[1]))] * PIECES,
        ],
        in_specs=[vm] * 5,
        out_specs=[vm] * (3 + PIECES),
        compiler_params=params(12),
        cost_estimate=cost(x.size * 10, x.size * 18),
        name="norm_one",
    )(x, own, recv, gain, bias)


def ln2_kernel(
    normed_ref, keep_ref, near_ref, dy_ref, gain_ref, bias_ref, *refs
):
    out_ref, d_ref, grads_ref, *low_refs = refs[PIECES:]
    branch = keep_ref[...].astype(F32) + near_ref[...].astype(F32) + far_rows(refs[:PIECES])
    xhat, r = centre(normed_ref[...] + branch)
    gain = gain_ref[...]
    out_ref[...] = (xhat * gain + bias_ref[...]).astype(BF)
    dy = dy_ref[...].astype(F32)
    d = norm_back(xhat, r, gain, dy)
    d_ref[...] = d
    store_pieces(d.astype(BF), low_refs)
    grads_ref[0:1, :] = jnp.sum(dy * xhat, axis=0, keepdims=True)
    grads_ref[1:2, :] = jnp.sum(dy, axis=0, keepdims=True)


def ln2(normed, keep, near, far, dy, gain, bias):
    shape = normed.shape
    return pl.pallas_call(
        ln2_kernel,
        out_shape=[
            out(shape),
            out(shape, F32),
            out((2, shape[1]), F32),
            out(shape),
            *[out((shape[0] // PIECES, shape[1]))] * PIECES,
        ],
        in_specs=vmem(6 + PIECES),
        out_specs=vmem(4 + PIECES),
        compiler_params=params(16),
        cost_estimate=cost(normed.size * 20, normed.size * 20),
        name="norm_two",
    )(normed, keep, near, dy, gain, bias, *far)


def ln1_back_kernel(
    pre_ref, d2_ref, keep_ref, near_ref, gain_ref, grads_two_ref, *refs
):
    d_ref, low_ref, norms_ref = refs[PIECES:]
    grad = d2_ref[...] + (
        keep_ref[...].astype(F32) + near_ref[...].astype(F32) + far_rows(refs[:PIECES])
    )
    xhat, r = centre(pre_ref[...])
    d = norm_back(xhat, r, gain_ref[...], grad)
    d_ref[...] = d
    width = d.shape[1]
    low_ref[...] = d.astype(BF)
    norms_ref[...] = jnp.concatenate(
        [
            jnp.sum(grad * xhat, axis=0, keepdims=True),
            jnp.sum(grad, axis=0, keepdims=True),
            grads_two_ref[...],
            jnp.zeros((NORM_ROWS - 4, width), F32),
        ],
        axis=0,
    ).astype(BF)


def ln1_back(pre, d2, keep, near, far, gain, grads_two):
    shape = pre.shape
    return pl.pallas_call(
        ln1_back_kernel,
        out_shape=[out(shape, F32), out(shape), out((NORM_ROWS, shape[1]))],
        in_specs=vmem(6 + PIECES),
        out_specs=vmem(3),
        compiler_params=params(16),
        cost_estimate=cost(pre.size * 20, pre.size * 20),
        name="norm_one_backward",
    )(pre, d2, keep, near, gain, grads_two, *far)


def swap(value, axis, bit):
    count = lax.axis_size(axis)
    return lax.ppermute(value, axis, [(i, i ^ bit) for i in range(count)])


def swap_chip_edges(value):
    count = lax.axis_size("seq") * lax.axis_size("tp")
    pairs = []
    for i in range(1, count - 1, 2):
        pairs += [(i, i + 1), (i + 1, i)]
    return lax.ppermute(value, ("seq", "tp"), pairs)


def fold_kernel(dims, place_ref, own_ref, recv_ref, keep_ref, send_ref):
    rows, half = recv_ref.shape[0], keep_ref.shape[0]
    base = place_ref[dims[0]] * rows
    cut = place_ref[dims[1]] * half
    for ref, at in ((keep_ref, cut), (send_ref, half - cut)):
        own = own_ref[pl.ds(pl.multiple_of(base + at, NORM_ROWS), half), :].astype(F32)
        recv = recv_ref[pl.ds(pl.multiple_of(at, NORM_ROWS), half), :].astype(F32)
        ref[...] = (own + recv).astype(BF)


def fold(place, dims, own, recv):
    rows, width = recv.shape
    vm = pl.BlockSpec(memory_space=pltpu.VMEM)
    return pl.pallas_call(
        functools.partial(fold_kernel, dims),
        out_shape=[jax.ShapeDtypeStruct((rows // 2, width), BF)] * 2,
        in_specs=[smem(), vm, vm],
        out_specs=[vm] * 2,
        compiler_params=params(10),
        cost_estimate=cost(recv.size, recv.size * 6),
        name="fold_half",
    )(place, own, recv)


def join_kernel(dim, place_ref, own_ref, recv_ref, out_ref):
    first = place_ref[dim] == 0
    half = own_ref.shape[0]
    own, recv = own_ref[...], recv_ref[...]
    out_ref[0:half, :] = jnp.where(first, own, recv).astype(out_ref.dtype)
    out_ref[half:, :] = jnp.where(first, recv, own).astype(out_ref.dtype)


def join(place, dim, own, recv, kind=BF):
    half, width = own.shape
    vm = pl.BlockSpec(memory_space=pltpu.VMEM)
    return pl.pallas_call(
        functools.partial(join_kernel, dim),
        out_shape=jax.ShapeDtypeStruct((2 * half, width), kind),
        in_specs=[smem(), vm, vm],
        out_specs=vm,
        compiler_params=params(10),
        cost_estimate=cost(0, own.size * 12),
        name="join_halves",
    )(place, own, recv)


def finish_in_kernel(dims, place_ref, g_ref, g_recv_ref, u_ref, u_recv_ref, out_ref):
    half = g_ref.shape[0]
    for i, (own_ref, recv_ref) in enumerate(((g_ref, g_recv_ref), (u_ref, u_recv_ref))):
        first = place_ref[dims[i]] == 0
        own, recv = own_ref[...], recv_ref[...]
        out_ref[0:half, i, :] = jnp.where(first, own, recv).astype(F32)
        out_ref[half:, i, :] = jnp.where(first, recv, own).astype(F32)


def finish_in(place, gate, up):
    half, width = gate[1].shape
    return pl.pallas_call(
        functools.partial(finish_in_kernel, (gate[0], up[0])),
        out_shape=out((2 * half, 2, width), F32),
        in_specs=[smem()] + vmem(4),
        out_specs=vmem(1)[0],
        compiler_params=params(16),
        cost_estimate=cost(0, gate[1].size * 24),
        name="finish_w_in_gradient",
    )(place, *gate[1:], *up[1:])


def finish_rest_kernel(
    dims, place_ref, a_ref, a_recv_ref, b_ref, b_recv_ref, qkv_ref, out_ref, norm_ref
):
    first = place_ref[dims[0]] == 0
    half = a_ref.shape[0]
    own, recv = a_ref[...], a_recv_ref[...]
    qkv_ref[0:half, :] = jnp.where(first, own, recv).astype(F32)
    qkv_ref[half : 2 * half, :] = jnp.where(first, recv, own).astype(F32)
    first = place_ref[dims[1]] == 0
    own, recv = b_ref[...], b_recv_ref[...]
    step = own.shape[0] // 2
    count = step - NORM_ROWS
    low = jnp.where(first, own, recv).astype(F32)
    high = jnp.where(first, recv, own).astype(F32)
    for ref, start, rows in ((qkv_ref, 2 * half, low), (out_ref, 0, high)):
        ref[start : start + count, :] = rows[0:count]
        ref[start + count : start + 2 * count, :] = rows[step : step + count]
    norm_ref[...] = low[count : count + 4]


def finish_rest(place, a, b):
    width = a[1].shape[1]
    rest = b[1].shape[0] - 2 * NORM_ROWS
    return pl.pallas_call(
        functools.partial(finish_rest_kernel, (a[0], b[0])),
        out_shape=[
            out((2 * a[1].shape[0] + rest, width), F32),
            out((rest, width), F32),
            out((4, width), F32),
        ],
        in_specs=[smem()] + vmem(4),
        out_specs=vmem(3),
        compiler_params=params(12),
        cost_estimate=cost(0, a[1].size * 24),
        name="finish_attention_gradients",
    )(place, *a[1:], *b[1:])


def send_half(place_ref, dim, ref, sent_ref):
    count = sent_ref.shape[0]
    at = (1 - place_ref[dim]) * count
    sent_ref[...] = ref[pl.ds(pl.multiple_of(at, NORM_ROWS), count), :]


def cut_a_kernel(dim, place_ref, own_ref, far_ref, a_ref, sent_ref):
    half = a_ref.shape[0]
    total = own_ref[0:half, :].astype(F32) + far_ref[...].astype(F32)
    a_ref[...] = total.astype(BF)
    send_half(place_ref, dim, a_ref, sent_ref)


def cut_a(place, dim, own, far):
    rows, width = far.shape
    return pl.pallas_call(
        functools.partial(cut_a_kernel, dim),
        out_shape=[out((rows, width)), out((rows // 2, width))],
        in_specs=[smem()] + vmem(2),
        out_specs=vmem(2),
        compiler_params=params(12),
        cost_estimate=cost(far.size, far.size * 8),
        name="add_far_shard_a",
    )(place, own, far)


def cut_b_kernel(dim, place_ref, own_ref, far_ref, out_ref, b_ref, sent_ref):
    rows = far_ref.shape[0]
    start = own_ref.shape[0] - rows
    value = (own_ref[start:, :].astype(F32) + far_ref[...].astype(F32)).astype(BF)
    step = b_ref.shape[0] // 4
    count = step - NORM_ROWS
    for i in range(4):
        at = (i % 2) * count
        source = value if i < 2 else out_ref
        b_ref[i * step : i * step + count, :] = source[at : at + count, :]
        b_ref[i * step + count : (i + 1) * step, :] = out_ref[2 * count :, :]
    send_half(place_ref, dim, b_ref, sent_ref)


def cut_b(place, dim, own, far, out_rows):
    width = own.shape[1]
    rows = far.shape[0] + out_rows.shape[0] + 3 * NORM_ROWS
    return pl.pallas_call(
        functools.partial(cut_b_kernel, dim),
        out_shape=[out((rows, width)), out((rows // 2, width))],
        in_specs=[smem()] + vmem(3),
        out_specs=vmem(2),
        compiler_params=params(12),
        cost_estimate=cost(far.size, far.size * 8),
        name="add_far_shard_b",
    )(place, own, far, out_rows)


def out_grad_kernel(ctx_ref, datt_ref, own_ref, far_ref, out_ref):
    count = ctx_ref.shape[0]
    near = dot(ctx_ref[...], datt_ref[...], 1, 0)
    out_ref[0:count, :] = (near + far_ref[0:count, :].astype(F32)).astype(BF)
    norms = own_ref[count:, :].astype(F32) + far_ref[count:, :].astype(F32)
    out_ref[count:, :] = norms.astype(BF)


def out_grad(ctx, datt, own, far):
    vm = pl.BlockSpec(memory_space=pltpu.VMEM)
    return pl.pallas_call(
        out_grad_kernel,
        out_shape=jax.ShapeDtypeStruct(far.shape, BF),
        in_specs=[vm] * 4,
        out_specs=vm,
        compiler_params=params(12),
        cost_estimate=cost(2 * ctx.size * datt.shape[1], datt.size * 2),
        name="out_gradient",
    )(ctx, datt, own, far)


class SeqSum:
    def __init__(self, place, order, dims, g, sent=None, last=None):
        self.place, self.order, self.dims, self.value = place, order, dims, g
        self.last = last
        self.stage = 1
        self.pairwise = lax.axis_size("seq") == 8
        if not self.pairwise:
            whole = lax.psum(g, "seq")
            half = g.shape[0] // 2
            self.dims = (len(dims),)
            self.value, self.moving = whole[:half], whole[half:]
            return
        if sent is None:
            half = g.shape[0] // 2
            sent = lax.dynamic_slice_in_dim(g, (1 - place[dims[0]]) * half, half, 0)
        self.send(0, sent)

    def send(self, dim, value):
        self.moving = swap(value, "seq", 1 << self.dims[dim])

    def step(self):
        stage, place, order, dims = self.stage, self.place, self.order, self.dims
        self.stage += 1
        if not self.pairwise and stage < 5:
            return
        value, moved = self.value, self.moving
        if stage < 5 or self.last is not None:
            value = order(value)
        if stage == 1:
            self.value, sent = fold(place, dims[:2], value, moved)
            order.note(sent)
            self.send(1, sent)
        elif stage in (2, 3):
            self.value = order.note(add(value, moved))
            self.send(2 if stage == 2 else 1, self.value)
        elif stage == 4:
            self.value = order.note(join(place, dims[1], value, moved))
            self.send(0, self.value)
        elif stage == 5:
            if self.last is None:
                self.result = (dims[0], self.value, moved)
                return
            self.result = self.last(place, dims[0], value, moved)
            order.note(jax.tree.leaves(self.result)[-1])


def add_kernel(a_ref, b_ref, out_ref):
    out_ref[...] = (a_ref[...].astype(F32) + b_ref[...].astype(F32)).astype(BF)


def add(a, b):
    return pl.pallas_call(
        add_kernel,
        out_shape=out(a.shape),
        in_specs=vmem(2),
        out_specs=vmem(1)[0],
        compiler_params=params(10),
        cost_estimate=cost(a.size, a.size * 6),
        name="add_pair",
    )(a, b)


def input_grad_kernel(place_ref, *refs):
    (*heads, wt_ref, wt_far_ref, own_ref, sent_ref, near_ref, far_ref) = refs
    stack_heads(heads[: len(heads) // 2], near_ref)
    stack_heads(heads[len(heads) // 2 :], far_ref)
    half = own_ref.shape[0]
    for ref, which in ((sent_ref, 1 - place_ref[4]), (own_ref, place_ref[4])):
        here = pl.ds(pl.multiple_of(which * half, 128), half)
        total = dot(near_ref[:, here], wt_ref[...], 0, 0)
        ref[...] = (total + dot(far_ref[:, here], wt_far_ref[...], 0, 0)).astype(ref.dtype)


def input_grad(place, near, far, wt, wt_far):
    count = near[0].shape[2]
    half, (size, width) = count // 2, wt.shape
    vm = pl.BlockSpec(memory_space=pltpu.VMEM)
    return pl.pallas_call(
        input_grad_kernel,
        out_shape=[
            jax.ShapeDtypeStruct((half, width), F32),
            jax.ShapeDtypeStruct((half, width), BF),
        ],
        in_specs=[smem()] + [vm] * (2 * len(near) + 2),
        out_specs=[vm] * 2,
        scratch_shapes=[pltpu.VMEM((size, count), BF)] * 2,
        compiler_params=params(16),
        cost_estimate=cost(4 * size * count * width, 12 * half * width),
        name="input_gradient",
    )(place, *near, *far, wt, wt_far)


def input_rows_kernel(place_ref, own_ref, recv_ref, pre_ref, out_ref, edge_ref):
    count, edge = out_ref.shape[0], edge_ref.shape[0]
    core = place_ref[4]
    at = pl.ds(pl.multiple_of(core * count, edge), edge)
    edge_ref[...] = (own_ref[at, :] + recv_ref[at, :].astype(F32)).astype(BF)
    at = pl.ds(pl.multiple_of((1 - core) * edge, edge), count)
    out_ref[...] = pre_ref[...] + (own_ref[at, :] + recv_ref[at, :].astype(F32))


def input_rows(place, own, recv, pre):
    vm = pl.BlockSpec(memory_space=pltpu.VMEM)
    return pl.pallas_call(
        input_rows_kernel,
        out_shape=[
            jax.ShapeDtypeStruct(pre.shape, F32),
            jax.ShapeDtypeStruct((QB, pre.shape[1]), BF),
        ],
        in_specs=[smem()] + [vm] * 3,
        out_specs=[vm] * 2,
        compiler_params=params(16),
        cost_estimate=cost(pre.size * 2, pre.size * 16),
        name="input_gradient_rows",
    )(place, own, recv, pre)


def input_edge_kernel(place_ref, rows_ref, edge_ref, out_ref):
    out_ref[...] = rows_ref[...]
    edge = edge_ref.shape[0]
    start = place_ref[4] * (rows_ref.shape[0] - edge)
    at = pl.ds(pl.multiple_of(start, edge), edge)
    out_ref[at, :] = rows_ref[at, :] + edge_ref[...].astype(F32)


def input_edge(place, rows, edge):
    vm = pl.BlockSpec(memory_space=pltpu.VMEM)
    return pl.pallas_call(
        input_edge_kernel,
        out_shape=jax.ShapeDtypeStruct(rows.shape, F32),
        in_specs=[smem()] + [vm] * 2,
        out_specs=vm,
        compiler_params=params(12),
        cost_estimate=cost(rows.size, rows.size * 10),
        name="input_gradient_edge",
    )(place, rows, edge)


def per_device(
    inputs, lengths, w_qkv, w_out, w_in, w_down, ln1_gain, ln1_bias, ln2_gain, ln2_bias, cotangent
):
    own_rows, width = inputs.shape
    tp_count = lax.axis_size("tp")
    head_width = w_qkv.shape[2]
    heads = head_width // HD
    chip_rows = 2 * own_rows
    tp = lax.axis_index("tp")
    seq = lax.axis_index("seq")
    core = tp & 1
    even = core == 0
    first = (seq * tp_count + 2 * (tp >> 1)) * own_rows
    place = jnp.stack([seq & 1, (seq >> 1) & 1, (seq >> 2) & 1, 0 * core, core]).astype(jnp.int32)

    bounds = jnp.cumsum(lengths)[:, None]
    tokens = (first + jnp.arange(chip_rows, dtype=jnp.int32))[None, :]
    before = bounds <= tokens
    start = jnp.max(jnp.where(before, bounds, 0), axis=0)
    end = jnp.min(jnp.where(before, jnp.iinfo(jnp.int32).max, bounds), axis=0)
    se = jnp.stack([start, end]) - (first - QB)
    se = jnp.pad(se, ((0, 6), (0, 0)))
    table = jnp.asarray(slope_table(HEADS))
    slopes = lax.dynamic_slice_in_dim(table, tp * heads, heads)
    slopes_far = lax.dynamic_slice_in_dim(table, (tp ^ 2) * heads, heads)

    wt = w_qkv.transpose(0, 2, 1).reshape(3 * head_width, width)
    wt_far = swap(wt, "tp", 2)

    sibling = swap(inputs, "tp", 1)
    edge = swap_chip_edges(
        lax.dynamic_slice_in_dim(inputs, core * (own_rows - QB), QB, axis=0)
    )
    edge_sibling = swap(edge, "tp", 1)
    rows, ctx, qkv, kv = attn_near(
        heads, place, slopes, se, inputs, sibling, edge, edge_sibling,
        wt.reshape(3, head_width, width),
    )
    w_out_far = swap(after(w_out, ctx), "tp", 2)
    near_sums = attended_halves(place, ctx, w_out)
    ctx_far, qkv_far, kv_far = attn_far(
        heads, slopes_far, se, rows, wt_far.reshape(3, head_width, width)
    )
    attended, attended_sent = attended_halves(place, ctx_far, w_out_far, near_sums)
    attended_sent = swap(attended_sent, "tp", 1)
    gain1, bias1 = ln1_gain[None], ln1_bias[None]
    gain2, bias2 = ln2_gain[None], ln2_bias[None]
    pre_one, normed, low, *low_pieces = ln1(inputs, attended, attended_sent, gain1, bias1)

    order = Order()
    w_in_late = after(w_in, low)
    wg, wu = w_in_late[:, 0], w_in_late[:, 1]

    def both_ways(own, pieces, work, between=lambda near_out: None):
        far = [swap(piece, "tp", 2) for piece in pieces]
        near_out = work(0, own, order(swap(own, "tp", 1)))
        near_keep, near_send = near_out[-2:]
        order.note(near_send)
        recv = swap(near_send, "tp", 1)
        between(near_out)
        far = [order(rows) for rows in far]
        far_sibling = [swap(rows, "tp", 1) for rows in far]
        outs, sums = [near_out], []
        for rows, rows_sibling in zip(far, far_sibling):
            outs.append(work(len(outs), order(rows), rows_sibling))
            order.note(outs[-1][-1])
        from_sibling = [swap(o[-1], "tp", 1) for o in outs[1:]]
        for i, (o, theirs) in enumerate(zip(outs[1:], from_sibling)):
            total = order.note(add(order(o[-2]), theirs))
            sums.append(swap(total, "tp", 2))
        return outs, (near_keep, recv, sums)

    order.note(low)
    forward, parts = both_ways(
        low, low_pieces, lambda i, a, b: ff_fwd((a, b), wg, wu, w_down)
    )
    layer_out, d_pre_two, grads_two, d_branch, *d_branch_pieces = ln2(
        normed, order(parts[0]), *parts[1:], cotangent, gain2, bias2
    )
    order.note(d_branch)

    weight_near_parts = []

    def grads_between(near_out):
        for x, d in weight_pairs:
            part = weight_near(order(forward[0][x]), near_out[d])
            weight_near_parts.append(order.note(part))

    weight_pairs = ((1, 0), (0, 2), (0, 1))
    backward, parts = both_ways(
        d_branch,
        d_branch_pieces,
        lambda i, a, b: ff_bwd((a, b), forward[i][2], forward[i][3], w_down, wg, wu),
        grads_between,
    )

    def join_whole(*halves):
        return join(*halves, F32)

    def weight_sum(which, dims):
        x, d = weight_pairs[which]
        pairs = [t for f, b in zip(forward[1:], backward[1:]) for t in (f[x], b[d])]
        total, sent = weight_far(
            place, dims[0], order(weight_near_parts[which]), *pairs
        )
        order.note(sent)
        return SeqSum(place, order, dims, total, sent, None if which else join_whole)

    d_far, d_near = [], []

    def one_head(h, far):
        kept = (slopes_far, se, qkv_far, kv_far) if far else (slopes, se, qkv, kv)
        return order.note(head_back(h, *kept, order(d_ctx_far if far else d_ctx)))

    down = weight_sum(0, (0, 1, 2))
    up = weight_sum(1, (0, 1, 2))
    gate = weight_sum(2, (1, 0, 2))
    d_pre_one, half, norms = ln1_back(
        pre_one, d_pre_two, order(parts[0]), *parts[1:], gain1, grads_two
    )
    order.note(half)
    half_sibling = swap(half, "tp", 1)
    norms_sibling = swap(norms, "tp", 1)
    down.step()
    gate.step()
    d_attended, sent_out, d_ctx, d_ctx_far = gather_back(
        place, order(ctx_far), half, half_sibling, norms, norms_sibling, w_out, w_out_far
    )
    order.note(d_ctx_far)
    far_out = swap(sent_out, "tp", 2)
    d_far.append(one_head(0, True))
    down.step()
    d_far.append(one_head(1, True))
    up.step()
    d_far.append(one_head(2, True))
    grad_out = order.note(out_grad(ctx, order(d_attended), sent_out, far_out))
    gate.step()
    far_qk, far_v = qkv_grad(d_far, order(rows), (2, 1))
    order.note(far_v)
    far_v = swap(far_v, "tp", 2)
    far_qk = swap(far_qk, "tp", 2)
    d_near.append(one_head(0, False))
    down.step()
    d_near.append(one_head(1, False))
    up.step()
    d_near.append(one_head(2, False))
    (own_qkv,) = qkv_grad(d_near, order(rows))
    order.note(own_qkv)
    total, sent = cut_b(place, 0, order(own_qkv), far_v, grad_out)
    order.note(sent)
    attn_b = SeqSum(place, order, (0, 1, 2), total, sent)
    gate.step()
    down.step()
    attn_b.step()
    total, sent = cut_a(place, 1, order(own_qkv), far_qk)
    order.note(sent)
    attn_a = SeqSum(place, order, (1, 0, 2), total, sent)
    up.step()
    window_own, window_sent = input_grad(
        place, [order(d_near[0]), *d_near[1:]], d_far, wt, wt_far
    )
    order.note(window_sent)
    window_sent = swap(window_sent, "tp", 1)
    attn_b.step()
    attn_a.step()
    down.step()
    gate.step()
    attn_a.step()
    up.step()
    attn_b.step()
    attn_a.step()
    attn_b.step()
    attn_a.step()
    grad_rows, d_edge = input_rows(place, order(window_own), window_sent, d_pre_one)
    order.note(d_edge)
    d_edge = swap_chip_edges(d_edge)
    up.step()
    gate.step()
    grad_in = order.note(
        finish_in(order(place), gate.result, up.result)
    )
    grad_input = order.note(input_edge(place, order(grad_rows), d_edge))
    attn_b.step()
    attn_a.step()
    grad_qkv, grad_out, norm_grads = finish_rest(order(place), attn_a.result, attn_b.result)
    order.note(norm_grads)
    assert all(unit.stage == 6 for unit in (down, gate, up, attn_a, attn_b))
    grad_down = down.result
    grad_qkv = grad_qkv.reshape(3, head_width, width).transpose(0, 2, 1)
    return (
        layer_out,
        grad_input,
        grad_qkv,
        grad_out,
        grad_in,
        grad_down,
        norm_grads[0],
        norm_grads[1],
        norm_grads[2],
        norm_grads[3],
    )


def solution(mesh):
    in_specs = (
        P(("seq", "tp"), None),
        P(),
        P(None, None, "tp"),
        P("tp", None),
        P(None, None, "tp"),
        P("tp", None),
        P(),
        P(),
        P(),
        P(),
        P(("seq", "tp"), None),
    )
    out_specs = (
        P(("seq", "tp"), None),
        P(("seq", "tp"), None),
        P(None, None, "tp"),
        P("tp", None),
        P(None, None, "tp"),
        P("tp", None),
        P(),
        P(),
        P(),
        P(),
    )
    return jax.shard_map(
        per_device, mesh=mesh, in_specs=in_specs, out_specs=out_specs, check_vma=False
    )
```

```python
import functools
import math

import jax
import jax.numpy as jnp
import numpy as np
from jax import lax
from jax.experimental import pallas as pl
from jax.experimental.pallas import tpu as pltpu
from jax.sharding import PartitionSpec as P

HEADS = 12
HD = 64
PIECES = 2
NORM_ROWS = 16
QB = 128
WINDOW = 3 * QB
EPSILON = 1e-12
FAR = 1e30

BF = jnp.bfloat16
F32 = jnp.float32


def dot(a, b, ca, cb):
    return lax.dot_general(a, b, (((ca,), (cb,)), ((), ())), preferred_element_type=F32)


def slope_table(count):
    power_two = 2 ** int(math.floor(math.log2(count)))
    leading = [2.0 ** (-8.0 * (head + 1) / power_two) for head in range(power_two)]
    trailing = [2.0 ** (-4.0 * (2 * other + 1) / power_two) for other in range(count - power_two)]
    return np.array(leading + trailing, np.float32)


def smem():
    return pl.BlockSpec(memory_space=pltpu.SMEM)


def full(shape):
    return pl.BlockSpec(shape, lambda *_: (0,) * len(shape))


def cost(flops, moved, transcendentals=0):
    return pl.CostEstimate(
        flops=flops // 1000,
        bytes_accessed=moved // 1000,
        transcendentals=transcendentals // 1000,
    )


def params(mib):
    return pltpu.CompilerParams(vmem_limit_bytes=mib * 1024 * 1024)


def out(shape, kind=BF):
    return jax.ShapeDtypeStruct(shape, kind)


def vmem(count):
    return [pl.BlockSpec(memory_space=pltpu.VMEM)] * count


def after(value, *others):
    return lax.optimization_barrier((value, others))[0]


class Order:
    def __init__(self):
        self.last = ()

    def __call__(self, value):
        return after(value, *self.last)

    def note(self, value):
        self.last = (value,)
        return value


def block_distance(se_ref, off):
    start = se_ref[0:1, pl.ds(off, QB)] - off
    end = se_ref[1:2, pl.ds(off, QB)] - off
    key = lax.broadcasted_iota(jnp.int32, (WINDOW, QB), 0)
    query = lax.broadcasted_iota(jnp.int32, (WINDOW, QB), 1) + QB
    valid = (key >= start) & (key < end)
    return jnp.where(valid, jnp.abs(key - query).astype(F32), FAR)


def softmax(scores):
    shifted = jnp.exp(scores - jnp.max(scores, axis=0, keepdims=True))
    return shifted * (1.0 / jnp.sum(shifted, axis=0, keepdims=True))


def attend(heads, slopes_ref, se_ref, rows_ref, wt_ref, ctx_ref, qkv_ref, kv_ref):
    zero = jnp.zeros((HD, QB), BF)
    starts = range(0, ctx_ref.shape[1], QB)
    weights = wt_ref[...].reshape(3 * heads * HD, wt_ref.shape[2])
    pairs = jnp.concatenate(
        [wt_ref[part, h * HD : (h + 1) * HD, :] for h in range(heads) for part in (1, 2)], axis=0
    )
    for c in range(0, rows_ref.shape[0], 256):
        rows = rows_ref[c : c + 256, :]
        turned = dot(weights, rows, 1, 1).astype(BF)
        qkv_ref[:, :, c : c + 256] = turned.reshape(3, heads * HD, 256)
        kv_ref[c : c + 256, :] = dot(rows, pairs, 1, 1).astype(BF)
    for h in range(heads):
        mine = slice(h * HD, (h + 1) * HD)
        pair = slice(h * 2 * HD, (h + 1) * 2 * HD)
        scores = []
        for off in starts:
            query = qkv_ref[0, mine, off + QB : off + 2 * QB] * BF(0.125)
            key = kv_ref[off : off + WINDOW, pair]
            scores.append(dot(key, jnp.concatenate([query, zero], axis=0), 1, 0))
        probs = [
            softmax(x - slopes_ref[h] * block_distance(se_ref, off)).astype(BF)
            for off, x in zip(starts, scores)
        ]
        for off, x in zip(starts, probs):
            value = qkv_ref[2, mine, off : off + WINDOW]
            ctx_ref[mine, off : off + QB] = dot(value, x, 1, 0).astype(BF)


def attn_near_kernel(
    heads, place_ref, slopes_ref, se_ref, own_ref, sib_ref, edge_ref, edge_sib_ref, wt_ref,
    rows_ref, ctx_ref, qkv_ref, kv_ref,
):
    even = place_ref[4] == 0
    count = own_ref.shape[0]
    own, sib, edge, edge_sib = (r[...] for r in (own_ref, sib_ref, edge_ref, edge_sib_ref))
    rows_ref[0:QB, :] = jnp.where(even, edge, edge_sib)
    rows_ref[QB : QB + count, :] = jnp.where(even, own, sib)
    rows_ref[QB + count : QB + 2 * count, :] = jnp.where(even, sib, own)
    rows_ref[QB + 2 * count :, :] = jnp.where(even, edge_sib, edge)
    attend(heads, slopes_ref, se_ref, rows_ref, wt_ref, ctx_ref, qkv_ref, kv_ref)


def attended_kernel(place_ref, ctx_ref, w_ref, *refs):
    (*sums, own_ref, sent_ref) = refs
    count = own_ref.shape[0]
    for i, (ref, which) in enumerate(((own_ref, place_ref[4]), (sent_ref, 1 - place_ref[4]))):
        here = pl.ds(pl.multiple_of(which * count, 128), count)
        total = dot(ctx_ref[:, here], w_ref[...], 0, 0)
        if sums:
            total = sums[i][...] + total
        ref[...] = total.astype(ref.dtype)


def attn_fwd_outs(heads, here, count):
    return [
        out((heads * HD, here)),
        out((3, heads * HD, count)),
        out((count, heads * 2 * HD)),
    ]


def attn_cost(heads, here, count, width):
    elements = heads * here * WINDOW
    flops = elements * HD * 8 + 10 * heads * HD * count * width
    return cost(flops, count * width * 8, elements)


def attn_near(heads, place, slopes, se, own, sib, edge, edge_sib, wt):
    here, width = se.shape[1], own.shape[1]
    count = here + 2 * QB
    return pl.pallas_call(
        functools.partial(attn_near_kernel, heads),
        out_shape=[out((count, width))] + attn_fwd_outs(heads, here, count),
        in_specs=[smem(), smem()] + vmem(6),
        out_specs=vmem(4),
        compiler_params=params(16),
        cost_estimate=attn_cost(heads, here, count, width),
        name="attention_forward_near",
    )(place, slopes, se, own, sib, edge, edge_sib, wt)


def attn_far(heads, slopes, se, rows, wt):
    here, (count, width) = se.shape[1], rows.shape
    return pl.pallas_call(
        functools.partial(attend, heads),
        out_shape=attn_fwd_outs(heads, here, count),
        in_specs=[smem()] + vmem(3),
        out_specs=vmem(3),
        compiler_params=params(16),
        cost_estimate=attn_cost(heads, here, count, width),
        name="attention_forward_far",
    )(slopes, se, rows, wt)


def attended_halves(place, ctx, w, sums=()):
    half, width = ctx.shape[1] // 2, w.shape[1]
    return pl.pallas_call(
        attended_kernel,
        out_shape=[out((half, width), F32), out((half, width), BF if sums else F32)],
        in_specs=[smem()] + vmem(2 + len(sums)),
        out_specs=vmem(2),
        compiler_params=params(12),
        cost_estimate=cost(4 * ctx.size * width, 12 * half * width),
        name="attended_halves",
    )(place, ctx, w, *sums)


def head_back_kernel(head, slopes_ref, se_ref, qkv_ref, kv_ref, dctx_ref, out_ref, acc_ref):
    here = dctx_ref.shape[1]
    mine = slice(head * HD, (head + 1) * HD)
    keys = slice(head * 2 * HD, (head + 1) * 2 * HD)
    acc_ref[...] = jnp.zeros_like(acc_ref)
    edge = jnp.zeros((HD, QB), BF)
    out_ref[0, :, 0:QB] = edge
    out_ref[0, :, QB + here :] = edge
    slope = slopes_ref[head]
    starts = range(0, here, QB)
    pairs = []
    for off in starts:
        query = qkv_ref[0, mine, off + QB : off + 2 * QB] * BF(0.125)
        d_rows = dctx_ref[mine, off : off + QB]
        pairs.append(
            jnp.concatenate(
                [
                    jnp.concatenate([query, edge], axis=1),
                    jnp.concatenate([edge, d_rows], axis=1),
                ],
                axis=0,
            )
        )
    both = [dot(kv_ref[off : off + WINDOW, keys], pair, 1, 0) for off, pair in zip(starts, pairs)]
    probs = [
        softmax(x[:, :QB] - slope * block_distance(se_ref, off)) for off, x in zip(starts, both)
    ]
    row_dots = [jnp.sum(x[:, QB:] * p, axis=0, keepdims=True) for x, p in zip(both, probs)]
    d_scores = [
        (p * (x[:, QB:] - row_dot)).astype(BF) for x, p, row_dot in zip(both, probs, row_dots)
    ]
    probs = [p.astype(BF) for p in probs]
    for off, d in zip(starts, d_scores):
        d_query = dot(qkv_ref[1, mine, off : off + WINDOW], d, 1, 0) * 0.125
        out_ref[0, :, off + QB : off + 2 * QB] = d_query.astype(BF)
    sums = [
        dot(pair, jnp.concatenate([d, p], axis=1), 1, 1)
        for pair, d, p in zip(pairs, d_scores, probs)
    ]
    for off, x in zip(starts, sums):
        acc_ref[:, off : off + WINDOW] += x
    out_ref[1, :, :] = acc_ref[0:HD, :].astype(BF)
    out_ref[2, :, :] = acc_ref[HD:, :].astype(BF)


def head_back(head, slopes, se, qkv, kv, dctx):
    here, count = se.shape[1], qkv.shape[2]
    elements = here * WINDOW
    return pl.pallas_call(
        functools.partial(head_back_kernel, head),
        out_shape=out((3, HD, count)),
        in_specs=[smem()] + vmem(4),
        out_specs=vmem(1)[0],
        scratch_shapes=[pltpu.VMEM((2 * HD, count), F32)],
        compiler_params=params(12),
        cost_estimate=cost(elements * HD * 24, count * HD * 18, elements),
        name="attention_backward_head",
    )(slopes, se, qkv, kv, dctx)


def stack_heads(refs, all_ref):
    heads = len(refs)
    for h, ref in enumerate(refs):
        for part in range(3):
            at = (part * heads + h) * HD
            all_ref[at : at + HD, :] = ref[part]


def qkv_grad_kernel(heads, *refs):
    (rows_ref, *out_refs, all_ref) = refs[heads:]
    stack_heads(refs[:heads], all_ref)
    for c in range(0, rows_ref.shape[1], 256):
        total = dot(all_ref[...], rows_ref[:, c : c + 256], 1, 0).astype(BF)
        at = 0
        for ref in out_refs:
            ref[:, c : c + 256] = total[at : at + ref.shape[0]]
            at += ref.shape[0]


def qkv_grad(heads, rows, parts=(3,)):
    count, width = rows.shape
    size = len(heads) * HD
    return pl.pallas_call(
        functools.partial(qkv_grad_kernel, len(heads)),
        out_shape=[out((part * size, width)) for part in parts],
        in_specs=vmem(len(heads) + 1),
        out_specs=vmem(len(parts)),
        scratch_shapes=[pltpu.VMEM((3 * size, count), BF)],
        compiler_params=params(12),
        cost_estimate=cost(6 * size * count * width, count * width * 4),
        name="projection_gradient",
    )(*heads, rows)


def gather_back_kernel(
    place_ref, ctx_ref, own_ref, sib_ref, norms_ref, norms_sib_ref, w_out_ref, w_far_ref,
    datt_ref, grad_ref, dctx_ref, dctx_far_ref,
):
    even = place_ref[4] == 0
    half = datt_ref.shape[0] // 2
    own, sib = own_ref[...], sib_ref[...]
    datt_ref[0:half, :] = jnp.where(even, own, sib)
    datt_ref[half:, :] = jnp.where(even, sib, own)
    for c in range(0, 2 * half, 256):
        rows = datt_ref[c : c + 256, :]
        dctx_far_ref[:, c : c + 256] = dot(w_far_ref[...], rows, 1, 1).astype(BF)
        dctx_ref[:, c : c + 256] = dot(w_out_ref[...], rows, 1, 1).astype(BF)
    count = ctx_ref.shape[0]
    grad_ref[0:count, :] = dot(ctx_ref[...], datt_ref[...], 1, 0).astype(BF)
    norms = norms_ref[...].astype(F32) + norms_sib_ref[...].astype(F32)
    grad_ref[count:, :] = norms.astype(BF)


def gather_back(place, ctx, own, sib, norms, norms_sib, w_out, w_far):
    half, width = own.shape
    vm = pl.BlockSpec(memory_space=pltpu.VMEM)
    return pl.pallas_call(
        gather_back_kernel,
        out_shape=[
            out((2 * half, width)),
            jax.ShapeDtypeStruct((ctx.shape[0] + NORM_ROWS, width), BF),
            jax.ShapeDtypeStruct(ctx.shape, BF),
            jax.ShapeDtypeStruct(ctx.shape, BF),
        ],
        in_specs=[smem()] + [vm] * 7,
        out_specs=[vm] * 4,
        compiler_params=params(16),
        cost_estimate=cost(6 * ctx.size * width, 12 * half * width),
        name="gather_d_attended",
    )(place, ctx, own, sib, norms, norms_sib, w_out, w_far)


def phi_pair(gate):
    bell = jnp.exp(gate * gate * -0.5)
    t = 1.0 / (1.0 + (0.3275911 / math.sqrt(2.0)) * jnp.abs(gate))
    poly = t * (
        0.254829592
        + t * (-0.284496736 + t * (1.421413741 + t * (-1.453152027 + t * 1.061405429)))
    )
    tail = 0.5 * poly * bell
    return jnp.where(gate >= 0.0, 1.0 - tail, tail), bell * (1.0 / math.sqrt(2.0 * math.pi))


def ff_fwd_kernel(
    x0_ref, x1_ref, wg_ref, wu_ref, wd_ref, x_ref, act_ref, a_ref, b_ref, keep_ref, send_ref
):
    half = x0_ref.shape[0]
    for i, (source, target) in enumerate(((x0_ref, keep_ref), (x1_ref, send_ref))):
        rows = slice(i * half, (i + 1) * half)
        x = source[...]
        x_ref[rows, :] = x
        for f in range(0, wd_ref.shape[0], 256):
            cols = slice(f, f + 256)
            gate = dot(x, wg_ref[:, cols], 1, 0)
            up = dot(x, wu_ref[:, cols], 1, 0)
            big, small = phi_pair(gate)
            gelu = gate * big
            act_ref[rows, cols] = (gelu * up).astype(BF)
            a_ref[rows, cols] = gelu.astype(BF)
            b_ref[rows, cols] = (up * (big + gate * small)).astype(BF)
        target[...] = dot(act_ref[rows, :], wd_ref[...], 1, 0).astype(BF)


def ff_fwd(pieces, wg, wu, wd):
    half, width = pieces[0].shape
    hidden = wd.shape[0]
    rows = 2 * half
    return pl.pallas_call(
        ff_fwd_kernel,
        out_shape=[out((rows, width))] + [out((rows, hidden))] * 3 + [out((half, width))] * 2,
        in_specs=vmem(5),
        out_specs=vmem(6),
        compiler_params=params(16),
        cost_estimate=cost(rows * width * hidden * 6, 12 * rows * width, 2 * rows * hidden),
        name="ff_forward",
    )(*pieces, wg, wu, wd)


def ff_bwd_kernel(
    d0_ref, d1_ref, a_ref, b_ref, wd_ref, wg_ref, wu_ref,
    db_ref, dg_ref, du_ref, keep_ref, send_ref,
):
    half = d0_ref.shape[0]
    for i, (source, target) in enumerate(((d0_ref, keep_ref), (d1_ref, send_ref))):
        rows = slice(i * half, (i + 1) * half)
        db = source[...]
        db_ref[rows, :] = db
        for f in range(0, wd_ref.shape[0], 256):
            cols = slice(f, f + 256)
            d_active = dot(db, wd_ref[cols, :], 1, 1)
            dg_ref[rows, cols] = (d_active * b_ref[rows, cols].astype(F32)).astype(BF)
            du_ref[rows, cols] = (d_active * a_ref[rows, cols].astype(F32)).astype(BF)
        part = dot(dg_ref[rows, :], wg_ref[...], 1, 1) + dot(du_ref[rows, :], wu_ref[...], 1, 1)
        target[...] = part.astype(BF)


def ff_bwd(pieces, a, b, wd, wg, wu):
    half, width = pieces[0].shape
    hidden = wd.shape[0]
    rows = 2 * half
    return pl.pallas_call(
        ff_bwd_kernel,
        out_shape=[out((rows, width))] + [out((rows, hidden))] * 2 + [out((half, width))] * 2,
        in_specs=vmem(7),
        out_specs=vmem(5),
        compiler_params=params(16),
        cost_estimate=cost(rows * width * hidden * 6, 12 * rows * width),
        name="ff_backward",
    )(*pieces, a, b, wd, wg, wu)


def weight_near_kernel(a_ref, d_ref, out_ref):
    out_ref[...] = dot(a_ref[...], d_ref[...], 0, 0)


def weight_near(a, d):
    size = (a.shape[1], d.shape[1])
    return pl.pallas_call(
        weight_near_kernel,
        out_shape=out(size, F32),
        in_specs=vmem(2),
        out_specs=vmem(1)[0],
        compiler_params=params(16),
        cost_estimate=cost(2 * a.size * d.shape[1], a.size * 8),
        name="weight_gradient_near",
    )(a, d)


def weight_far_kernel(dim, place_ref, acc_ref, *refs):
    pairs, (out_ref, sent_ref) = refs[:-2], refs[-2:]
    a = jnp.concatenate([ref[...] for ref in pairs[0::2]], axis=0)
    d = jnp.concatenate([ref[...] for ref in pairs[1::2]], axis=0)
    out_ref[...] = (acc_ref[...] + dot(a, d, 0, 0)).astype(BF)
    half = sent_ref.shape[0]
    at = (1 - place_ref[dim]) * half
    sent_ref[...] = out_ref[pl.ds(pl.multiple_of(at, half), half), :]


def weight_far(place, dim, acc, *pairs):
    rows, width = acc.shape
    return pl.pallas_call(
        functools.partial(weight_far_kernel, dim),
        out_shape=[out((rows, width)), out((rows // 2, width))],
        in_specs=[smem()] + vmem(1 + len(pairs)),
        out_specs=vmem(2),
        compiler_params=params(16),
        cost_estimate=cost(2 * acc.size * rows, acc.size * 12),
        name="weight_gradient_far",
    )(place, acc, *pairs)


def centre(pre):
    mean = jnp.mean(pre, axis=-1, keepdims=True)
    centred = pre - mean
    r = lax.rsqrt(jnp.mean(centred * centred, axis=-1, keepdims=True) + EPSILON)
    return centred * r, r


def norm_back(xhat, r, gain, grad):
    e = grad * gain
    return r * (
        e
        - jnp.mean(e, axis=-1, keepdims=True)
        - xhat * jnp.mean(e * xhat, axis=-1, keepdims=True)
    )


def store_pieces(value, refs):
    refs[0][...] = value
    at = 0
    for ref in refs[1:]:
        ref[...] = value[at : at + ref.shape[0]]
        at += ref.shape[0]


def far_rows(refs):
    return jnp.concatenate([ref[...].astype(F32) for ref in refs], axis=0)


def ln1_kernel(
    x_ref, own_ref, recv_ref, gain_ref, bias_ref, pre_ref, normed_ref, *low_refs
):
    pre = x_ref[...].astype(F32) + (own_ref[...] + recv_ref[...].astype(F32))
    pre_ref[...] = pre
    xhat, _ = centre(pre)
    normed = xhat * gain_ref[...] + bias_ref[...]
    normed_ref[...] = normed
    store_pieces(normed.astype(BF), low_refs)


def ln1(x, own, recv, gain, bias):
    shape = x.shape
    vm = pl.BlockSpec(memory_space=pltpu.VMEM)
    return pl.pallas_call(
        ln1_kernel,
        out_shape=[
            out(shape, F32),
            out(shape, F32),
            out(shape),
            *[out((shape[0] // PIECES, shape[1]))] * PIECES,
        ],
        in_specs=[vm] * 5,
        out_specs=[vm] * (3 + PIECES),
        compiler_params=params(12),
        cost_estimate=cost(x.size * 10, x.size * 18),
        name="norm_one",
    )(x, own, recv, gain, bias)


def ln2_kernel(
    normed_ref, keep_ref, near_ref, dy_ref, gain_ref, bias_ref, *refs
):
    out_ref, d_ref, grads_ref, *low_refs = refs[PIECES:]
    branch = keep_ref[...].astype(F32) + near_ref[...].astype(F32) + far_rows(refs[:PIECES])
    xhat, r = centre(normed_ref[...] + branch)
    gain = gain_ref[...]
    out_ref[...] = (xhat * gain + bias_ref[...]).astype(BF)
    dy = dy_ref[...].astype(F32)
    d = norm_back(xhat, r, gain, dy)
    d_ref[...] = d
    store_pieces(d.astype(BF), low_refs)
    grads_ref[0:1, :] = jnp.sum(dy * xhat, axis=0, keepdims=True)
    grads_ref[1:2, :] = jnp.sum(dy, axis=0, keepdims=True)


def ln2(normed, keep, near, far, dy, gain, bias):
    shape = normed.shape
    return pl.pallas_call(
        ln2_kernel,
        out_shape=[
            out(shape),
            out(shape, F32),
            out((2, shape[1]), F32),
            out(shape),
            *[out((shape[0] // PIECES, shape[1]))] * PIECES,
        ],
        in_specs=vmem(6 + PIECES),
        out_specs=vmem(4 + PIECES),
        compiler_params=params(16),
        cost_estimate=cost(normed.size * 20, normed.size * 20),
        name="norm_two",
    )(normed, keep, near, dy, gain, bias, *far)


def ln1_back_kernel(
    pre_ref, d2_ref, keep_ref, near_ref, gain_ref, grads_two_ref, *refs
):
    d_ref, low_ref, norms_ref = refs[PIECES:]
    grad = d2_ref[...] + (
        keep_ref[...].astype(F32) + near_ref[...].astype(F32) + far_rows(refs[:PIECES])
    )
    xhat, r = centre(pre_ref[...])
    d = norm_back(xhat, r, gain_ref[...], grad)
    d_ref[...] = d
    width = d.shape[1]
    low_ref[...] = d.astype(BF)
    norms_ref[...] = jnp.concatenate(
        [
            jnp.sum(grad * xhat, axis=0, keepdims=True),
            jnp.sum(grad, axis=0, keepdims=True),
            grads_two_ref[...],
            jnp.zeros((NORM_ROWS - 4, width), F32),
        ],
        axis=0,
    ).astype(BF)


def ln1_back(pre, d2, keep, near, far, gain, grads_two):
    shape = pre.shape
    return pl.pallas_call(
        ln1_back_kernel,
        out_shape=[out(shape, F32), out(shape), out((NORM_ROWS, shape[1]))],
        in_specs=vmem(6 + PIECES),
        out_specs=vmem(3),
        compiler_params=params(16),
        cost_estimate=cost(pre.size * 20, pre.size * 20),
        name="norm_one_backward",
    )(pre, d2, keep, near, gain, grads_two, *far)


def swap(value, axis, bit):
    count = lax.axis_size(axis)
    return lax.ppermute(value, axis, [(i, i ^ bit) for i in range(count)])


def swap_chip_edges(value):
    count = lax.axis_size("seq") * lax.axis_size("tp")
    pairs = []
    for i in range(1, count - 1, 2):
        pairs += [(i, i + 1), (i + 1, i)]
    return lax.ppermute(value, ("seq", "tp"), pairs)


def fold_kernel(dims, place_ref, own_ref, recv_ref, keep_ref, send_ref):
    rows, half = recv_ref.shape[0], keep_ref.shape[0]
    base = place_ref[dims[0]] * rows
    cut = place_ref[dims[1]] * half
    for ref, at in ((keep_ref, cut), (send_ref, half - cut)):
        own = own_ref[pl.ds(pl.multiple_of(base + at, NORM_ROWS), half), :].astype(F32)
        recv = recv_ref[pl.ds(pl.multiple_of(at, NORM_ROWS), half), :].astype(F32)
        ref[...] = (own + recv).astype(BF)


def fold(place, dims, own, recv):
    rows, width = recv.shape
    vm = pl.BlockSpec(memory_space=pltpu.VMEM)
    return pl.pallas_call(
        functools.partial(fold_kernel, dims),
        out_shape=[jax.ShapeDtypeStruct((rows // 2, width), BF)] * 2,
        in_specs=[smem(), vm, vm],
        out_specs=[vm] * 2,
        compiler_params=params(10),
        cost_estimate=cost(recv.size, recv.size * 6),
        name="fold_half",
    )(place, own, recv)


def join_kernel(dim, place_ref, own_ref, recv_ref, out_ref):
    first = place_ref[dim] == 0
    half = own_ref.shape[0]
    own, recv = own_ref[...], recv_ref[...]
    out_ref[0:half, :] = jnp.where(first, own, recv).astype(out_ref.dtype)
    out_ref[half:, :] = jnp.where(first, recv, own).astype(out_ref.dtype)


def join(place, dim, own, recv, kind=BF):
    half, width = own.shape
    vm = pl.BlockSpec(memory_space=pltpu.VMEM)
    return pl.pallas_call(
        functools.partial(join_kernel, dim),
        out_shape=jax.ShapeDtypeStruct((2 * half, width), kind),
        in_specs=[smem(), vm, vm],
        out_specs=vm,
        compiler_params=params(10),
        cost_estimate=cost(0, own.size * 12),
        name="join_halves",
    )(place, own, recv)


def finish_in_kernel(dims, place_ref, g_ref, g_recv_ref, u_ref, u_recv_ref, out_ref):
    half = g_ref.shape[0]
    for i, (own_ref, recv_ref) in enumerate(((g_ref, g_recv_ref), (u_ref, u_recv_ref))):
        first = place_ref[dims[i]] == 0
        own, recv = own_ref[...], recv_ref[...]
        out_ref[0:half, i, :] = jnp.where(first, own, recv).astype(F32)
        out_ref[half:, i, :] = jnp.where(first, recv, own).astype(F32)


def finish_in(place, gate, up):
    half, width = gate[1].shape
    return pl.pallas_call(
        functools.partial(finish_in_kernel, (gate[0], up[0])),
        out_shape=out((2 * half, 2, width), F32),
        in_specs=[smem()] + vmem(4),
        out_specs=vmem(1)[0],
        compiler_params=params(16),
        cost_estimate=cost(0, gate[1].size * 24),
        name="finish_w_in_gradient",
    )(place, *gate[1:], *up[1:])


def finish_rest_kernel(
    dims, place_ref, a_ref, a_recv_ref, b_ref, b_recv_ref, qkv_ref, out_ref, *norm_refs
):
    first = place_ref[dims[0]] == 0
    half = a_ref.shape[0]
    own, recv = a_ref[...], a_recv_ref[...]
    qkv_ref[0:half, :] = jnp.where(first, own, recv).astype(F32)
    qkv_ref[half : 2 * half, :] = jnp.where(first, recv, own).astype(F32)
    first = place_ref[dims[1]] == 0
    own, recv = b_ref[...], b_recv_ref[...]
    step = own.shape[0] // 2
    count = step - NORM_ROWS
    low = jnp.where(first, own, recv).astype(F32)
    high = jnp.where(first, recv, own).astype(F32)
    for ref, start, rows in ((qkv_ref, 2 * half, low), (out_ref, 0, high)):
        ref[start : start + count, :] = rows[0:count]
        ref[start + count : start + 2 * count, :] = rows[step : step + count]
    for i, ref in enumerate(norm_refs):
        ref[...] = low[count + i]


def finish_rest(place, a, b):
    width = a[1].shape[1]
    rest = b[1].shape[0] - 2 * NORM_ROWS
    return pl.pallas_call(
        functools.partial(finish_rest_kernel, (a[0], b[0])),
        out_shape=[
            out((2 * a[1].shape[0] + rest, width), F32),
            out((rest, width), F32),
            *[out((width,), F32)] * 4,
        ],
        in_specs=[smem()] + vmem(4),
        out_specs=vmem(6),
        compiler_params=params(12),
        cost_estimate=cost(0, a[1].size * 24),
        name="finish_attention_gradients",
    )(place, *a[1:], *b[1:])


def send_half(place_ref, dim, ref, sent_ref):
    count = sent_ref.shape[0]
    at = (1 - place_ref[dim]) * count
    sent_ref[...] = ref[pl.ds(pl.multiple_of(at, NORM_ROWS), count), :]


def cut_a_kernel(dim, place_ref, own_ref, far_ref, a_ref, sent_ref):
    half = a_ref.shape[0]
    total = own_ref[0:half, :].astype(F32) + far_ref[...].astype(F32)
    a_ref[...] = total.astype(BF)
    send_half(place_ref, dim, a_ref, sent_ref)


def cut_a(place, dim, own, far):
    rows, width = far.shape
    return pl.pallas_call(
        functools.partial(cut_a_kernel, dim),
        out_shape=[out((rows, width)), out((rows // 2, width))],
        in_specs=[smem()] + vmem(2),
        out_specs=vmem(2),
        compiler_params=params(12),
        cost_estimate=cost(far.size, far.size * 8),
        name="add_far_shard_a",
    )(place, own, far)


def cut_b_kernel(dim, place_ref, own_ref, far_ref, out_ref, b_ref, sent_ref):
    rows = far_ref.shape[0]
    start = own_ref.shape[0] - rows
    value = (own_ref[start:, :].astype(F32) + far_ref[...].astype(F32)).astype(BF)
    step = b_ref.shape[0] // 4
    count = step - NORM_ROWS
    for i in range(4):
        at = (i % 2) * count
        source = value if i < 2 else out_ref
        b_ref[i * step : i * step + count, :] = source[at : at + count, :]
        b_ref[i * step + count : (i + 1) * step, :] = out_ref[2 * count :, :]
    send_half(place_ref, dim, b_ref, sent_ref)


def cut_b(place, dim, own, far, out_rows):
    width = own.shape[1]
    rows = far.shape[0] + out_rows.shape[0] + 3 * NORM_ROWS
    return pl.pallas_call(
        functools.partial(cut_b_kernel, dim),
        out_shape=[out((rows, width)), out((rows // 2, width))],
        in_specs=[smem()] + vmem(3),
        out_specs=vmem(2),
        compiler_params=params(12),
        cost_estimate=cost(far.size, far.size * 8),
        name="add_far_shard_b",
    )(place, own, far, out_rows)


def out_grad_kernel(ctx_ref, datt_ref, own_ref, far_ref, out_ref):
    count = ctx_ref.shape[0]
    near = dot(ctx_ref[...], datt_ref[...], 1, 0)
    out_ref[0:count, :] = (near + far_ref[0:count, :].astype(F32)).astype(BF)
    norms = own_ref[count:, :].astype(F32) + far_ref[count:, :].astype(F32)
    out_ref[count:, :] = norms.astype(BF)


def out_grad(ctx, datt, own, far):
    vm = pl.BlockSpec(memory_space=pltpu.VMEM)
    return pl.pallas_call(
        out_grad_kernel,
        out_shape=jax.ShapeDtypeStruct(far.shape, BF),
        in_specs=[vm] * 4,
        out_specs=vm,
        compiler_params=params(12),
        cost_estimate=cost(2 * ctx.size * datt.shape[1], datt.size * 2),
        name="out_gradient",
    )(ctx, datt, own, far)


class SeqSum:
    def __init__(self, place, order, dims, g, sent=None, last=None):
        self.place, self.order, self.dims, self.value = place, order, dims, g
        self.last = last
        self.stage = 1
        self.pairwise = lax.axis_size("seq") == 8
        if not self.pairwise:
            whole = lax.psum(g, "seq")
            half = g.shape[0] // 2
            self.dims = (len(dims),)
            self.value, self.moving = whole[:half], whole[half:]
            return
        if sent is None:
            half = g.shape[0] // 2
            sent = lax.dynamic_slice_in_dim(g, (1 - place[dims[0]]) * half, half, 0)
        self.send(0, sent)

    def send(self, dim, value):
        self.moving = swap(value, "seq", 1 << self.dims[dim])

    def step(self):
        stage, place, order, dims = self.stage, self.place, self.order, self.dims
        self.stage += 1
        if not self.pairwise and stage < 5:
            return
        value, moved = self.value, self.moving
        if stage < 5 or self.last is not None:
            value = order(value)
        if stage == 1:
            self.value, sent = fold(place, dims[:2], value, moved)
            order.note(sent)
            self.send(1, sent)
        elif stage in (2, 3):
            self.value = order.note(add(value, moved))
            self.send(2 if stage == 2 else 1, self.value)
        elif stage == 4:
            self.value = order.note(join(place, dims[1], value, moved))
            self.send(0, self.value)
        elif stage == 5:
            if self.last is None:
                self.result = (dims[0], self.value, moved)
                return
            self.result = self.last(place, dims[0], value, moved)
            order.note(jax.tree.leaves(self.result)[-1])


def add_kernel(a_ref, b_ref, out_ref):
    out_ref[...] = (a_ref[...].astype(F32) + b_ref[...].astype(F32)).astype(BF)


def add(a, b):
    return pl.pallas_call(
        add_kernel,
        out_shape=out(a.shape),
        in_specs=vmem(2),
        out_specs=vmem(1)[0],
        compiler_params=params(10),
        cost_estimate=cost(a.size, a.size * 6),
        name="add_pair",
    )(a, b)


def input_grad_kernel(place_ref, *refs):
    (*heads, wt_ref, wt_far_ref, own_ref, sent_ref, near_ref, far_ref) = refs
    stack_heads(heads[: len(heads) // 2], near_ref)
    stack_heads(heads[len(heads) // 2 :], far_ref)
    half = own_ref.shape[0]
    for ref, which in ((sent_ref, 1 - place_ref[4]), (own_ref, place_ref[4])):
        here = pl.ds(pl.multiple_of(which * half, 128), half)
        total = dot(near_ref[:, here], wt_ref[...], 0, 0)
        ref[...] = (total + dot(far_ref[:, here], wt_far_ref[...], 0, 0)).astype(ref.dtype)


def input_grad(place, near, far, wt, wt_far):
    count = near[0].shape[2]
    half, (size, width) = count // 2, wt.shape
    vm = pl.BlockSpec(memory_space=pltpu.VMEM)
    return pl.pallas_call(
        input_grad_kernel,
        out_shape=[
            jax.ShapeDtypeStruct((half, width), F32),
            jax.ShapeDtypeStruct((half, width), BF),
        ],
        in_specs=[smem()] + [vm] * (2 * len(near) + 2),
        out_specs=[vm] * 2,
        scratch_shapes=[pltpu.VMEM((size, count), BF)] * 2,
        compiler_params=params(16),
        cost_estimate=cost(4 * size * count * width, 12 * half * width),
        name="input_gradient",
    )(place, *near, *far, wt, wt_far)


def input_rows_kernel(place_ref, own_ref, recv_ref, pre_ref, out_ref, edge_ref):
    count, edge = out_ref.shape[0], edge_ref.shape[0]
    core = place_ref[4]
    at = pl.ds(pl.multiple_of(core * count, edge), edge)
    edge_ref[...] = (own_ref[at, :] + recv_ref[at, :].astype(F32)).astype(BF)
    at = pl.ds(pl.multiple_of((1 - core) * edge, edge), count)
    out_ref[...] = pre_ref[...] + (own_ref[at, :] + recv_ref[at, :].astype(F32))


def input_rows(place, own, recv, pre):
    vm = pl.BlockSpec(memory_space=pltpu.VMEM)
    return pl.pallas_call(
        input_rows_kernel,
        out_shape=[
            jax.ShapeDtypeStruct(pre.shape, F32),
            jax.ShapeDtypeStruct((QB, pre.shape[1]), BF),
        ],
        in_specs=[smem()] + [vm] * 3,
        out_specs=[vm] * 2,
        compiler_params=params(16),
        cost_estimate=cost(pre.size * 2, pre.size * 16),
        name="input_gradient_rows",
    )(place, own, recv, pre)


def input_edge_kernel(place_ref, rows_ref, edge_ref, out_ref):
    out_ref[...] = rows_ref[...]
    edge = edge_ref.shape[0]
    start = place_ref[4] * (rows_ref.shape[0] - edge)
    at = pl.ds(pl.multiple_of(start, edge), edge)
    out_ref[at, :] = rows_ref[at, :] + edge_ref[...].astype(F32)


def input_edge(place, rows, edge):
    vm = pl.BlockSpec(memory_space=pltpu.VMEM)
    return pl.pallas_call(
        input_edge_kernel,
        out_shape=jax.ShapeDtypeStruct(rows.shape, F32),
        in_specs=[smem()] + [vm] * 2,
        out_specs=vm,
        compiler_params=params(12),
        cost_estimate=cost(rows.size, rows.size * 10),
        name="input_gradient_edge",
    )(place, rows, edge)


def per_device(
    inputs, lengths, w_qkv, w_out, w_in, w_down, ln1_gain, ln1_bias, ln2_gain, ln2_bias, cotangent
):
    own_rows, width = inputs.shape
    tp_count = lax.axis_size("tp")
    head_width = w_qkv.shape[2]
    heads = head_width // HD
    chip_rows = 2 * own_rows
    tp = lax.axis_index("tp")
    seq = lax.axis_index("seq")
    core = tp & 1
    even = core == 0
    first = (seq * tp_count + 2 * (tp >> 1)) * own_rows
    place = jnp.stack([seq & 1, (seq >> 1) & 1, (seq >> 2) & 1, 0 * core, core]).astype(jnp.int32)

    bounds = jnp.cumsum(lengths)[:, None]
    tokens = (first + jnp.arange(chip_rows, dtype=jnp.int32))[None, :]
    before = bounds <= tokens
    start = jnp.max(jnp.where(before, bounds, 0), axis=0)
    end = jnp.min(jnp.where(before, jnp.iinfo(jnp.int32).max, bounds), axis=0)
    se = jnp.stack([start, end]) - (first - QB)
    se = jnp.pad(se, ((0, 6), (0, 0)))
    table = jnp.asarray(slope_table(HEADS))
    slopes = lax.dynamic_slice_in_dim(table, tp * heads, heads)
    slopes_far = lax.dynamic_slice_in_dim(table, (tp ^ 2) * heads, heads)

    wt = w_qkv.transpose(0, 2, 1).reshape(3 * head_width, width)
    wt_far = swap(wt, "tp", 2)

    sibling = swap(inputs, "tp", 1)
    edge = swap_chip_edges(
        lax.dynamic_slice_in_dim(inputs, core * (own_rows - QB), QB, axis=0)
    )
    edge_sibling = swap(edge, "tp", 1)
    rows, ctx, qkv, kv = attn_near(
        heads, place, slopes, se, inputs, sibling, edge, edge_sibling,
        wt.reshape(3, head_width, width),
    )
    w_out_far = swap(after(w_out, ctx), "tp", 2)
    near_sums = attended_halves(place, ctx, w_out)
    ctx_far, qkv_far, kv_far = attn_far(
        heads, slopes_far, se, rows, wt_far.reshape(3, head_width, width)
    )
    attended, attended_sent = attended_halves(place, ctx_far, w_out_far, near_sums)
    attended_sent = swap(attended_sent, "tp", 1)
    gain1, bias1 = ln1_gain[None], ln1_bias[None]
    gain2, bias2 = ln2_gain[None], ln2_bias[None]
    pre_one, normed, low, *low_pieces = ln1(inputs, attended, attended_sent, gain1, bias1)

    order = Order()
    w_in_late = after(w_in, low)
    wg, wu = w_in_late[:, 0], w_in_late[:, 1]

    def both_ways(own, pieces, work, between=lambda near_out: None):
        far = [swap(piece, "tp", 2) for piece in pieces]
        near_out = work(0, own, order(swap(own, "tp", 1)))
        near_keep, near_send = near_out[-2:]
        order.note(near_send)
        recv = swap(near_send, "tp", 1)
        between(near_out)
        far = [order(rows) for rows in far]
        far_sibling = [swap(rows, "tp", 1) for rows in far]
        outs, sums = [near_out], []
        for rows, rows_sibling in zip(far, far_sibling):
            outs.append(work(len(outs), order(rows), rows_sibling))
            order.note(outs[-1][-1])
        from_sibling = [swap(o[-1], "tp", 1) for o in outs[1:]]
        for i, (o, theirs) in enumerate(zip(outs[1:], from_sibling)):
            total = order.note(add(order(o[-2]), theirs))
            sums.append(swap(total, "tp", 2))
        return outs, (near_keep, recv, sums)

    order.note(low)
    forward, parts = both_ways(
        low, low_pieces, lambda i, a, b: ff_fwd((a, b), wg, wu, w_down)
    )
    layer_out, d_pre_two, grads_two, d_branch, *d_branch_pieces = ln2(
        normed, order(parts[0]), *parts[1:], cotangent, gain2, bias2
    )
    order.note(d_branch)

    weight_near_parts = []

    def grads_between(near_out):
        for x, d in weight_pairs:
            part = weight_near(order(forward[0][x]), near_out[d])
            weight_near_parts.append(order.note(part))

    weight_pairs = ((1, 0), (0, 2), (0, 1))
    backward, parts = both_ways(
        d_branch,
        d_branch_pieces,
        lambda i, a, b: ff_bwd((a, b), forward[i][2], forward[i][3], w_down, wg, wu),
        grads_between,
    )

    def join_whole(*halves):
        return join(*halves, F32)

    def weight_sum(which, dims):
        x, d = weight_pairs[which]
        pairs = [t for f, b in zip(forward[1:], backward[1:]) for t in (f[x], b[d])]
        total, sent = weight_far(
            place, dims[0], order(weight_near_parts[which]), *pairs
        )
        order.note(sent)
        return SeqSum(place, order, dims, total, sent, None if which else join_whole)

    d_far, d_near = [], []

    def one_head(h, far):
        kept = (slopes_far, se, qkv_far, kv_far) if far else (slopes, se, qkv, kv)
        return order.note(head_back(h, *kept, order(d_ctx_far if far else d_ctx)))

    down = weight_sum(0, (0, 1, 2))
    up = weight_sum(1, (0, 1, 2))
    gate = weight_sum(2, (1, 0, 2))
    d_pre_one, half, norms = ln1_back(
        pre_one, d_pre_two, order(parts[0]), *parts[1:], gain1, grads_two
    )
    order.note(half)
    half_sibling = swap(half, "tp", 1)
    norms_sibling = swap(norms, "tp", 1)
    down.step()
    gate.step()
    d_attended, sent_out, d_ctx, d_ctx_far = gather_back(
        place, order(ctx_far), half, half_sibling, norms, norms_sibling, w_out, w_out_far
    )
    order.note(d_ctx_far)
    far_out = swap(sent_out, "tp", 2)
    d_far.append(one_head(0, True))
    down.step()
    d_far.append(one_head(1, True))
    up.step()
    d_far.append(one_head(2, True))
    grad_out = order.note(out_grad(ctx, order(d_attended), sent_out, far_out))
    gate.step()
    far_qk, far_v = qkv_grad(d_far, order(rows), (2, 1))
    order.note(far_v)
    far_v = swap(far_v, "tp", 2)
    far_qk = swap(far_qk, "tp", 2)
    d_near.append(one_head(0, False))
    down.step()
    d_near.append(one_head(1, False))
    up.step()
    d_near.append(one_head(2, False))
    (own_qkv,) = qkv_grad(d_near, order(rows))
    order.note(own_qkv)
    total, sent = cut_b(place, 0, order(own_qkv), far_v, grad_out)
    order.note(sent)
    attn_b = SeqSum(place, order, (0, 1, 2), total, sent)
    gate.step()
    down.step()
    attn_b.step()
    total, sent = cut_a(place, 1, order(own_qkv), far_qk)
    order.note(sent)
    attn_a = SeqSum(place, order, (1, 0, 2), total, sent)
    up.step()
    window_own, window_sent = input_grad(
        place, [order(d_near[0]), *d_near[1:]], d_far, wt, wt_far
    )
    order.note(window_sent)
    window_sent = swap(window_sent, "tp", 1)
    attn_b.step()
    attn_a.step()
    down.step()
    gate.step()
    attn_a.step()
    up.step()
    attn_b.step()
    attn_a.step()
    attn_b.step()
    attn_a.step()
    grad_rows, d_edge = input_rows(place, order(window_own), window_sent, d_pre_one)
    order.note(d_edge)
    d_edge = swap_chip_edges(d_edge)
    up.step()
    gate.step()
    grad_in = order.note(
        finish_in(order(place), gate.result, up.result)
    )
    grad_input = order.note(input_edge(place, order(grad_rows), d_edge))
    attn_b.step()
    attn_a.step()
    grad_qkv, grad_out, *norm_grads = finish_rest(order(place), attn_a.result, attn_b.result)
    order.note(norm_grads[0])
    assert all(unit.stage == 6 for unit in (down, gate, up, attn_a, attn_b))
    grad_down = down.result
    grad_qkv = grad_qkv.reshape(3, head_width, width).transpose(0, 2, 1)
    return (
        layer_out,
        grad_input,
        grad_qkv,
        grad_out,
        grad_in,
        grad_down,
        norm_grads[0],
        norm_grads[1],
        norm_grads[2],
        norm_grads[3],
    )


def solution(mesh):
    in_specs = (
        P(("seq", "tp"), None),
        P(),
        P(None, None, "tp"),
        P("tp", None),
        P(None, None, "tp"),
        P("tp", None),
        P(),
        P(),
        P(),
        P(),
        P(("seq", "tp"), None),
    )
    out_specs = (
        P(("seq", "tp"), None),
        P(("seq", "tp"), None),
        P(None, None, "tp"),
        P("tp", None),
        P(None, None, "tp"),
        P("tp", None),
        P(),
        P(),
        P(),
        P(),
    )
    return jax.shard_map(
        per_device, mesh=mesh, in_specs=in_specs, out_specs=out_specs, check_vma=False
    )
```
